128 devices in a mesh: row: 32 (over z, x, y_lo), feat: 4 (over y_hi, core).
Axes of the slice: x: 4, y: 4 (y_hi: 2, y_lo: 2; y = y_hi * 2 + y_lo), z: 4, core: 2. Of those that a mesh axis runs over, the one named last changes fastest.
Arguments:
- cells: bfloat16 [6144, 8, 192], P('row', 'feat'), may hold values from -16 to 16
- w_query: bfloat16 [192, 192], replicated, may hold values from -0.25 to 0.25
- w_key: bfloat16 [192, 192], replicated, may hold values from -0.25 to 0.25
- w_value: bfloat16 [192, 192], replicated, may hold values from -0.4375 to 0.4375
- w_out: bfloat16 [192, 192], replicated, may hold values from -0.4375 to 0.4375
- train_flag: int32 [6144], P('row'), may hold values from 0 to 1, as said below
- grad_out: bfloat16 [6144, 8, 192], P('row', 'feat'), may hold values from -6 to 6
Outputs:
- grad_cells: bfloat16 [6144, 8, 192], P('row', 'feat')
- grad_w_query: float32 [192, 192], replicated
- grad_w_key: float32 [192, 192], replicated
- grad_w_value: float32 [192, 192], replicated
- grad_w_out: float32 [192, 192], replicated
The draws below stay inside these ranges and needn't reach their ends.
Inputs may be any that keep to these rules, and one draw needn't show every extreme that they name: train_flag is 1 on the first rows of the table and 0 on all later rows; at least 3072 rows are training rows and at least one row is a test row.
All inputs are finite; a program needn't handle non-finite values.
Results may differ from the reference program's by a relative error of at most 0.04.
The reference program's roundings to bfloat16 on the way (of `attention_b`, `attended`, `grad_attended` and `grad_scores`) count: a program that leaves them out, or rounds other values in their place, can miss the bound.
Values may be sent and summed in bfloat16 or wider, within the bound.
A program may use at most 128 MiB of HBM per device.

```python
import jax
import jax.numpy as jnp
from jax import lax

E = 192
HEADS = 6
F = 8
HD = 32
R = 6144


def shared_matrix(key):
    return jax.random.normal(key, (E, E), jnp.float32) * float(E) ** (-0.5)


def draw_w_query(key, part):
    shared = shared_matrix(key)
    return (0.25 * jnp.tanh(4.0 * shared)).astype(jnp.bfloat16)


def draw_w_key(key, part):
    key = jax.random.fold_in(key, 3)
    own = jax.random.normal(key, (E, E), jnp.float32) * float(E) ** (-0.5)
    mixed = own
    return (0.25 * jnp.tanh(4.0 * mixed)).astype(jnp.bfloat16)


def draw_cells(key, part):
    key = jax.random.fold_in(key, 5)
    third = jax.random.fold_in(key, 2)
    values = jax.random.normal(third, (R, F, E), jnp.float32)
    return jnp.clip(values, -6.0, 6.0).astype(jnp.bfloat16)


def draw_train_flag(key, part):
    key = jax.random.fold_in(key, 7)
    train_rows = jax.random.randint(key, (), R // 2, R)
    return (jnp.arange(R) < train_rows).astype(jnp.int32)


def block_levels(rng, dims, pieces, least, top_value):
    loudness = 1.0
    for dim, parts in pieces:
        draws = jax.random.uniform(jax.random.fold_in(jax.random.fold_in(rng, 6), dim), (parts,), jnp.float32, least / len(pieces), top_value / len(pieces))
        loudness = loudness * jnp.repeat(jnp.exp(draws), dims[dim] // parts).reshape((-1,) + (1,) * (len(dims) - 1 - dim))
    return loudness


def noise(rng, shape, spread, most, cuts=(), held_as=jnp.bfloat16):
    factor_of = block_levels(rng, shape, cuts, -0.22, 0.18) if cuts else 1.0
    drawn = jax.random.normal(rng, shape, jnp.float32) * spread * factor_of
    return jnp.minimum(jnp.maximum(drawn, -most), most).astype(held_as)


def setup_inputs(seed: int = 0) -> dict:
    splits = jax.random.split(jax.random.key(seed), 8)
    return {
        "cells": draw_cells(jax.random.fold_in(splits[7], 71), 0),
        "w_query": draw_w_query(jax.random.fold_in(splits[7], 71), 0),
        "w_key": draw_w_key(jax.random.fold_in(splits[7], 71), 0),
        "w_value": noise(splits[3], (E, E), E ** -0.5, 0.4375),
        "w_out": noise(splits[4], (E, E), E ** -0.5, 0.4375),
        "train_flag": draw_train_flag(jax.random.fold_in(splits[7], 71), 0),
        "grad_out": noise(splits[6], (R, F, E), 1.0, 6.0, ((0, 32), (1, 4))),
    }


MASKED = -1.0e30


def heads_first(array):
    return array.reshape(R, F, HEADS, HD).transpose(1, 2, 0, 3).reshape(F * HEADS, R, HD)


def rows_first(array):
    return array.reshape(F, HEADS, R, HD).transpose(2, 0, 1, 3).reshape(R * F, E)


def project(left, right):
    return jnp.dot(left, right, preferred_element_type=jnp.float32).astype(jnp.bfloat16)


def attention_of(query_head, key_head, keep):
    scores = jnp.dot(query_head, key_head.T, preferred_element_type=jnp.float32) * (float(HD) ** -0.5)
    scores = jnp.where(keep[None, :], scores, MASKED)
    maxima = jnp.max(scores, axis=1, keepdims=True)
    weights = jnp.exp(scores - maxima)
    return weights / jnp.sum(weights, axis=1, keepdims=True)


def reference(cells, w_query, w_key, w_value, w_out, train_flag, grad_out):
    flat_cells = cells.reshape(R * F, E)
    flat_grad = grad_out.reshape(R * F, E)
    query = project(flat_cells, w_query)
    key = project(flat_cells, w_key)
    value = project(flat_cells, w_value)
    keep = train_flag > 0
    query_heads = heads_first(query)
    key_heads = heads_first(key)
    value_heads = heads_first(value)

    def forward(operands):
        query_head, key_head, value_head = operands
        attention = attention_of(query_head, key_head, keep).astype(jnp.bfloat16)
        return project(attention, value_head)

    attended_heads = lax.map(forward, (query_heads, key_heads, value_heads))
    attended = rows_first(attended_heads)
    grad_attended = project(flat_grad, w_out.T)
    grad_att_heads = heads_first(grad_attended)

    def backward(operands):
        query_head, key_head, value_head, attended_head, grad_head = operands
        attention = attention_of(query_head, key_head, keep)
        attention_b = attention.astype(jnp.bfloat16)
        grad_attention = jnp.dot(grad_head, value_head.T, preferred_element_type=jnp.float32)
        delta = jnp.sum(grad_head.astype(jnp.float32) * attended_head.astype(jnp.float32), axis=1)
        grad_scores = (attention * (grad_attention - delta[:, None]) * (float(HD) ** -0.5)).astype(jnp.bfloat16)
        grad_q = project(grad_scores, key_head)
        grad_k = project(grad_scores.T, query_head)
        grad_v = project(attention_b.T, grad_head)
        return grad_q, grad_k, grad_v

    grad_q_heads, grad_k_heads, grad_v_heads = lax.map(backward, (query_heads, key_heads, value_heads, attended_heads, grad_att_heads))
    grad_query = rows_first(grad_q_heads)
    grad_key = rows_first(grad_k_heads)
    grad_value = rows_first(grad_v_heads)
    grad_w_out = jnp.dot(attended.T, flat_grad, preferred_element_type=jnp.float32)
    grad_w_query = jnp.dot(flat_cells.T, grad_query, preferred_element_type=jnp.float32)
    grad_w_key = jnp.dot(flat_cells.T, grad_key, preferred_element_type=jnp.float32)
    grad_w_value = jnp.dot(flat_cells.T, grad_value, preferred_element_type=jnp.float32)
    summed = flat_grad.astype(jnp.float32)
    summed = summed + jnp.dot(grad_query, w_query.T, preferred_element_type=jnp.float32)
    summed = summed + jnp.dot(grad_key, w_key.T, preferred_element_type=jnp.float32)
    summed = summed + jnp.dot(grad_value, w_value.T, preferred_element_type=jnp.float32)
    grad_cells = summed.astype(jnp.bfloat16).reshape(R, F, E)
    return grad_cells, grad_w_query, grad_w_key, grad_w_value, grad_w_out
```

```python
import functools

import jax
import jax.numpy as jnp
from jax import lax
from jax.experimental import pallas as pl
from jax.experimental.pallas import tpu as pltpu
from jax.sharding import PartitionSpec as P


HD = 32
SCALE = float(HD) ** -0.5
SCALE_LOG2E = SCALE * 1.4426950408889634
BIAS = -1e30
F32 = jnp.float32
BF = jnp.bfloat16
MESH = pl.DeviceIdType.MESH

E = 192
HALF = 96
ROWS = 192
NQ = 768
NR = 6144
KC = 1024


def dot(a, b):
    return jnp.dot(a, b, preferred_element_type=F32)


def dot_t(a, b):
    return lax.dot_general(a, b, (((1,), (1,)), ((), ())), preferred_element_type=F32)


def t_dot(a, b):
    return lax.dot_general(a, b, (((0,), (0,)), ((), ())), preferred_element_type=F32)


def place():
    row = lax.axis_index("row")
    feat = lax.axis_index("feat")
    return row // 8, (row // 2) % 4, row % 2, feat // 2, feat % 2


def device(z, x, yl, yh, c):
    return ((z * 4 + x) * 2 + yl, yh * 2 + c)


def iotas(shape):
    return lax.broadcasted_iota(jnp.int32, shape, 0), lax.broadcasted_iota(jnp.int32, shape, 1)


def pick_rows(f):
    i, j = iotas((ROWS, 2 * ROWS))
    return (j == 2 * i + f).astype(F32).astype(BF)


def spread_lanes():
    i, j = iotas((E, 256))
    return (j == i + jnp.where(i >= HALF, 128 - HALF, 0)).astype(F32).astype(BF)


def rcopy(src, dst, send, recv, to):
    return pltpu.make_async_remote_copy(
        src_ref=src, dst_ref=dst, send_sem=send, recv_sem=recv, device_id=to, device_id_type=MESH
    )


def share_kernel(cells_ref, grad_ref, wq_ref, wk_ref, wv_ref, wo_ref, flag_ref, kv_ref, qg_ref,
                 kvs, qgs, s1, r1, s2, r2, zs, zr, fs, fr, cs, cr):
    z, x, yl, yh, c = place()
    mine = x // 2 == c
    own = jnp.where(mine, 1, 0)
    zp, zn = (z + 1) % 4, (z + 3) % 4
    up, down, twin = device(zp, x, yl, yh, c), device(zn, x, yl, yh, c), device(z, x, yl, yh, 1 - c)
    slot = (x % 2) * 2 + yl

    barrier = pltpu.get_barrier_semaphore()
    for to in (up, down, twin):
        pl.semaphore_signal(barrier, inc=1, device_id=to, device_id_type=MESH)
    for s in range(4):
        @pl.when(jnp.logical_not(jnp.logical_and(mine, slot == s)))
        def _():
            pl.semaphore_signal(
                barrier, inc=1, device_id=device(z, 2 * c + s // 2, s % 2, yh, x // 2), device_id_type=MESH
            )

    spread = spread_lanes()
    lane = lax.broadcasted_iota(jnp.int32, (ROWS, 128), 1)
    k_extra = jnp.where((lane == HALF) & (flag_ref[...] <= 0), BIAS, 0.0)
    v_extra = jnp.where((lane >= HALF) & (lane < HALF + 3), 1.0, 0.0)
    cells = cells_ref[...]
    grad = grad_ref[...]
    for f in range(2):
        pick = pick_rows(f)
        cf = dot(pick, cells).astype(BF)
        gf = dot(pick, grad).astype(BF)
        k = dot(dot(cf, wk_ref[...]).astype(BF), spread)
        v = dot(dot(cf, wv_ref[...]).astype(BF), spread)
        q = dot(dot(cf, wq_ref[...]).astype(BF), spread)
        g = dot(dot_t(gf, wo_ref[...]).astype(BF), spread)
        for h in range(2):
            a = slice(128 * h, 128 * h + 128)
            kvs[2 * f + h, :, 0:128] = (k[:, a] + k_extra).astype(BF)
            kvs[2 * f + h, :, 128:256] = (v[:, a] + v_extra).astype(BF)
            qgs[2 * f + h, :, 0:128] = q[:, a].astype(BF)
            qgs[2 * f + h, :, 128:256] = g[:, a].astype(BF)

    pl.semaphore_wait(barrier, 7 - own)

    my_rows = pl.ds(pl.multiple_of(z * 1536 + x * 384 + yl * 192, 192), 192)
    my_slot = pl.ds(pl.multiple_of(slot * 192, 192), 192)

    def first(j):
        to = device(z, 2 * c + j // 2, j % 2, yh, x // 2)
        a = rcopy(kvs.at[j], kv_ref.at[my_rows, :], s1.at[j], r1.at[slot], to)
        b = rcopy(qgs.at[j], qg_ref.at[my_slot, :], s2.at[j], r2.at[slot], to)
        return a, b

    for j in range(4):
        keep = jnp.logical_and(mine, slot == j)

        @pl.when(keep)
        def _():
            pltpu.make_async_copy(kvs.at[j], kv_ref.at[my_rows, :], r1.at[slot]).start()
            pltpu.make_async_copy(qgs.at[j], qg_ref.at[my_slot, :], r2.at[slot]).start()

        @pl.when(jnp.logical_not(keep))
        def _():
            a, b = first(j)
            a.start()
            b.start()

    def rows_of(zz, cc, s):
        return pl.ds(pl.multiple_of(zz * 1536 + cc * 768 + s * 192, 192), 192)

    def move(zz, s, send, recv, to):
        r = rows_of(zz, c, s)
        return rcopy(kv_ref.at[r, :], kv_ref.at[r, :], send, recv, to)

    def landed(zz, cc, s, recv):
        r = rows_of(zz, cc, s)
        pltpu.make_async_copy(kv_ref.at[r, :], kv_ref.at[r, :], recv).wait()

    sent = []

    def go(copy):
        copy.start()
        sent.append(copy)

    for s in range(4):
        landed(z, c, s, r1.at[s])
        go(move(z, s, zs.at[s], zr.at[s], up))
        go(move(z, s, zs.at[4 + s], zr.at[4 + s], down))
        go(move(z, s, cs.at[s], cr.at[s], twin))
    for i in range(4):
        s = i
        landed(zn, c, s, zr.at[s])
        if s < 2:
            go(move(zn, s, fs.at[s], fr.at[s], up))
        go(move(zn, s, cs.at[4 + s], cr.at[4 + s], twin))
        s = (i + 2) % 4
        landed(zp, c, s, zr.at[4 + s])
        if s >= 2:
            go(move(zp, s, fs.at[s], fr.at[s], down))
        go(move(zp, s, cs.at[8 + s], cr.at[8 + s], twin))
    zo = (z + 2) % 4
    for s in (0, 2, 1, 3):
        landed(zo, c, s, fr.at[s])
        go(move(zo, s, cs.at[12 + s], cr.at[12 + s], twin))
    for n, zz in ((0, z), (1, zn), (2, zp), (3, zo)):
        for s in range(4):
            landed(zz, 1 - c, s, cr.at[4 * n + s])
    for s in range(4):
        q = pl.ds(s * 192, 192)
        pltpu.make_async_copy(qg_ref.at[q, :], qg_ref.at[q, :], r2.at[s]).wait()
    for copy in sent:
        copy.wait_send()
    for j in range(4):
        @pl.when(jnp.logical_not(jnp.logical_and(mine, slot == j)))
        def _():
            a, b = first(j)
            a.wait_send()
            b.wait_send()


def attention_kernel(kv_ref, qg_ref, dkv_ref, qa_ref, e_ref, mb_ref, kT_ref, vT_ref, qT_ref, gT_ref, qm_ref, gm_ref,
                     qmT_ref, gmT_ref, acc_ref, m_ref, dkv_acc, attT_ref, dqT_ref):
    lane = lax.broadcasted_iota(jnp.int32, (1, 128), 1)

    def rows(c):
        return pl.ds(pl.multiple_of(c * KC, KC), KC)

    def count(c, total):
        kept = jnp.where(kv_ref[rows(c), 0:128].astype(F32) > 0.5 * BIAS, 1.0, 0.0)
        return total + jnp.sum(kept, axis=0, keepdims=True)

    kept = lax.fori_loop(0, NR // KC, count, jnp.zeros((1, 128), F32))
    train = jnp.sum(jnp.where(lane == HALF, kept, 0.0)).astype(jnp.int32)
    nk = lax.div(train + KC - 1, KC)

    @pl.loop(nk, NR // KC)
    def _(c):
        dkv_ref[rows(c), :] = jnp.zeros((KC, 256), BF)

    @pl.loop(0, nk)
    def _(c):
        r = rows(c)
        kT_ref[:, r] = kv_ref[r, 0:128].T
        vT_ref[:, r] = kv_ref[r, 128:256].T

    qT_ref[...] = qg_ref[:, 0:128].T
    gT_ref[...] = qg_ref[:, 128:256].T
    attT_ref[...] = jnp.zeros_like(attT_ref)
    dqT_ref[...] = jnp.zeros_like(dqT_ref)
    i16 = lax.broadcasted_iota(jnp.int32, (16, NQ), 0)

    for h in range(3):
        hs = slice(32 * h, 32 * h + 32)
        qmT_ref[...] = jnp.zeros_like(qmT_ref)
        qmT_ref[hs, :] = qT_ref[hs, :]
        qm_ref[...] = qmT_ref[...].T
        qmT_ref[96:112, :] = jnp.where(i16 == 0, 1.0, 0.0).astype(BF)
        acc_ref[...] = jnp.zeros_like(acc_ref)
        m_ref[...] = jnp.full_like(m_ref, BIAS)

        @pl.loop(0, nk)
        def _(c):
            r = rows(c)
            vt = jnp.concatenate([vT_ref[hs, r], vT_ref[96:112, r]], 0)
            s = dot(kv_ref[r, 0:128], qmT_ref[...]) * SCALE_LOG2E
            old = m_ref[0:1, :]
            new = jnp.maximum(old, jnp.ceil(jnp.max(s, axis=0, keepdims=True)))
            e = jnp.exp2(s - new).astype(BF)
            e_ref[r, :] = e
            m_ref[0:1, :] = new
            mb_ref[c, 0:1, :] = new
            acc_ref[...] = acc_ref[...] * jnp.exp2(old - new) + dot(vt, e)

        inv = 1.0 / acc_ref[32:33, :]
        att = (acc_ref[0:32, :] * inv).astype(BF)
        attT_ref[hs, :] = att
        gp = (gT_ref[hs, :].astype(F32) * inv).astype(BF)
        delta = -jnp.sum(gp.astype(F32) * att.astype(F32), axis=0, keepdims=True)
        d0 = delta.astype(BF).astype(F32)
        d1 = (delta - d0).astype(BF).astype(F32)
        d2 = delta - d0 - d1
        gmT_ref[...] = jnp.zeros_like(gmT_ref)
        gmT_ref[hs, :] = gp
        gm_ref[...] = gmT_ref[...].T
        gmT_ref[96:112, :] = jnp.where(i16 == 0, d0, jnp.where(i16 == 1, d1, jnp.where(i16 == 2, d2, 0.0))).astype(BF)
        acc_ref[...] = jnp.zeros_like(acc_ref)

        @pl.loop(0, nk)
        def _(c):
            r = rows(c)
            ga = dot(kv_ref[r, 128:256], gmT_ref[...]).astype(BF)
            es = e_ref[r, :] * jnp.exp2(mb_ref[c, 0:1, :] - m_ref[0:1, :]).astype(BF)
            ds = es * ga
            dv = dot(es, gm_ref[...])
            dk = dot(ds, qm_ref[...]) * SCALE
            acc_ref[0:32, :] += dot(kT_ref[hs, r], ds)
            if h == 0:
                dkv_acc[r, 0:128] = dk
                dkv_acc[r, 128:256] = dv
            elif h == 1:
                dkv_acc[r, 0:128] += dk
                dkv_acc[r, 128:256] += dv
            else:
                dkv_ref[r, 0:128] = (dkv_acc[r, 0:128] + dk).astype(BF)
                dkv_ref[r, 128:256] = (dkv_acc[r, 128:256] + dv).astype(BF)

        dqT_ref[hs, :] = (acc_ref[0:32, :] * SCALE).astype(BF)

    qa_ref[:, 0:128] = dqT_ref[...].T
    qa_ref[:, 128:256] = attT_ref[...].T


def back_kernel(dkv_ref, qa_ref, cells_ref, grad_ref, wq_ref, wk_ref, wv_ref, wo_ref,
                gc_ref, gwq_ref, gwk_ref, gwv_ref, gwo_ref,
                tw, part, hp, hn, fp, fn, fin, rkv, rqa, wp, rs, p2, wf,
                qs, qr, ts, tr, hs_, hr, fs, fr, ks, kr, as_, ar, bs, br, cs, cr):
    z, x, yl, yh, c = place()
    mine = x // 2 == c
    own = jnp.where(mine, 1, 0)
    zp, zn = (z + 1) % 4, (z + 3) % 4
    zo = (z + 2) % 4
    up, down, twin = device(zp, x, yl, yh, c), device(zn, x, yl, yh, c), device(z, x, yl, yh, 1 - c)
    slot = (x % 2) * 2 + yl
    i16 = z * 4 + x
    i8 = (yh * 2 + yl) * 2 + c

    def dev16(j):
        return device(j // 4, j % 4, yl, yh, c)

    def dev8(j):
        return device(z, x, (j // 2) % 2, j // 4, j % 2)

    barrier = pltpu.get_barrier_semaphore()

    def greet(to):
        pl.semaphore_signal(barrier, inc=1, device_id=to, device_id_type=MESH)

    for to in (up, down, twin):
        greet(to)
    for j in range(4):
        @pl.when(jnp.logical_not(jnp.logical_and(mine, slot == j)))
        def _():
            greet(device(z, 2 * c + j // 2, j % 2, yh, x // 2))

    @pl.loop(1, 16)
    def _(n):
        greet(dev16((i16 + n) % 16))

    @pl.loop(1, 8)
    def _(n):
        greet(dev8((i8 + n) % 8))

    pl.semaphore_wait(barrier, 3 + 4 - own + 15 + 7)

    def back(s, src, dst, send, recv):
        q = pl.ds(s * 192, 192)
        to = device(z, 2 * c + s // 2, s % 2, yh, x // 2)
        return rcopy(src.at[q, :], dst.at[slot], send.at[s], recv.at[slot], to)

    def go_back(src, dst, send, recv):
        for s in range(4):
            keep = jnp.logical_and(mine, slot == s)

            @pl.when(keep)
            def _():
                pltpu.make_async_copy(src.at[pl.ds(s * 192, 192), :], dst.at[slot], recv.at[slot]).start()

            @pl.when(jnp.logical_not(keep))
            def _():
                back(s, src, dst, send, recv).start()

    def sent_back(src, dst, send, recv):
        for s in range(4):
            @pl.when(jnp.logical_not(jnp.logical_and(mine, slot == s)))
            def _():
                back(s, src, dst, send, recv).wait_send()

    def came_back(dst, recv):
        for j in range(4):
            pltpu.make_async_copy(dst.at[j], dst.at[j], recv.at[j]).wait()

    def block(zz, cc):
        return pl.ds(pl.multiple_of(zz * 1536 + cc * 768, 768), 768)

    sent = []

    def go(copy):
        copy.start()
        sent.append(copy)

    for n, zz in enumerate((zo, zp, zn, z)):
        go(rcopy(dkv_ref.at[block(zz, 1 - c), :], tw.at[n], ts.at[n], tr.at[n], twin))
    go_back(qa_ref, rqa, qs, qr)

    def with_twin(n, zz):
        pltpu.make_async_copy(tw.at[n], tw.at[n], tr.at[n]).wait()
        return dkv_ref[block(zz, c), :].astype(F32) + tw[n].astype(F32)

    lo, hi = pl.ds(0, 384), pl.ds(384, 384)
    part[0] = with_twin(0, zo).astype(BF)
    go(rcopy(part.at[0, lo, :], hp, hs_.at[0], hr.at[0], up))
    go(rcopy(part.at[0, hi, :], hn, hs_.at[1], hr.at[1], down))
    part[1] = with_twin(1, zp).astype(BF)
    go(rcopy(part.at[1, hi, :], fp.at[hi, :], fs.at[0], fr.at[0], up))
    part[2] = with_twin(2, zn).astype(BF)
    go(rcopy(part.at[2, lo, :], fn.at[lo, :], fs.at[1], fr.at[1], down))
    pltpu.make_async_copy(hp, hp, hr.at[0]).wait()
    part[1, 0:384, :] = (part[1, 0:384, :].astype(F32) + hp[...].astype(F32)).astype(BF)
    go(rcopy(part.at[1, lo, :], fp.at[lo, :], fs.at[2], fr.at[2], up))
    pltpu.make_async_copy(hn, hn, hr.at[1]).wait()
    part[2, 384:768, :] = (part[2, 384:768, :].astype(F32) + hn[...].astype(F32)).astype(BF)
    go(rcopy(part.at[2, hi, :], fn.at[hi, :], fs.at[3], fr.at[3], down))

    came_back(rqa, qr)
    i, j = iotas((128, E))

    def join(ref, f, a):
        left = (j == i) & (i < HALF)
        right = (j == i + HALF) & (i < HALF)
        return (
            dot(ref[2 * f, :, a], left.astype(F32).astype(BF)) + dot(ref[2 * f + 1, :, a], right.astype(F32).astype(BF))
        ).astype(BF)

    left_half, right_half = slice(0, 128), slice(128, 256)
    picks = [pick_rows(f) for f in range(2)]
    cf = [dot(p, cells_ref[...]).astype(BF) for p in picks]
    gf = [dot(p, grad_ref[...]).astype(BF) for p in picks]
    dq = [join(rqa, f, left_half) for f in range(2)]
    at = [join(rqa, f, right_half) for f in range(2)]
    wp[0:192, :] = (t_dot(cf[0], dq[0]) + t_dot(cf[1], dq[1])).astype(BF)
    wp[576:768, :] = (t_dot(at[0], gf[0]) + t_dot(at[1], gf[1])).astype(BF)
    total = [gf[f].astype(F32) + dot_t(dq[f], wq_ref[...]) for f in range(2)]

    mine_sum = with_twin(3, z)
    pltpu.make_async_copy(fp.at[hi, :], fp.at[hi, :], fr.at[0]).wait()
    pltpu.make_async_copy(fn.at[lo, :], fn.at[lo, :], fr.at[1]).wait()
    pltpu.make_async_copy(fp.at[lo, :], fp.at[lo, :], fr.at[2]).wait()
    pltpu.make_async_copy(fn.at[hi, :], fn.at[hi, :], fr.at[3]).wait()
    fin[...] = (mine_sum + fp[...].astype(F32) + fn[...].astype(F32)).astype(BF)
    go_back(fin, rkv, ks, kr)
    came_back(rkv, kr)
    dk = [join(rkv, f, left_half) for f in range(2)]
    dv = [join(rkv, f, right_half) for f in range(2)]
    wp[192:384, :] = (t_dot(cf[0], dk[0]) + t_dot(cf[1], dk[1])).astype(BF)
    wp[384:576, :] = (t_dot(cf[0], dv[0]) + t_dot(cf[1], dv[1])).astype(BF)

    def slab(n):
        return pl.ds(pl.multiple_of(n * 48, 16), 48)

    def one(n):
        to = (i16 + n) % 16
        return rcopy(wp.at[slab(to), :], rs.at[i16], as_.at[n], ar.at[i16], dev16(to))

    def two(n):
        to = (i8 + n) % 8
        return rcopy(p2.at[i8], p2.at[i8], bs.at[n], br.at[i8], dev8(to))

    def three(n):
        to = (i16 + n) % 16
        return rcopy(wf.at[slab(i16), :], wf.at[slab(i16), :], cs.at[n], cr.at[i16], dev16(to))

    @pl.loop(1, 16)
    def _(n):
        one(n).start()

    for f in range(2):
        total[f] = total[f] + dot_t(dk[f], wk_ref[...]) + dot_t(dv[f], wv_ref[...])
    gc_ref[...] = (t_dot(picks[0], total[0].astype(BF)) + t_dot(picks[1], total[1].astype(BF))).astype(BF)

    rs[i16] = wp[slab(i16), :]

    @pl.loop(1, 16)
    def _(n):
        m = (i16 + n) % 16
        pltpu.make_async_copy(rs.at[m], rs.at[m], ar.at[m]).wait()

    acc = rs[0].astype(F32)
    for n in range(1, 16):
        acc = acc + rs[n].astype(F32)
    p2[i8] = acc.astype(BF)

    @pl.loop(1, 8)
    def _(n):
        two(n).start()

    @pl.loop(1, 8)
    def _(n):
        m = (i8 + n) % 8
        pltpu.make_async_copy(p2.at[m], p2.at[m], br.at[m]).wait()

    acc = p2[0].astype(F32)
    for n in range(1, 8):
        acc = acc + p2[n].astype(F32)
    wf[slab(i16), :] = acc.astype(BF)

    @pl.loop(1, 16)
    def _(n):
        three(n).start()

    @pl.loop(1, 16)
    def _(n):
        m = (i16 + n) % 16
        pltpu.make_async_copy(wf.at[slab(m), :], wf.at[slab(m), :], cr.at[m]).wait()

    gwq_ref[...] = wf[0:192, :].astype(F32)
    gwk_ref[...] = wf[192:384, :].astype(F32)
    gwv_ref[...] = wf[384:576, :].astype(F32)
    gwo_ref[...] = wf[576:768, :].astype(F32)

    for copy in sent:
        copy.wait_send()
    sent_back(qa_ref, rqa, qs, qr)
    sent_back(fin, rkv, ks, kr)

    @pl.loop(1, 16)
    def _(n):
        one(n).wait_send()
        three(n).wait_send()

    @pl.loop(1, 8)
    def _(n):
        two(n).wait_send()


def sds(shape, dtype=BF):
    return jax.ShapeDtypeStruct(shape, dtype)


VM = pl.BlockSpec(memory_space=pltpu.VMEM)
DMA = pltpu.SemaphoreType.DMA


def share(*args):
    return pl.pallas_call(
        share_kernel,
        out_shape=[sds((NR, 256)), sds((NQ, 256))],
        in_specs=[VM] * 7,
        out_specs=[VM] * 2,
        scratch_shapes=[
            pltpu.VMEM((4, ROWS, 256), BF), pltpu.VMEM((4, ROWS, 256), BF),
            DMA((4,)), DMA((4,)), DMA((4,)), DMA((4,)), DMA((8,)), DMA((8,)), DMA((4,)), DMA((4,)), DMA((16,)), DMA((16,)),
        ],
        compiler_params=pltpu.CompilerParams(collective_id=1, has_side_effects=True, vmem_limit_bytes=40 * 2**20),
        name="share",
    )(*args)


def attention(*args):
    return pl.pallas_call(
        attention_kernel,
        out_shape=[sds((NR, 256)), sds((NQ, 256))],
        in_specs=[VM] * 2,
        out_specs=[VM] * 2,
        scratch_shapes=[
            pltpu.VMEM((NR, NQ), BF), pltpu.VMEM((NR // KC, 8, NQ), F32),
            pltpu.VMEM((128, NR), BF), pltpu.VMEM((128, NR), BF),
            pltpu.VMEM((128, NQ), BF), pltpu.VMEM((128, NQ), BF),
            pltpu.VMEM((NQ, 128), BF), pltpu.VMEM((NQ, 128), BF),
            pltpu.VMEM((128, NQ), BF), pltpu.VMEM((128, NQ), BF),
            pltpu.VMEM((48, NQ), F32), pltpu.VMEM((8, NQ), F32),
            pltpu.VMEM((NR, 256), F32),
            pltpu.VMEM((128, NQ), BF), pltpu.VMEM((128, NQ), BF),
        ],
        compiler_params=pltpu.CompilerParams(vmem_limit_bytes=56 * 2**20),
        name="attention",
    )(*args)


def finish(*args):
    w = sds((E, E), F32)
    return pl.pallas_call(
        back_kernel,
        out_shape=[sds((2 * ROWS, E)), w, w, w, w],
        in_specs=[VM] * 8,
        out_specs=[VM] * 5,
        scratch_shapes=[
            pltpu.VMEM((4, NQ, 256), BF), pltpu.VMEM((3, NQ, 256), BF),
            pltpu.VMEM((384, 256), BF), pltpu.VMEM((384, 256), BF),
            pltpu.VMEM((NQ, 256), BF), pltpu.VMEM((NQ, 256), BF), pltpu.VMEM((NQ, 256), BF),
            pltpu.VMEM((4, ROWS, 256), BF), pltpu.VMEM((4, ROWS, 256), BF),
            pltpu.VMEM((768, E), BF), pltpu.VMEM((16, 48, E), BF), pltpu.VMEM((8, 48, E), BF), pltpu.VMEM((768, E), BF),
            DMA((4,)), DMA((4,)), DMA((4,)), DMA((4,)), DMA((2,)), DMA((2,)), DMA((4,)), DMA((4,)), DMA((4,)), DMA((4,)),
            DMA((16,)), DMA((16,)), DMA((8,)), DMA((8,)), DMA((16,)), DMA((16,)),
        ],
        compiler_params=pltpu.CompilerParams(collective_id=2, has_side_effects=True, vmem_limit_bytes=40 * 2**20),
        name="finish",
    )(*args)


def body(cells, w_query, w_key, w_value, w_out, train_flag, grad_out):
    flat_cells = cells.reshape(2 * ROWS, E)
    flat_grad = grad_out.reshape(2 * ROWS, E)
    weights = (w_query, w_key, w_value, w_out)
    kv, qg = share(flat_cells, flat_grad, *weights, train_flag.reshape(ROWS, 1))
    dkv, qa = attention(kv, qg)
    grad_cells, gq, gk, gv, go = finish(dkv, qa, flat_cells, flat_grad, *weights)
    return grad_cells.reshape(cells.shape), gq, gk, gv, go


def solution(mesh):
    return jax.shard_map(
        body,
        mesh=mesh,
        in_specs=(P("row", "feat", None), P(), P(), P(), P(), P("row"), P("row", "feat", None)),
        out_specs=(P("row", "feat", None), P(), P(), P(), P()),
        check_vma=False,
    )
```

```python
import jax
import jax.numpy as jnp
from jax import lax
from jax.experimental import pallas as pl
from jax.experimental.pallas import tpu as pltpu
from jax.sharding import PartitionSpec as P


HD = 32
SCALE = float(HD) ** -0.5
SCALE_LOG2E = SCALE * 1.4426950408889634
BIAS = -1e30
F32 = jnp.float32
BF = jnp.bfloat16
MESH = pl.DeviceIdType.MESH

E = 192
HALF = 96
ROWS = 192
NQ = 768
NR = 6144
KC = 768
PC = 384
BLOCKS = 8


def dot(a, b):
    return jnp.dot(a, b, preferred_element_type=F32)


def t_dot(a, b):
    return lax.dot_general(a, b, (((0,), (0,)), ((), ())), preferred_element_type=F32)


def place():
    row = lax.axis_index("row")
    feat = lax.axis_index("feat")
    return row // 8, (row // 2) % 4, row % 2, feat // 2, feat % 2


def device(z, x, yl, yh, c):
    return ((z * 4 + x) * 2 + yl, yh * 2 + c)


def iotas(shape):
    return lax.broadcasted_iota(jnp.int32, shape, 0), lax.broadcasted_iota(jnp.int32, shape, 1)


def ones_where(mask):
    return mask.astype(F32).astype(BF)


def shifted(shape, by, most=None):
    i, j = iotas(shape)
    mask = j == i + by
    if most is not None:
        mask = mask & (i < most)
    return ones_where(mask)


def by_feature():
    i, j = iotas((2 * ROWS, 2 * ROWS))
    second = i >= ROWS
    return ones_where(j == jnp.where(second, 2 * (i - ROWS) + 1, 2 * i))


def rcopy(src, dst, send, recv, to):
    return pltpu.make_async_remote_copy(
        src_ref=src, dst_ref=dst, send_sem=send, recv_sem=recv, device_id=to, device_id_type=MESH
    )


def wait_for(ref, sem):
    pltpu.make_async_copy(ref, ref, sem).wait()


def share_kernel(cells_ref, grad_ref, flag_ref, pk_ref, gp_ref, cnt_ref,
                 cs, gs, cb, zb, s1, r1, s2, r2, zs, zr, fs, fr, ts, tr, ns, nr, ms, mr):
    z, x, yl, yh, c = place()
    mine = x // 2 == c
    own = jnp.where(mine, 1, 0)
    zp, zo, zn = (z + 1) % 4, (z + 2) % 4, (z + 3) % 4
    up, down, twin = device(zp, x, yl, yh, c), device(zn, x, yl, yh, c), device(z, x, yl, yh, 1 - c)
    slot = (x % 2) * 2 + yl
    i8 = x * 2 + yl

    def dev8(n):
        return device(z, n // 2, n % 2, yh, c)

    barrier = pltpu.get_barrier_semaphore()

    def greet(to):
        pl.semaphore_signal(barrier, inc=1, device_id=to, device_id_type=MESH)

    for s in range(4):
        @pl.when(jnp.logical_not(jnp.logical_and(mine, slot == s)))
        def _():
            greet(device(z, 2 * c + s // 2, s % 2, yh, x // 2))
    for to in (up, down, twin):
        greet(to)
    for n in range(1, 8):
        greet(dev8((i8 + n) % 8))
    for n in range(1, 4):
        greet(device((z + n) % 4, x, yl, yh, c))

    sort = by_feature()
    left, right = shifted((ROWS, 2 * E), 0), shifted((ROWS, 2 * E), E)

    def pack(ref, out):
        rows = dot(sort, ref[...].reshape(2 * ROWS, E)).astype(BF)
        for f in range(2):
            r = f * ROWS
            out[f] = (dot(rows[r:r + HALF], left) + dot(rows[r + HALF:r + ROWS], right)).astype(BF)

    pack(cells_ref, cs)
    pack(grad_ref, gs)

    def add(n, total):
        return total + flag_ref[n]

    flags = lax.fori_loop(0, ROWS, add, jnp.int32(0), unroll=16)
    cb[i8] = jnp.full((8, 128), flags.astype(F32), F32)

    pl.semaphore_wait(barrier, 4 - own + 3 + 7 + 3)

    my_rows = pl.ds(pl.multiple_of(((z * 4 + x) * 2 + yl) * HALF, HALF), HALF)
    my_slot = pl.ds(pl.multiple_of(slot * HALF, HALF), HALF)

    def first(j):
        to = device(z, 2 * c + j // 2, j % 2, yh, x // 2)
        a = rcopy(cs.at[j // 2], pk_ref.at[my_rows, :], s1.at[j], r1.at[slot], to)
        b = rcopy(gs.at[j // 2], gp_ref.at[my_slot, :], s2.at[j], r2.at[slot], to)
        return a, b

    for j in range(4):
        keep = jnp.logical_and(mine, slot == j)

        @pl.when(keep)
        def _():
            pltpu.make_async_copy(cs.at[j // 2], pk_ref.at[my_rows, :], r1.at[slot]).start()

        @pl.when(jnp.logical_not(keep))
        def _():
            first(j)[0].start()

    def plane(n):
        return rcopy(cb.at[i8], cb.at[i8], ns.at[n], nr.at[i8], dev8((i8 + n) % 8))

    def column(n):
        return rcopy(zb.at[z], zb.at[z], ms.at[n], mr.at[z], device((z + n) % 4, x, yl, yh, c))

    def rows_of(zz, cc, s):
        return pl.ds(pl.multiple_of((zz * 2 + cc) * PC + s * HALF, HALF), HALF)

    def move(zz, s, send, recv, to):
        r = rows_of(zz, c, s)
        return rcopy(pk_ref.at[r, :], pk_ref.at[r, :], send, recv, to)

    def landed(zz, cc, s, recv):
        wait_for(pk_ref.at[rows_of(zz, cc, s), :], recv)

    sent = []

    def go(copy):
        copy.start()
        sent.append(copy)

    for s in range(4):
        landed(z, c, s, r1.at[s])
        go(move(z, s, zs.at[s], zr.at[s], up))
        go(move(z, s, zs.at[4 + s], zr.at[4 + s], down))
        go(move(z, s, ts.at[s], tr.at[s], twin))

    for n in range(1, 8):
        go(plane(n))
    for j in range(4):
        keep = jnp.logical_and(mine, slot == j)

        @pl.when(keep)
        def _():
            pltpu.make_async_copy(gs.at[j // 2], gp_ref.at[my_slot, :], r2.at[slot]).start()

        @pl.when(jnp.logical_not(keep))
        def _():
            first(j)[1].start()

    for i in range(4):
        s = i
        landed(zn, c, s, zr.at[s])
        if s < 2:
            go(move(zn, s, fs.at[s], fr.at[s], up))
        go(move(zn, s, ts.at[4 + s], tr.at[4 + s], twin))
        s = (i + 2) % 4
        landed(zp, c, s, zr.at[4 + s])
        if s >= 2:
            go(move(zp, s, fs.at[s], fr.at[s], down))
        go(move(zp, s, ts.at[8 + s], tr.at[8 + s], twin))

    for n in range(1, 8):
        m = (i8 + n) % 8
        wait_for(cb.at[m], nr.at[m])
    total = cb[0]
    for n in range(1, 8):
        total = total + cb[n]
    zb[z] = total
    for n in range(1, 4):
        go(column(n))

    for s in (0, 2, 1, 3):
        landed(zo, c, s, fr.at[s])
        go(move(zo, s, ts.at[12 + s], tr.at[12 + s], twin))

    for n in range(1, 4):
        m = (z + n) % 4
        wait_for(zb.at[m], mr.at[m])
    cnt_ref[...] = zb[0] + zb[1] + zb[2] + zb[3]

    for n, zz in ((0, z), (1, zn), (2, zp), (3, zo)):
        for s in range(4):
            landed(zz, 1 - c, s, tr.at[4 * n + s])
    for s in range(4):
        wait_for(gp_ref.at[pl.ds(s * HALF, HALF), :], r2.at[s])
    for copy in sent:
        copy.wait_send()
    for j in range(4):
        @pl.when(jnp.logical_not(jnp.logical_and(mine, slot == j)))
        def _():
            a, b = first(j)
            a.wait_send()
            b.wait_send()


def attention_kernel(pk_ref, gp_ref, cnt_ref, wq_ref, wk_ref, wv_ref, wo_ref, g_ref, gq_ref, w_ref,
                     e_ref, mb_ref, kv_ref, kT_ref, vT_ref, pT_ref, qT_ref, gT_ref, qm_ref, gm_ref,
                     qmT_ref, gmT_ref, acc_ref, m_ref, dkv_acc, dkv_ref, attT_ref, dqT_ref, wacc_ref,
                     wkva, wkvb, wqa, wqb, wga, wgb, ua, ub):
    z, x, yl, yh, c = place()
    train = jnp.max(cnt_ref[...]).astype(jnp.int32)
    nk = lax.div(train + KC - 1, KC)

    def rows(n):
        return pl.ds(pl.multiple_of(n * KC, KC), KC)

    def packs(n):
        return pl.ds(pl.multiple_of(n * PC, PC), PC)

    @pl.loop(nk, BLOCKS)
    def _(n):
        g_ref[packs(n), :] = jnp.zeros((PC, 384), BF)

    i, j = iotas((E, 128))
    heads = ones_where((i == j + HALF * yl) & (j < HALF))
    wq = dot(wq_ref[...], heads).astype(BF)
    wk = dot(wk_ref[...], heads).astype(BF)
    wv = dot(wv_ref[...], heads).astype(BF)
    wo = t_dot(wo_ref[...], heads).astype(BF)
    for a, b, w in ((wkva, wkvb, jnp.concatenate([wk, wv], 1)), (wqa, wqb, wq), (wga, wgb, wo)):
        a[0:192, :] = w
        a[192:256, :] = jnp.zeros((64, w.shape[1]), BF)
        b[64:256, :] = w
        b[0:64, :] = jnp.zeros((64, w.shape[1]), BF)
    left, right = shifted((E, 2 * E), 0), shifted((E, 2 * E), E)
    for n, w in enumerate((wk, wv, wq)):
        ua[128 * n:128 * n + 128, :] = t_dot(w, left).astype(BF)
        ub[128 * n:128 * n + 128, :] = t_dot(w, right).astype(BF)

    lane = lax.broadcasted_iota(jnp.int32, (PC, 128), 1)
    sub = lax.broadcasted_iota(jnp.int32, (PC, 128), 0)
    real = sub + 96 * ((sub >= 96).astype(jnp.int32) + (sub >= 192).astype(jnp.int32) + (sub >= 288).astype(jnp.int32))
    v_extra = jnp.where((lane >= HALF) & (lane < HALF + 3), 1.0, 0.0)

    @pl.loop(0, nk)
    def _(n):
        p = pk_ref[packs(n), :]
        pT_ref[:, packs(n)] = p.T
        for h, (part, w) in enumerate(((p[:, 0:256], wkva), (p[:, 128:384], wkvb))):
            kv = dot(part, w[...])
            bias = jnp.where((lane == HALF) & (real + (n * KC + HALF * h) >= train), BIAS, 0.0)
            r = pl.ds(pl.multiple_of(n * KC + PC * h, PC), PC)
            k = (kv[:, 0:128] + bias).astype(BF)
            v = (kv[:, 128:256] + v_extra).astype(BF)
            kv_ref[r, 0:128] = k
            kv_ref[r, 128:256] = v
            kT_ref[:, r] = k.T
            vT_ref[:, r] = v.T

    block = z * 2 + c
    po = pk_ref[packs(block), :]
    go = gp_ref[...]
    for src, a, b, out in ((po, wqa, wqb, qT_ref), (go, wga, wgb, gT_ref)):
        out[:, 0:PC] = dot(src[:, 0:256], a[...]).astype(BF).T
        out[:, PC:NQ] = dot(src[:, 128:384], b[...]).astype(BF).T
    attT_ref[...] = jnp.zeros_like(attT_ref)
    dqT_ref[...] = jnp.zeros_like(dqT_ref)
    wacc_ref[...] = jnp.zeros_like(wacc_ref)
    i16 = lax.broadcasted_iota(jnp.int32, (16, NQ), 0)

    for h in range(3):
        hs = slice(32 * h, 32 * h + 32)
        qmT_ref[...] = jnp.zeros_like(qmT_ref)
        qmT_ref[hs, :] = qT_ref[hs, :]
        qm_ref[...] = qmT_ref[...].T
        qmT_ref[96:112, :] = jnp.where(i16 == 0, 1.0, 0.0).astype(BF)
        acc_ref[...] = jnp.zeros_like(acc_ref)
        m_ref[...] = jnp.full_like(m_ref, BIAS)

        @pl.loop(0, nk)
        def _(n):
            r = rows(n)
            vt = jnp.concatenate([vT_ref[hs, r], vT_ref[96:112, r]], 0)
            s = dot(kv_ref[r, 0:128], qmT_ref[...]) * SCALE_LOG2E
            old = m_ref[0:1, :]
            new = jnp.maximum(old, jnp.ceil(jnp.max(s, axis=0, keepdims=True)))
            e = jnp.exp2(s - new).astype(BF)
            e_ref[r, :] = e
            m_ref[0:1, :] = new
            mb_ref[n, 0:1, :] = new
            acc_ref[...] = acc_ref[...] * jnp.exp2(old - new) + dot(vt, e)

        inv = 1.0 / acc_ref[32:33, :]
        att = (acc_ref[0:32, :] * inv).astype(BF)
        attT_ref[hs, :] = att
        gp = (gT_ref[hs, :].astype(F32) * inv).astype(BF)
        delta = -jnp.sum(gp.astype(F32) * att.astype(F32), axis=0, keepdims=True)
        d0 = delta.astype(BF).astype(F32)
        d1 = (delta - d0).astype(BF).astype(F32)
        d2 = delta - d0 - d1
        gmT_ref[...] = jnp.zeros_like(gmT_ref)
        gmT_ref[hs, :] = gp
        gm_ref[...] = gmT_ref[...].T
        gmT_ref[96:112, :] = jnp.where(i16 == 0, d0, jnp.where(i16 == 1, d1, jnp.where(i16 == 2, d2, 0.0))).astype(BF)
        acc_ref[...] = jnp.zeros_like(acc_ref)

        @pl.loop(0, nk)
        def _(n):
            r = rows(n)
            ga = dot(kv_ref[r, 128:256], gmT_ref[...]).astype(BF)
            es = e_ref[r, :] * jnp.exp2(mb_ref[n, 0:1, :] - m_ref[0:1, :]).astype(BF)
            ds = es * ga
            dv = dot(es, gm_ref[...])
            dk = dot(ds, qm_ref[...]) * SCALE
            acc_ref[0:32, :] += dot(kT_ref[hs, r], ds)
            if h == 0:
                dkv_acc[r, 0:128] = dk
                dkv_acc[r, 128:256] = dv
            elif h == 1:
                dkv_acc[r, 0:128] += dk
                dkv_acc[r, 128:256] += dv
            else:
                dkv_ref[:, 0:128] = (dkv_acc[r, 0:128] + dk).astype(BF)
                dkv_ref[:, 128:256] = (dkv_acc[r, 128:256] + dv).astype(BF)
                da, db = dkv_ref[0:PC, :], dkv_ref[PC:KC, :]
                g_ref[packs(n), :] = (dot(da, ua[0:256, :]) + dot(db, ub[0:256, :])).astype(BF)
                wacc_ref[...] += dot(pT_ref[0:E, packs(n)], da) + dot(pT_ref[E:2 * E, packs(n)], db)

        dqT_ref[hs, :] = (acc_ref[0:32, :] * SCALE).astype(BF)

    dq, at = dqT_ref[...].T, attT_ref[...].T
    gq_ref[...] = dot(dq[0:PC], ua[256:384, :]) + dot(dq[PC:NQ], ub[256:384, :])
    poT, goT = po.T, go.T
    w_q = dot(poT[0:E], dq[0:PC]) + dot(poT[E:2 * E], dq[PC:NQ])
    w_o = dot(goT[0:E], at[0:PC]) + dot(goT[E:2 * E], at[PC:NQ])
    w_ref[...] = (
        dot(w_q.astype(BF), shifted((128, 384), 0, HALF))
        + dot(w_o.astype(BF), shifted((128, 384), HALF, HALF))
        + dot(wacc_ref[:, 0:128].astype(BF), shifted((128, 384), 2 * HALF, HALF))
        + dot(wacc_ref[:, 128:256].astype(BF), shifted((128, 384), 3 * HALF, HALF))
    ).astype(BF)


def reduce_kernel(g_ref, gq_ref, w_ref, ret_ref, wf_ref,
                  tw, part, hp, hn, fp, fn, fin, rs, p2,
                  ts, tr, hs_, hr, fs, fr, ks, kr, as_, ar, bs, br, cs, cr):
    z, x, yl, yh, c = place()
    mine = x // 2 == c
    own = jnp.where(mine, 1, 0)
    zp, zo, zn = (z + 1) % 4, (z + 2) % 4, (z + 3) % 4
    up, down, twin = device(zp, x, yl, yh, c), device(zn, x, yl, yh, c), device(z, x, yl, yh, 1 - c)
    slot = (x % 2) * 2 + yl
    i16 = z * 4 + x
    i8 = (yh * 2 + yl) * 2 + c
    owner = i16 < SLABS
    owns = jnp.where(owner, 1, 0)

    def dev16(n):
        return device(n // 4, n % 4, yl, yh, c)

    def dev8(n):
        return device(z, x, (n // 2) % 2, n // 4, n % 2)

    barrier = pltpu.get_barrier_semaphore()

    def greet(to):
        pl.semaphore_signal(barrier, inc=1, device_id=to, device_id_type=MESH)

    for to in (twin, up, down):
        greet(to)
    for j in range(4):
        @pl.when(jnp.logical_not(jnp.logical_and(mine, slot == j)))
        def _():
            greet(device(z, 2 * c + j // 2, j % 2, yh, x // 2))

    @pl.loop(1, 16)
    def _(n):
        greet(dev16((i16 + n) % 16))

    @pl.loop(1, 8)
    def _(n):
        greet(dev8((i8 + n) % 8))

    pl.semaphore_wait(barrier, 3 + 4 - own + 15 + 7)

    sent = []

    def go(copy):
        copy.start()
        sent.append(copy)

    def block(zz, cc):
        return pl.ds(pl.multiple_of((zz * 2 + cc) * PC, PC), PC)

    for n, zz in enumerate((zo, zp, zn, z)):
        go(rcopy(g_ref.at[block(zz, 1 - c), :], tw.at[n], ts.at[n], tr.at[n], twin))

    def slab(n):
        return pl.ds(pl.multiple_of(n * 16, 16), 16)

    def one(n):
        to = (i16 + n) % 16
        return to < SLABS, rcopy(w_ref.at[slab(jnp.minimum(to, SLABS - 1)), :], rs.at[i16], as_.at[n], ar.at[i16], dev16(to))

    def two(n):
        return rcopy(p2.at[i8], p2.at[i8], bs.at[n], br.at[i8], dev8((i8 + n) % 8))

    def three(n):
        mine_ = slab(jnp.minimum(i16, SLABS - 1))
        return rcopy(wf_ref.at[:, mine_, :], wf_ref.at[:, mine_, :], cs.at[n], cr.at[i16], dev16((i16 + n) % 16))

    @pl.loop(1, 16)
    def _(n):
        ok, copy = one(n)

        @pl.when(ok)
        def _():
            copy.start()

    def with_twin(n, zz):
        wait_for(tw.at[n], tr.at[n])
        return g_ref[block(zz, c), :].astype(F32) + tw[n].astype(F32)

    lo, hi = pl.ds(0, 192), pl.ds(192, 192)
    part[0] = with_twin(0, zo).astype(BF)
    go(rcopy(part.at[0, lo, :], hp, hs_.at[0], hr.at[0], up))
    go(rcopy(part.at[0, hi, :], hn, hs_.at[1], hr.at[1], down))
    part[1] = with_twin(1, zp).astype(BF)
    go(rcopy(part.at[1, hi, :], fp.at[hi, :], fs.at[0], fr.at[0], up))
    part[2] = with_twin(2, zn).astype(BF)
    go(rcopy(part.at[2, lo, :], fn.at[lo, :], fs.at[1], fr.at[1], down))

    @pl.when(owner)
    def _():
        rs[i16] = w_ref[slab(jnp.minimum(i16, SLABS - 1)), :]

        @pl.loop(1, 16)
        def _(n):
            m = (i16 + n) % 16
            wait_for(rs.at[m], ar.at[m])

        acc = rs[0].astype(F32)
        for n in range(1, 16):
            acc = acc + rs[n].astype(F32)
        p2[i8] = acc.astype(BF)

        @pl.loop(1, 8)
        def _(n):
            two(n).start()

    wait_for(hp, hr.at[0])
    part[1, 0:192, :] = (part[1, 0:192, :].astype(F32) + hp[...].astype(F32)).astype(BF)
    go(rcopy(part.at[1, lo, :], fp.at[lo, :], fs.at[2], fr.at[2], up))
    wait_for(hn, hr.at[1])
    part[2, 192:384, :] = (part[2, 192:384, :].astype(F32) + hn[...].astype(F32)).astype(BF)
    go(rcopy(part.at[2, hi, :], fn.at[hi, :], fs.at[3], fr.at[3], down))

    @pl.when(owner)
    def _():
        @pl.loop(1, 8)
        def _(n):
            m = (i8 + n) % 8
            wait_for(p2.at[m], br.at[m])

        for half in range(2):
            n = 2 * half
            acc = p2[n].astype(F32) + p2[n + 1].astype(F32) + p2[n + 4].astype(F32) + p2[n + 5].astype(F32)
            wf_ref[half, slab(jnp.minimum(i16, SLABS - 1)), :] = acc.astype(BF)

        @pl.loop(1, 16)
        def _(n):
            three(n).start()

    total = with_twin(3, z) + gq_ref[...]
    wait_for(fp.at[hi, :], fr.at[0])
    wait_for(fn.at[lo, :], fr.at[1])
    wait_for(fp.at[lo, :], fr.at[2])
    wait_for(fn.at[hi, :], fr.at[3])
    fin[...] = (total + fp[...].astype(F32) + fn[...].astype(F32)).astype(BF)

    def back(s):
        to = device(z, 2 * c + s // 2, s % 2, yh, x // 2)
        return rcopy(fin.at[pl.ds(s * HALF, HALF), :], ret_ref.at[slot], ks.at[s], kr.at[slot], to)

    for s in range(4):
        keep = jnp.logical_and(mine, slot == s)

        @pl.when(keep)
        def _():
            pltpu.make_async_copy(fin.at[pl.ds(s * HALF, HALF), :], ret_ref.at[slot], kr.at[slot]).start()

        @pl.when(jnp.logical_not(keep))
        def _():
            back(s).start()

    for n in range(4):
        wait_for(ret_ref.at[n], kr.at[n])

    @pl.loop(1, 16)
    def _(n):
        m = (i16 + n) % 16

        @pl.when(m < SLABS)
        def _():
            r = slab(jnp.minimum(m, SLABS - 1))
            wait_for(wf_ref.at[:, r, :], cr.at[m])

    for copy in sent:
        copy.wait_send()
    for s in range(4):
        @pl.when(jnp.logical_not(jnp.logical_and(mine, slot == s)))
        def _():
            back(s).wait_send()

    @pl.loop(1, 16)
    def _(n):
        ok, copy = one(n)

        @pl.when(ok)
        def _():
            copy.wait_send()

        @pl.when(owner)
        def _():
            three(n).wait_send()

    @pl.when(owner)
    def _():
        @pl.loop(1, 8)
        def _(n):
            two(n).wait_send()


def final_kernel(ret_ref, wf_ref, grad_ref, gc_ref, gwq_ref, gwk_ref, gwv_ref, gwo_ref):
    sort = by_feature()
    i, j = iotas((256, E))
    right = ones_where(i == j + 64)
    total = grad_ref[...].reshape(2 * ROWS, E).astype(F32)
    for half in range(2):
        parts = []
        for f in range(2):
            r = ret_ref[2 * f + half]
            parts += [r[:, 0:E], dot(r[:, 128:384], right).astype(BF)]
        total = total + t_dot(sort, jnp.concatenate(parts, 0))
    gc_ref[...] = total.astype(BF).reshape(ROWS, 2, E)

    i, j = iotas((384, E))

    def weight(first):
        low = ones_where((i == j + first) & (j < HALF))
        high = ones_where((i == j - HALF + first) & (j >= HALF))
        return dot(wf_ref[0], low) + dot(wf_ref[1], high)

    gwq_ref[...] = weight(0)
    gwo_ref[...] = weight(HALF).T
    gwk_ref[...] = weight(2 * HALF)
    gwv_ref[...] = weight(3 * HALF)


SLABS = 12
VM = pl.BlockSpec(memory_space=pltpu.VMEM)
SM = pl.BlockSpec(memory_space=pltpu.SMEM)
DMA = pltpu.SemaphoreType.DMA


def sds(shape, dtype=BF):
    return jax.ShapeDtypeStruct(shape, dtype)


def share(*args):
    return pl.pallas_call(
        share_kernel,
        out_shape=[sds((NR // 2, 384)), sds((PC, 384)), sds((8, 128), F32)],
        in_specs=[VM, VM, SM],
        out_specs=[VM] * 3,
        scratch_shapes=[
            pltpu.VMEM((2, HALF, 384), BF), pltpu.VMEM((2, HALF, 384), BF),
            pltpu.VMEM((8, 8, 128), F32), pltpu.VMEM((4, 8, 128), F32),
            DMA((4,)), DMA((4,)), DMA((4,)), DMA((4,)), DMA((8,)), DMA((8,)), DMA((4,)), DMA((4,)), DMA((16,)), DMA((16,)),
            DMA((8,)), DMA((8,)), DMA((4,)), DMA((4,)),
        ],
        compiler_params=pltpu.CompilerParams(collective_id=1, has_side_effects=True, vmem_limit_bytes=24 * 2**20),
        name="share",
    )(*args)


def attention(*args):
    return pl.pallas_call(
        attention_kernel,
        out_shape=[sds((NR // 2, 384)), sds((PC, 384), F32), sds((E, 384))],
        in_specs=[VM] * 7,
        out_specs=[VM] * 3,
        scratch_shapes=[
            pltpu.VMEM((NR, NQ), BF), pltpu.VMEM((BLOCKS, 8, NQ), F32), pltpu.VMEM((NR, 256), BF),
            pltpu.VMEM((128, NR), BF), pltpu.VMEM((128, NR), BF), pltpu.VMEM((384, NR // 2), BF),
            pltpu.VMEM((128, NQ), BF), pltpu.VMEM((128, NQ), BF),
            pltpu.VMEM((NQ, 128), BF), pltpu.VMEM((NQ, 128), BF),
            pltpu.VMEM((128, NQ), BF), pltpu.VMEM((128, NQ), BF),
            pltpu.VMEM((48, NQ), F32), pltpu.VMEM((8, NQ), F32),
            pltpu.VMEM((NR, 256), F32), pltpu.VMEM((KC, 256), BF),
            pltpu.VMEM((128, NQ), BF), pltpu.VMEM((128, NQ), BF), pltpu.VMEM((E, 256), F32),
            pltpu.VMEM((256, 256), BF), pltpu.VMEM((256, 256), BF), pltpu.VMEM((256, 128), BF), pltpu.VMEM((256, 128), BF),
            pltpu.VMEM((256, 128), BF), pltpu.VMEM((256, 128), BF), pltpu.VMEM((384, 384), BF), pltpu.VMEM((384, 384), BF),
        ],
        compiler_params=pltpu.CompilerParams(vmem_limit_bytes=VLIM * 2**20),
        name="attention",
    )(*args)


VLIM = 46


def reduce(*args):
    return pl.pallas_call(
        reduce_kernel,
        out_shape=[sds((4, HALF, 384)), sds((2, E, 384))],
        in_specs=[VM] * 3,
        out_specs=[VM] * 2,
        scratch_shapes=[
            pltpu.VMEM((4, PC, 384), BF), pltpu.VMEM((3, PC, 384), BF),
            pltpu.VMEM((192, 384), BF), pltpu.VMEM((192, 384), BF),
            pltpu.VMEM((PC, 384), BF), pltpu.VMEM((PC, 384), BF), pltpu.VMEM((PC, 384), BF),
            pltpu.VMEM((16, 16, 384), BF), pltpu.VMEM((8, 16, 384), BF),
            DMA((4,)), DMA((4,)), DMA((2,)), DMA((2,)), DMA((4,)), DMA((4,)), DMA((4,)), DMA((4,)),
            DMA((16,)), DMA((16,)), DMA((8,)), DMA((8,)), DMA((16,)), DMA((16,)),
        ],
        compiler_params=pltpu.CompilerParams(collective_id=2, has_side_effects=True, vmem_limit_bytes=24 * 2**20),
        name="reduce",
    )(*args)


def final(*args):
    w = sds((E, E), F32)
    return pl.pallas_call(
        final_kernel,
        out_shape=[sds((ROWS, 2, E)), w, w, w, w],
        in_specs=[VM] * 3,
        out_specs=[VM] * 5,
        compiler_params=pltpu.CompilerParams(vmem_limit_bytes=24 * 2**20),
        name="final",
    )(*args)


def body(cells, w_query, w_key, w_value, w_out, train_flag, grad_out):
    packs, grads, count = share(cells, grad_out, train_flag)
    g, gq, w = attention(packs, grads, count, w_query, w_key, w_value, w_out)
    ret, wf = reduce(g, gq, w)
    return final(ret, wf, grad_out)


def solution(mesh):
    return jax.shard_map(
        body,
        mesh=mesh,
        in_specs=(P("row", "feat", None), P(), P(), P(), P(), P("row"), P("row", "feat", None)),
        out_specs=(P("row", "feat", None), P(), P(), P(), P()),
        check_vma=False,
    )
```

```python
import jax
import jax.numpy as jnp
from jax import lax
from jax.experimental import pallas as pl
from jax.experimental.pallas import tpu as pltpu
from jax.sharding import PartitionSpec as P


HD = 32
SCALE = float(HD) ** -0.5
SCALE_LOG2E = SCALE * 1.4426950408889634
BIAS = -1e30
F32 = jnp.float32
BF = jnp.bfloat16
MESH = pl.DeviceIdType.MESH

E = 192
HALF = 96
ROWS = 192
NQ = 768
NR = 6144
KC = 768
PC = 384
BLOCKS = 8


def dot(a, b):
    return jnp.dot(a, b, preferred_element_type=F32)


def t_dot(a, b):
    return lax.dot_general(a, b, (((0,), (0,)), ((), ())), preferred_element_type=F32)


def place():
    row = lax.axis_index("row")
    feat = lax.axis_index("feat")
    return row // 8, (row // 2) % 4, row % 2, feat // 2, feat % 2


def device(z, x, yl, yh, c):
    return ((z * 4 + x) * 2 + yl, yh * 2 + c)


def iotas(shape):
    return lax.broadcasted_iota(jnp.int32, shape, 0), lax.broadcasted_iota(jnp.int32, shape, 1)


def ones_where(mask):
    return mask.astype(F32).astype(BF)


def shifted(shape, by, most=None):
    i, j = iotas(shape)
    mask = j == i + by
    if most is not None:
        mask = mask & (i < most)
    return ones_where(mask)


def by_feature():
    i, j = iotas((2 * ROWS, 2 * ROWS))
    second = i >= ROWS
    return ones_where(j == jnp.where(second, 2 * (i - ROWS) + 1, 2 * i))


def rcopy(src, dst, send, recv, to):
    return pltpu.make_async_remote_copy(
        src_ref=src, dst_ref=dst, send_sem=send, recv_sem=recv, device_id=to, device_id_type=MESH
    )


def wait_for(ref, sem):
    pltpu.make_async_copy(ref, ref, sem).wait()


def share_kernel(in_ref, pk_ref, gp_ref, cnt_ref, cs, gs, cb, zb, s1, r1, s2, r2, zs, zr, fs, fr, ts, tr, ns, nr, ms, mr):
    z, x, yl, yh, c = place()
    mine = x // 2 == c
    own = jnp.where(mine, 1, 0)
    zp, zo, zn = (z + 1) % 4, (z + 2) % 4, (z + 3) % 4
    up, down, twin = device(zp, x, yl, yh, c), device(zn, x, yl, yh, c), device(z, x, yl, yh, 1 - c)
    slot = (x % 2) * 2 + yl
    i8 = x * 2 + yl

    def dev8(n):
        return device(z, n // 2, n % 2, yh, c)

    barrier = pltpu.get_barrier_semaphore()

    def greet(to):
        pl.semaphore_signal(barrier, inc=1, device_id=to, device_id_type=MESH)

    for s in range(4):
        @pl.when(jnp.logical_not(jnp.logical_and(mine, slot == s)))
        def _():
            greet(device(z, 2 * c + s // 2, s % 2, yh, x // 2))
    for to in (up, down, twin):
        greet(to)
    for n in range(1, 8):
        greet(dev8((i8 + n) % 8))
    for n in range(1, 4):
        greet(device((z + n) % 4, x, yl, yh, c))

    sort = by_feature()
    left, right = shifted((ROWS, 2 * E), 0), shifted((ROWS, 2 * E), E)

    def pack(first, out):
        rows = dot(sort, in_ref[first:first + ROWS].reshape(2 * ROWS, E)).astype(BF)
        for f in range(2):
            r = f * ROWS
            out[f] = (dot(rows[r:r + HALF], left) + dot(rows[r + HALF:r + ROWS], right)).astype(BF)

    pack(0, cs)
    pl.semaphore_wait(barrier, 4 - own + 3 + 7 + 3)

    my_rows = pl.ds(pl.multiple_of(((z * 4 + x) * 2 + yl) * HALF, HALF), HALF)
    my_slot = pl.ds(pl.multiple_of(slot * HALF, HALF), HALF)

    def first(j):
        to = device(z, 2 * c + j // 2, j % 2, yh, x // 2)
        a = rcopy(cs.at[j // 2], pk_ref.at[my_rows, :], s1.at[j], r1.at[slot], to)
        b = rcopy(gs.at[j // 2], gp_ref.at[my_slot, :], s2.at[j], r2.at[slot], to)
        return a, b

    for j in range(4):
        keep = jnp.logical_and(mine, slot == j)

        @pl.when(keep)
        def _():
            pltpu.make_async_copy(cs.at[j // 2], pk_ref.at[my_rows, :], r1.at[slot]).start()

        @pl.when(jnp.logical_not(keep))
        def _():
            first(j)[0].start()

    flags = jnp.sum(in_ref[2 * ROWS, 0:1, :].astype(F32), axis=1, keepdims=True)
    cb[i8] = jnp.broadcast_to(flags, (8, 128))

    def plane(n):
        return rcopy(cb.at[i8], cb.at[i8], ns.at[n], nr.at[i8], dev8((i8 + n) % 8))

    def column(n):
        return rcopy(zb.at[z], zb.at[z], ms.at[n], mr.at[z], device((z + n) % 4, x, yl, yh, c))

    def rows_of(zz, cc, s):
        return pl.ds(pl.multiple_of((zz * 2 + cc) * PC + s * HALF, HALF), HALF)

    def move(zz, s, send, recv, to):
        r = rows_of(zz, c, s)
        return rcopy(pk_ref.at[r, :], pk_ref.at[r, :], send, recv, to)

    def landed(zz, cc, s, recv):
        wait_for(pk_ref.at[rows_of(zz, cc, s), :], recv)

    sent = []

    def go(copy):
        copy.start()
        sent.append(copy)

    for n in range(1, 8):
        go(plane(n))
    for s in range(4):
        landed(z, c, s, r1.at[s])
        go(move(z, s, zs.at[s], zr.at[s], up))
        go(move(z, s, zs.at[4 + s], zr.at[4 + s], down))
        go(move(z, s, ts.at[s], tr.at[s], twin))

    pack(ROWS, gs)
    for j in range(4):
        keep = jnp.logical_and(mine, slot == j)

        @pl.when(keep)
        def _():
            pltpu.make_async_copy(gs.at[j // 2], gp_ref.at[my_slot, :], r2.at[slot]).start()

        @pl.when(jnp.logical_not(keep))
        def _():
            first(j)[1].start()

    for i in range(4):
        s = i
        landed(zn, c, s, zr.at[s])
        if s < 2:
            go(move(zn, s, fs.at[s], fr.at[s], up))
        go(move(zn, s, ts.at[4 + s], tr.at[4 + s], twin))
        s = (i + 2) % 4
        landed(zp, c, s, zr.at[4 + s])
        if s >= 2:
            go(move(zp, s, fs.at[s], fr.at[s], down))
        go(move(zp, s, ts.at[8 + s], tr.at[8 + s], twin))

    for n in range(1, 8):
        m = (i8 + n) % 8
        wait_for(cb.at[m], nr.at[m])
    total = cb[0]
    for n in range(1, 8):
        total = total + cb[n]
    zb[z] = total
    for n in range(1, 4):
        go(column(n))

    for s in (0, 2, 1, 3):
        landed(zo, c, s, fr.at[s])
        go(move(zo, s, ts.at[12 + s], tr.at[12 + s], twin))

    for n in range(1, 4):
        m = (z + n) % 4
        wait_for(zb.at[m], mr.at[m])
    cnt_ref[...] = zb[0] + zb[1] + zb[2] + zb[3]

    for n, zz in ((0, z), (1, zn), (2, zp), (3, zo)):
        for s in range(4):
            landed(zz, 1 - c, s, tr.at[4 * n + s])
    for s in range(4):
        wait_for(gp_ref.at[pl.ds(s * HALF, HALF), :], r2.at[s])
    for copy in sent:
        copy.wait_send()
    for j in range(4):
        @pl.when(jnp.logical_not(jnp.logical_and(mine, slot == j)))
        def _():
            a, b = first(j)
            a.wait_send()
            b.wait_send()


def attention_kernel(pk_ref, gp_ref, cnt_ref, weights, g_ref, gq_ref, w_ref, e_ref, mb_ref, kv_ref, qT_ref, gT_ref, qm_ref, gm_ref,
                     qmT_ref, gmT_ref, acc_ref, m_ref, s_ref, dkv_ref, attT_ref, dqT_ref, wacc_ref,
                     wkva, wkvb, wqa, wqb, wga, wgb, ua, ub):
    z, x, yl, yh, c = place()
    train = jnp.max(cnt_ref[...]).astype(jnp.int32)
    nk = lax.div(train + KC - 1, KC)

    def rows(n):
        return pl.ds(pl.multiple_of(n * KC, KC), KC)

    def packs(n):
        return pl.ds(pl.multiple_of(n * PC, PC), PC)

    @pl.loop(nk, BLOCKS)
    def _(n):
        g_ref[packs(n), :] = jnp.zeros((PC, 384), BF)

    i, j = iotas((E, 128))
    heads = ones_where((i == j + HALF * yl) & (j < HALF))
    wq = dot(weights[0:192, :], heads).astype(BF)
    wk = dot(weights[192:384, :], heads).astype(BF)
    wv = dot(weights[384:576, :], heads).astype(BF)
    wo = t_dot(weights[576:768, :], heads).astype(BF)
    for a, b, w in ((wkva, wkvb, jnp.concatenate([wk, wv], 1)), (wqa, wqb, wq), (wga, wgb, wo)):
        a[0:192, :] = w
        a[192:256, :] = jnp.zeros((64, w.shape[1]), BF)
        b[64:256, :] = w
        b[0:64, :] = jnp.zeros((64, w.shape[1]), BF)
    left, right = shifted((E, 2 * E), 0), shifted((E, 2 * E), E)
    for n, w in enumerate((wk, wv, wq)):
        ua[128 * n:128 * n + 128, :] = t_dot(w, left).astype(BF)
        ub[128 * n:128 * n + 128, :] = t_dot(w, right).astype(BF)

    lane = lax.broadcasted_iota(jnp.int32, (PC, 128), 1)
    sub = lax.broadcasted_iota(jnp.int32, (PC, 128), 0)
    real = sub + 96 * ((sub >= 96).astype(jnp.int32) + (sub >= 192).astype(jnp.int32) + (sub >= 288).astype(jnp.int32))
    v_extra = jnp.where((lane >= HALF) & (lane < HALF + 3), 1.0, 0.0)

    @pl.loop(0, nk)
    def _(n):
        p = pk_ref[packs(n), :]
        for h, (part, w) in enumerate(((p[:, 0:256], wkva), (p[:, 128:384], wkvb))):
            kv = dot(part, w[...])
            bias = jnp.where((lane == HALF) & (real + (n * KC + HALF * h) >= train), BIAS, 0.0)
            r = pl.ds(pl.multiple_of(n * KC + PC * h, PC), PC)
            kv_ref[r, 0:128] = (kv[:, 0:128] + bias).astype(BF)
            kv_ref[r, 128:256] = (kv[:, 128:256] + v_extra).astype(BF)

    block = z * 2 + c
    po = pk_ref[packs(block), :]
    go = gp_ref[...]
    for src, a, b, out in ((po, wqa, wqb, qT_ref), (go, wga, wgb, gT_ref)):
        out[:, 0:PC] = dot(src[:, 0:256], a[...]).astype(BF).T
        out[:, PC:NQ] = dot(src[:, 128:384], b[...]).astype(BF).T
    attT_ref[...] = jnp.zeros_like(attT_ref)
    dqT_ref[...] = jnp.zeros_like(dqT_ref)
    wacc_ref[...] = jnp.zeros_like(wacc_ref)
    i16 = lax.broadcasted_iota(jnp.int32, (16, NQ), 0)
    lanes = [slice(NQ * h, NQ * h + NQ) for h in range(3)]
    subs = [slice(32 * h, 32 * h + 32) for h in range(3)]

    qmT_ref[...] = jnp.zeros_like(qmT_ref)
    gmT_ref[...] = jnp.zeros_like(gmT_ref)
    for q, hs in zip(lanes, subs):
        qmT_ref[hs, q] = qT_ref[hs, :]
        qm_ref[q, :] = qmT_ref[:, q].T
        qmT_ref[96:112, q] = jnp.where(i16 == 0, 1.0, 0.0).astype(BF)
    acc_ref[...] = jnp.zeros_like(acc_ref)
    m_ref[...] = jnp.full_like(m_ref, BIAS)

    def piece(n, t):
        return pl.ds(pl.multiple_of(n * KC + (t // 3) * PC, PC), PC), lanes[t % 3]

    def score(n, t):
        r, q = piece(n, t)
        s = dot(kv_ref[r, 0:128], qmT_ref[:, q])
        s_ref[t % 2] = s
        m_ref[2 + t % 2:3 + t % 2, q] = jnp.max(s, axis=0, keepdims=True)

    def weigh(n, t):
        r, q = piece(n, t)
        old = m_ref[0:1, q]
        new = jnp.maximum(old, jnp.ceil(m_ref[2 + t % 2:3 + t % 2, q] * SCALE_LOG2E))
        e = jnp.exp2(s_ref[t % 2] * SCALE_LOG2E - new).astype(BF)
        e_ref[r, q] = e
        m_ref[0:1, q] = new
        mb_ref[n, t // 3:t // 3 + 1, q] = new
        vT = kv_ref[r, 128:256].T
        vt = jnp.concatenate([vT[subs[t % 3]], vT[96:112]], 0)
        acc_ref[:, q] = acc_ref[:, q] * jnp.exp2(old - new) + dot(vt, e)

    score(0, 0)

    @pl.loop(0, nk)
    def _(n):
        for t in range(6):
            if t < 5:
                score(n, t + 1)
            else:
                score(jnp.minimum(n + 1, nk - 1), 0)
            weigh(n, t)

    for q, hs in zip(lanes, subs):
        inv = 1.0 / acc_ref[32:33, q]
        att = (acc_ref[0:32, q] * inv).astype(BF)
        attT_ref[hs, :] = att
        gp = (gT_ref[hs, :].astype(F32) * inv).astype(BF)
        delta = -jnp.sum(gp.astype(F32) * att.astype(F32), axis=0, keepdims=True)
        d0 = delta.astype(BF).astype(F32)
        d1 = (delta - d0).astype(BF).astype(F32)
        d2 = delta - d0 - d1
        gmT_ref[hs, q] = gp
        gm_ref[q, :] = gmT_ref[:, q].T
        gmT_ref[96:112, q] = jnp.where(i16 == 0, d0, jnp.where(i16 == 1, d1, jnp.where(i16 == 2, d2, 0.0))).astype(BF)
    acc_ref[...] = jnp.zeros_like(acc_ref)

    @pl.loop(0, nk)
    def _(n):
        r = rows(n)
        v = kv_ref[r, 128:256]
        kT, pT = kv_ref[r, 0:128].T, pk_ref[packs(n), :].T
        dk, dv = jnp.zeros((KC, 128), F32), jnp.zeros((KC, 128), F32)
        for h in range(3):
            q = lanes[h]
            ga = dot(v, gmT_ref[:, q]).astype(BF)
            by = [jnp.exp2(mb_ref[n, t:t + 1, q] - m_ref[0:1, q]).astype(BF) for t in range(2)]
            e = e_ref[r, q]
            es = jnp.concatenate([e[0:PC] * by[0], e[PC:KC] * by[1]], 0)
            ds = es * ga
            dv = dv + dot(es, gm_ref[q, :])
            dk = dk + dot(ds, qm_ref[q, :])
            acc_ref[0:32, q] += dot(kT[subs[h]], ds)
        dkv_ref[:, 0:128] = (dk * SCALE).astype(BF)
        dkv_ref[:, 128:256] = dv.astype(BF)
        da, db = dkv_ref[0:PC, :], dkv_ref[PC:KC, :]
        g_ref[packs(n), :] = (dot(da, ua[0:256, :]) + dot(db, ub[0:256, :])).astype(BF)
        wacc_ref[...] += dot(pT[0:E], da) + dot(pT[E:2 * E], db)

    for q, hs in zip(lanes, subs):
        dqT_ref[hs, :] = (acc_ref[0:32, q] * SCALE).astype(BF)

    dq, at = dqT_ref[...].T, attT_ref[...].T
    gq_ref[...] = dot(dq[0:PC], ua[256:384, :]) + dot(dq[PC:NQ], ub[256:384, :])
    poT, goT = po.T, go.T
    w_q = dot(poT[0:E], dq[0:PC]) + dot(poT[E:2 * E], dq[PC:NQ])
    w_o = dot(goT[0:E], at[0:PC]) + dot(goT[E:2 * E], at[PC:NQ])
    w_ref[...] = (
        dot(w_q.astype(BF), shifted((128, 384), 0, HALF))
        + dot(w_o.astype(BF), shifted((128, 384), HALF, HALF))
        + dot(wacc_ref[:, 0:128].astype(BF), shifted((128, 384), 2 * HALF, HALF))
        + dot(wacc_ref[:, 128:256].astype(BF), shifted((128, 384), 3 * HALF, HALF))
    ).astype(BF)


def reduce_kernel(g_ref, gq_ref, w_ref, ret_ref, wf_ref,
                  tw, part, hp, hn, fp, fn, fin, rs, p2,
                  ts, tr, hs_, hr, fs, fr, ks, kr, as_, ar, bs, br, cs, cr):
    z, x, yl, yh, c = place()
    mine = x // 2 == c
    own = jnp.where(mine, 1, 0)
    zp, zo, zn = (z + 1) % 4, (z + 2) % 4, (z + 3) % 4
    up, down, twin = device(zp, x, yl, yh, c), device(zn, x, yl, yh, c), device(z, x, yl, yh, 1 - c)
    slot = (x % 2) * 2 + yl
    i16 = z * 4 + x
    i8 = (yh * 2 + yl) * 2 + c
    owner = i16 < SLABS
    owns = jnp.where(owner, 1, 0)

    def dev16(n):
        return device(n // 4, n % 4, yl, yh, c)

    def dev8(n):
        return device(z, x, (n // 2) % 2, n // 4, n % 2)

    barrier = pltpu.get_barrier_semaphore()

    def greet(to):
        pl.semaphore_signal(barrier, inc=1, device_id=to, device_id_type=MESH)

    for to in (twin, up, down):
        greet(to)
    for j in range(4):
        @pl.when(jnp.logical_not(jnp.logical_and(mine, slot == j)))
        def _():
            greet(device(z, 2 * c + j // 2, j % 2, yh, x // 2))

    @pl.loop(1, 16)
    def _(n):
        greet(dev16((i16 + n) % 16))

    @pl.loop(1, 8)
    def _(n):
        greet(dev8((i8 + n) % 8))

    pl.semaphore_wait(barrier, 3 + 4 - own + 15 + 7)

    sent = []

    def go(copy):
        copy.start()
        sent.append(copy)

    def block(zz, cc):
        return pl.ds(pl.multiple_of((zz * 2 + cc) * PC, PC), PC)

    for n, zz in enumerate((zo, zp, zn, z)):
        go(rcopy(g_ref.at[block(zz, 1 - c), :], tw.at[n], ts.at[n], tr.at[n], twin))

    def slab(n):
        return pl.ds(pl.multiple_of(n * 16, 16), 16)

    def one(n):
        to = (i16 + n) % 16
        return to < SLABS, rcopy(w_ref.at[slab(jnp.minimum(to, SLABS - 1)), :], rs.at[i16], as_.at[n], ar.at[i16], dev16(to))

    def two(n):
        return rcopy(p2.at[i8], p2.at[i8], bs.at[n], br.at[i8], dev8((i8 + n) % 8))

    def three(n):
        mine_ = slab(jnp.minimum(i16, SLABS - 1))
        return rcopy(wf_ref.at[:, mine_, :], wf_ref.at[:, mine_, :], cs.at[n], cr.at[i16], dev16((i16 + n) % 16))

    @pl.loop(1, 16)
    def _(n):
        ok, copy = one(n)

        @pl.when(ok)
        def _():
            copy.start()

    def with_twin(n, zz):
        wait_for(tw.at[n], tr.at[n])
        return g_ref[block(zz, c), :].astype(F32) + tw[n].astype(F32)

    lo, hi = pl.ds(0, 192), pl.ds(192, 192)
    part[0] = with_twin(0, zo).astype(BF)
    go(rcopy(part.at[0, lo, :], hp, hs_.at[0], hr.at[0], up))
    go(rcopy(part.at[0, hi, :], hn, hs_.at[1], hr.at[1], down))
    part[1] = with_twin(1, zp).astype(BF)
    go(rcopy(part.at[1, hi, :], fp.at[hi, :], fs.at[0], fr.at[0], up))
    part[2] = with_twin(2, zn).astype(BF)
    go(rcopy(part.at[2, lo, :], fn.at[lo, :], fs.at[1], fr.at[1], down))

    @pl.when(owner)
    def _():
        rs[i16] = w_ref[slab(jnp.minimum(i16, SLABS - 1)), :]

        @pl.loop(1, 16)
        def _(n):
            m = (i16 + n) % 16
            wait_for(rs.at[m], ar.at[m])

        acc = rs[0].astype(F32)
        for n in range(1, 16):
            acc = acc + rs[n].astype(F32)
        p2[i8] = acc.astype(BF)

        @pl.loop(1, 8)
        def _(n):
            two(n).start()

    wait_for(hp, hr.at[0])
    part[1, 0:192, :] = (part[1, 0:192, :].astype(F32) + hp[...].astype(F32)).astype(BF)
    go(rcopy(part.at[1, lo, :], fp.at[lo, :], fs.at[2], fr.at[2], up))
    wait_for(hn, hr.at[1])
    part[2, 192:384, :] = (part[2, 192:384, :].astype(F32) + hn[...].astype(F32)).astype(BF)
    go(rcopy(part.at[2, hi, :], fn.at[hi, :], fs.at[3], fr.at[3], down))

    @pl.when(owner)
    def _():
        @pl.loop(1, 8)
        def _(n):
            m = (i8 + n) % 8
            wait_for(p2.at[m], br.at[m])

        for half in range(2):
            n = 2 * half
            acc = p2[n].astype(F32) + p2[n + 1].astype(F32) + p2[n + 4].astype(F32) + p2[n + 5].astype(F32)
            wf_ref[half, slab(jnp.minimum(i16, SLABS - 1)), :] = acc.astype(BF)

        @pl.loop(1, 16)
        def _(n):
            three(n).start()

    total = with_twin(3, z) + gq_ref[...]
    wait_for(fp.at[hi, :], fr.at[0])
    wait_for(fn.at[lo, :], fr.at[1])
    wait_for(fp.at[lo, :], fr.at[2])
    wait_for(fn.at[hi, :], fr.at[3])
    fin[...] = (total + fp[...].astype(F32) + fn[...].astype(F32)).astype(BF)

    def back(s):
        to = device(z, 2 * c + s // 2, s % 2, yh, x // 2)
        return rcopy(fin.at[pl.ds(s * HALF, HALF), :], ret_ref.at[slot], ks.at[s], kr.at[slot], to)

    for s in range(4):
        keep = jnp.logical_and(mine, slot == s)

        @pl.when(keep)
        def _():
            pltpu.make_async_copy(fin.at[pl.ds(s * HALF, HALF), :], ret_ref.at[slot], kr.at[slot]).start()

        @pl.when(jnp.logical_not(keep))
        def _():
            back(s).start()

    for n in range(4):
        wait_for(ret_ref.at[n], kr.at[n])

    @pl.loop(1, 16)
    def _(n):
        m = (i16 + n) % 16

        @pl.when(m < SLABS)
        def _():
            r = slab(jnp.minimum(m, SLABS - 1))
            wait_for(wf_ref.at[:, r, :], cr.at[m])

    for copy in sent:
        copy.wait_send()
    for s in range(4):
        @pl.when(jnp.logical_not(jnp.logical_and(mine, slot == s)))
        def _():
            back(s).wait_send()

    @pl.loop(1, 16)
    def _(n):
        ok, copy = one(n)

        @pl.when(ok)
        def _():
            copy.wait_send()

        @pl.when(owner)
        def _():
            three(n).wait_send()

    @pl.when(owner)
    def _():
        @pl.loop(1, 8)
        def _(n):
            two(n).wait_send()


def final_kernel(ret_ref, wf_ref, grad_ref, gc_ref, gwq_ref, gwk_ref, gwv_ref, gwo_ref):
    sort = by_feature()
    i, j = iotas((256, E))
    right = ones_where(i == j + 64)
    total = grad_ref[...].reshape(2 * ROWS, E).astype(F32)
    for half in range(2):
        parts = []
        for f in range(2):
            r = ret_ref[2 * f + half]
            parts += [r[:, 0:E], dot(r[:, 128:384], right).astype(BF)]
        total = total + t_dot(sort, jnp.concatenate(parts, 0))
    gc_ref[...] = total.astype(BF).reshape(ROWS, 2, E)

    i, j = iotas((384, E))

    def weight(first):
        low = ones_where((i == j + first) & (j < HALF))
        high = ones_where((i == j - HALF + first) & (j >= HALF))
        return dot(wf_ref[0], low) + dot(wf_ref[1], high)

    gwq_ref[...] = weight(0)
    gwo_ref[...] = weight(HALF).T
    gwk_ref[...] = weight(2 * HALF)
    gwv_ref[...] = weight(3 * HALF)


SLABS = 12
VM = pl.BlockSpec(memory_space=pltpu.VMEM)
DMA = pltpu.SemaphoreType.DMA


def sds(shape, dtype=BF):
    return jax.ShapeDtypeStruct(shape, dtype)


def share(*args):
    return pl.pallas_call(
        share_kernel,
        out_shape=[sds((NR // 2, 384)), sds((PC, 384)), sds((8, 128), F32)],
        in_specs=[VM],
        out_specs=[VM] * 3,
        scratch_shapes=[
            pltpu.VMEM((2, HALF, 384), BF), pltpu.VMEM((2, HALF, 384), BF),
            pltpu.VMEM((8, 8, 128), F32), pltpu.VMEM((4, 8, 128), F32),
            DMA((4,)), DMA((4,)), DMA((4,)), DMA((4,)), DMA((8,)), DMA((8,)), DMA((4,)), DMA((4,)), DMA((16,)), DMA((16,)),
            DMA((8,)), DMA((8,)), DMA((4,)), DMA((4,)),
        ],
        compiler_params=pltpu.CompilerParams(collective_id=1, has_side_effects=True, vmem_limit_bytes=24 * 2**20),
        cost_estimate=pl.CostEstimate(flops=10**8, bytes_accessed=60 * 10**6, transcendentals=0),
        name="share",
    )(*args)


def attention(*args):
    return pl.pallas_call(
        attention_kernel,
        out_shape=[sds((NR // 2, 384)), sds((PC, 384), F32), sds((E, 384))],
        in_specs=[VM] * 4,
        out_specs=[VM] * 3,
        scratch_shapes=[
            pltpu.VMEM((NR, 3 * NQ), BF), pltpu.VMEM((BLOCKS, 8, 3 * NQ), F32), pltpu.VMEM((NR, 256), BF),
            pltpu.VMEM((128, NQ), BF), pltpu.VMEM((128, NQ), BF),
            pltpu.VMEM((3 * NQ, 128), BF), pltpu.VMEM((3 * NQ, 128), BF),
            pltpu.VMEM((128, 3 * NQ), BF), pltpu.VMEM((128, 3 * NQ), BF),
            pltpu.VMEM((48, 3 * NQ), F32), pltpu.VMEM((8, 3 * NQ), F32),
            pltpu.VMEM((2, PC, NQ), F32), pltpu.VMEM((KC, 256), BF),
            pltpu.VMEM((128, NQ), BF), pltpu.VMEM((128, NQ), BF), pltpu.VMEM((E, 256), F32),
            pltpu.VMEM((256, 256), BF), pltpu.VMEM((256, 256), BF), pltpu.VMEM((256, 128), BF), pltpu.VMEM((256, 128), BF),
            pltpu.VMEM((256, 128), BF), pltpu.VMEM((256, 128), BF), pltpu.VMEM((384, 384), BF), pltpu.VMEM((384, 384), BF),
        ],
        compiler_params=pltpu.CompilerParams(vmem_limit_bytes=VLIM * 2**20),
        cost_estimate=pl.CostEstimate(flops=3 * 10**10, bytes_accessed=10**7, transcendentals=14 * 10**6),
        name="attention",
    )(*args)


VLIM = 48


def reduce(*args):
    return pl.pallas_call(
        reduce_kernel,
        out_shape=[sds((4, HALF, 384)), sds((2, E, 384))],
        in_specs=[VM] * 3,
        out_specs=[VM] * 2,
        scratch_shapes=[
            pltpu.VMEM((4, PC, 384), BF), pltpu.VMEM((3, PC, 384), BF),
            pltpu.VMEM((192, 384), BF), pltpu.VMEM((192, 384), BF),
            pltpu.VMEM((PC, 384), BF), pltpu.VMEM((PC, 384), BF), pltpu.VMEM((PC, 384), BF),
            pltpu.VMEM((16, 16, 384), BF), pltpu.VMEM((8, 16, 384), BF),
            DMA((4,)), DMA((4,)), DMA((2,)), DMA((2,)), DMA((4,)), DMA((4,)), DMA((4,)), DMA((4,)),
            DMA((16,)), DMA((16,)), DMA((8,)), DMA((8,)), DMA((16,)), DMA((16,)),
        ],
        compiler_params=pltpu.CompilerParams(collective_id=2, has_side_effects=True, vmem_limit_bytes=24 * 2**20),
        cost_estimate=pl.CostEstimate(flops=10**8, bytes_accessed=60 * 10**6, transcendentals=0),
        name="reduce",
    )(*args)


def final(*args):
    w = sds((E, E), F32)
    return pl.pallas_call(
        final_kernel,
        out_shape=[sds((ROWS, 2, E)), w, w, w, w],
        in_specs=[VM] * 3,
        out_specs=[VM] * 5,
        compiler_params=pltpu.CompilerParams(vmem_limit_bytes=24 * 2**20),
        name="final",
    )(*args)


def body(cells, w_query, w_key, w_value, w_out, train_flag, grad_out):
    flags = jnp.broadcast_to(train_flag.astype(BF), (1, 2, ROWS))
    packs, grads, count = share(jnp.concatenate([cells, grad_out, flags], 0))
    g, gq, w = attention(packs, grads, count, jnp.concatenate([w_query, w_key, w_value, w_out], 0))
    ret, wf = reduce(g, gq, w)
    return final(ret, wf, grad_out)


def solution(mesh):
    return jax.shard_map(
        body,
        mesh=mesh,
        in_specs=(P("row", "feat", None), P(), P(), P(), P(), P("row"), P("row", "feat", None)),
        out_specs=(P("row", "feat", None), P(), P(), P(), P()),
        check_vma=False,
    )
```

```python
import jax
import jax.numpy as jnp
from jax import lax
from jax.experimental import pallas as pl
from jax.experimental.pallas import tpu as pltpu
from jax.sharding import PartitionSpec as P


HD = 32
SCALE = float(HD) ** -0.5
SCALE_LOG2E = SCALE * 1.4426950408889634
BIAS = -1e30
F32 = jnp.float32
BF = jnp.bfloat16
MESH = pl.DeviceIdType.MESH

E = 192
HALF = 96
ROWS = 192
NQ = 768
NR = 6144
KC = 768
PC = 384
BLOCKS = 8


def dot(a, b):
    return jnp.dot(a, b, preferred_element_type=F32)


def t_dot(a, b):
    return lax.dot_general(a, b, (((0,), (0,)), ((), ())), preferred_element_type=F32)


def place():
    row = lax.axis_index("row")
    feat = lax.axis_index("feat")
    return row // 8, (row // 2) % 4, row % 2, feat // 2, feat % 2


def device(z, x, yl, yh, c):
    return ((z * 4 + x) * 2 + yl, yh * 2 + c)


def iotas(shape):
    return lax.broadcasted_iota(jnp.int32, shape, 0), lax.broadcasted_iota(jnp.int32, shape, 1)


def ones_where(mask):
    return mask.astype(F32).astype(BF)


def shifted(shape, by, most=None):
    i, j = iotas(shape)
    mask = j == i + by
    if most is not None:
        mask = mask & (i < most)
    return ones_where(mask)


def by_feature():
    i, j = iotas((2 * ROWS, 2 * ROWS))
    second = i >= ROWS
    return ones_where(j == jnp.where(second, 2 * (i - ROWS) + 1, 2 * i))


def rcopy(src, dst, send, recv, to):
    return pltpu.make_async_remote_copy(
        src_ref=src, dst_ref=dst, send_sem=send, recv_sem=recv, device_id=to, device_id_type=MESH
    )


def wait_for(ref, sem):
    pltpu.make_async_copy(ref, ref, sem).wait()


def share_kernel(in_ref, pk_ref, gp_ref, cnt_ref, cs, gs, cf, cb, four, zb, s1, r1, s2, r2, zs, zr, fs, fr, ts, tr, ns, nr, ms, mr):
    z, x, yl, yh, c = place()
    mine = x // 2 == c
    own = jnp.where(mine, 1, 0)
    zp, zo, zn = (z + 1) % 4, (z + 2) % 4, (z + 3) % 4
    up, down, twin = device(zp, x, yl, yh, c), device(zn, x, yl, yh, c), device(z, x, yl, yh, 1 - c)
    far = device(zo, x, yl, yh, c)
    slot = (x % 2) * 2 + yl

    barrier = pltpu.get_barrier_semaphore()

    def greet(to):
        pl.semaphore_signal(barrier, inc=1, device_id=to, device_id_type=MESH)

    for s in range(4):
        @pl.when(jnp.logical_not(jnp.logical_and(mine, slot == s)))
        def _():
            greet(device(z, 2 * c + s // 2, s % 2, yh, x // 2))
    for to in (up, down, twin):
        greet(to)
    greet(far)

    sort = by_feature()
    left, right = shifted((ROWS, 2 * E), 0), shifted((ROWS, 2 * E), E)

    def pack(first, out):
        rows = dot(sort, in_ref[first:first + ROWS].reshape(2 * ROWS, E)).astype(BF)
        for f in range(2):
            r = f * ROWS
            out[f] = (dot(rows[r:r + HALF], left) + dot(rows[r + HALF:r + ROWS], right)).astype(BF)

    flags = jnp.sum(in_ref[2 * ROWS, 0:1, :].astype(F32), axis=1, keepdims=True)
    cf[...] = jnp.broadcast_to(flags, (8, 128))
    pack(0, cs)
    pl.semaphore_wait(barrier, 4 - own + 4)

    my_rows = pl.ds(pl.multiple_of(((z * 4 + x) * 2 + yl) * HALF, HALF), HALF)
    my_slot = pl.ds(pl.multiple_of(slot * HALF, HALF), HALF)

    def first(j):
        to = device(z, 2 * c + j // 2, j % 2, yh, x // 2)
        a = rcopy(cs.at[j // 2], pk_ref.at[my_rows, :], s1.at[j], r1.at[slot], to)
        b = rcopy(gs.at[j // 2], gp_ref.at[my_slot, :], s2.at[j], r2.at[slot], to)
        return a, b

    for j in range(4):
        keep = jnp.logical_and(mine, slot == j)

        @pl.when(keep)
        def _():
            pltpu.make_async_copy(cs.at[j // 2], pk_ref.at[my_rows, :], r1.at[slot]).start()

        @pl.when(jnp.logical_not(keep))
        def _():
            first(j)[0].start()

    def count(j):
        return rcopy(cf, cb.at[slot], ns.at[j], nr.at[slot], device(z, 2 * c + j // 2, j % 2, yh, x // 2))

    for j in range(4):
        keep = jnp.logical_and(mine, slot == j)

        @pl.when(keep)
        def _():
            pltpu.make_async_copy(cf, cb.at[slot], nr.at[slot]).start()

        @pl.when(jnp.logical_not(keep))
        def _():
            count(j).start()

    def rows_of(zz, cc, s):
        return pl.ds(pl.multiple_of((zz * 2 + cc) * PC + s * HALF, HALF), HALF)

    def move(zz, s, send, recv, to):
        r = rows_of(zz, c, s)
        return rcopy(pk_ref.at[r, :], pk_ref.at[r, :], send, recv, to)

    def landed(zz, cc, s, recv):
        wait_for(pk_ref.at[rows_of(zz, cc, s), :], recv)

    sent = []

    def go(copy):
        copy.start()
        sent.append(copy)

    for s in range(4):
        landed(z, c, s, r1.at[s])
        go(move(z, s, zs.at[s], zr.at[s], up))
        go(move(z, s, zs.at[4 + s], zr.at[4 + s], down))
        go(move(z, s, ts.at[s], tr.at[s], twin))

    for s in range(4):
        wait_for(cb.at[s], nr.at[s])
    four[0] = cb[0] + cb[1] + cb[2] + cb[3]
    go(rcopy(four.at[0], four.at[1], ms.at[0], mr.at[0], twin))
    pack(ROWS, gs)
    for j in range(4):
        keep = jnp.logical_and(mine, slot == j)

        @pl.when(keep)
        def _():
            pltpu.make_async_copy(gs.at[j // 2], gp_ref.at[my_slot, :], r2.at[slot]).start()

        @pl.when(jnp.logical_not(keep))
        def _():
            first(j)[1].start()

    wait_for(four.at[1], mr.at[0])
    zb[0] = four[0] + four[1]
    for n, to in ((1, up), (2, far), (3, down)):
        go(rcopy(zb.at[0], zb.at[n], ms.at[n], mr.at[n], to))

    for i in range(4):
        s = i
        landed(zn, c, s, zr.at[s])
        if s < 2:
            go(move(zn, s, fs.at[s], fr.at[s], up))
        go(move(zn, s, ts.at[4 + s], tr.at[4 + s], twin))
        s = (i + 2) % 4
        landed(zp, c, s, zr.at[4 + s])
        if s >= 2:
            go(move(zp, s, fs.at[s], fr.at[s], down))
        go(move(zp, s, ts.at[8 + s], tr.at[8 + s], twin))

    for s in (0, 2, 1, 3):
        landed(zo, c, s, fr.at[s])
        go(move(zo, s, ts.at[12 + s], tr.at[12 + s], twin))

    for n in range(1, 4):
        wait_for(zb.at[n], mr.at[n])
    cnt_ref[...] = zb[0] + zb[1] + zb[2] + zb[3]

    for n, zz in ((0, z), (1, zn), (2, zp), (3, zo)):
        for s in range(4):
            landed(zz, 1 - c, s, tr.at[4 * n + s])
    for s in range(4):
        wait_for(gp_ref.at[pl.ds(s * HALF, HALF), :], r2.at[s])
    for copy in sent:
        copy.wait_send()
    for j in range(4):
        @pl.when(jnp.logical_not(jnp.logical_and(mine, slot == j)))
        def _():
            a, b = first(j)
            a.wait_send()
            b.wait_send()
            count(j).wait_send()


def attention_kernel(pk_ref, gp_ref, cnt_ref, weights, g_ref, gq_ref, w_ref, e_ref, mb_ref, kv_ref, qT_ref, gT_ref, qm_ref, gm_ref,
                     qmT_ref, gmT_ref, acc_ref, m_ref, s_ref, dkv_ref, attT_ref, dqT_ref, wacc_ref,
                     wkva, wkvb, wqa, wqb, wga, wgb, ua, ub):
    z, x, yl, yh, c = place()
    train = jnp.max(cnt_ref[...]).astype(jnp.int32)
    halves = lax.div(train + PC - 1, PC)
    full, odd = lax.div(halves, 2), lax.rem(halves, 2)
    last = lax.div(halves - 1, 2)

    def rows(n):
        return pl.ds(pl.multiple_of(n * KC, KC), KC)

    def packs(n):
        return pl.ds(pl.multiple_of(n * PC, PC), PC)

    def half_packs(n):
        return pl.ds(pl.multiple_of(n * ROWS, ROWS), ROWS)

    @pl.loop(halves, 2 * BLOCKS)
    def _(n):
        g_ref[half_packs(n), :] = jnp.zeros((ROWS, 384), BF)

    i, j = iotas((E, 128))
    heads = ones_where((i == j + HALF * yl) & (j < HALF))
    wq = dot(weights[0:192, :], heads).astype(BF)
    wk = dot(weights[192:384, :], heads).astype(BF)
    wv = dot(weights[384:576, :], heads).astype(BF)
    wo = t_dot(weights[576:768, :], heads).astype(BF)
    for a, b, w in ((wkva, wkvb, jnp.concatenate([wk, wv], 1)), (wqa, wqb, wq), (wga, wgb, wo)):
        a[0:192, :] = w
        a[192:256, :] = jnp.zeros((64, w.shape[1]), BF)
        b[64:256, :] = w
        b[0:64, :] = jnp.zeros((64, w.shape[1]), BF)
    left, right = shifted((E, 2 * E), 0), shifted((E, 2 * E), E)
    for n, w in enumerate((wk, wv, wq)):
        ua[128 * n:128 * n + 128, :] = t_dot(w, left).astype(BF)
        ub[128 * n:128 * n + 128, :] = t_dot(w, right).astype(BF)

    lane = lax.broadcasted_iota(jnp.int32, (ROWS, 128), 1)
    sub = lax.broadcasted_iota(jnp.int32, (ROWS, 128), 0)
    real = sub + HALF * (sub >= HALF).astype(jnp.int32)
    v_extra = jnp.where((lane >= HALF) & (lane < HALF + 3), 1.0, 0.0)

    def project(n):
        p = pk_ref[packs(n), :]
        for side, (cells, w) in enumerate(((p[:, 0:256], wkva), (p[:, 128:384], wkvb))):
            kv = dot(cells, w[...])
            for half in range(2):
                first = n * KC + PC * half
                bias = jnp.where((lane == HALF) & (real + (first + HALF * side) >= train), BIAS, 0.0)
                r = pl.ds(pl.multiple_of(first + ROWS * side, ROWS), ROWS)
                own = slice(ROWS * half, ROWS * half + ROWS)
                kv_ref[r, 0:128] = (kv[own, 0:128] + bias).astype(BF)
                kv_ref[r, 128:256] = (kv[own, 128:256] + v_extra).astype(BF)

    project(0)
    project(jnp.minimum(1, last))

    block = z * 2 + c
    po = pk_ref[packs(block), :]
    go = gp_ref[...]
    for src, a, b, out in ((po, wqa, wqb, qT_ref), (go, wga, wgb, gT_ref)):
        out[:, 0:PC] = dot(src[:, 0:256], a[...]).astype(BF).T
        out[:, PC:NQ] = dot(src[:, 128:384], b[...]).astype(BF).T
    attT_ref[...] = jnp.zeros_like(attT_ref)
    dqT_ref[...] = jnp.zeros_like(dqT_ref)
    wacc_ref[...] = jnp.zeros_like(wacc_ref)
    i16 = lax.broadcasted_iota(jnp.int32, (16, NQ), 0)
    lanes = [slice(NQ * h, NQ * h + NQ) for h in range(3)]
    subs = [slice(32 * h, 32 * h + 32) for h in range(3)]

    qmT_ref[...] = jnp.zeros_like(qmT_ref)
    gmT_ref[...] = jnp.zeros_like(gmT_ref)
    for q, hs in zip(lanes, subs):
        qmT_ref[hs, q] = qT_ref[hs, :]
        qm_ref[q, :] = qmT_ref[:, q].T
        qmT_ref[96:112, q] = jnp.where(i16 == 0, 1.0, 0.0).astype(BF)
    acc_ref[...] = jnp.zeros_like(acc_ref)
    m_ref[...] = jnp.full_like(m_ref, BIAS)

    def piece(n, t):
        return pl.ds(pl.multiple_of(n * KC + (t // 3) * PC, PC), PC), lanes[t % 3]

    def score(n, t):
        r, q = piece(n, t)
        s = dot(kv_ref[r, 0:128], qmT_ref[:, q])
        s_ref[t % 2] = s
        m_ref[2 + t % 2:3 + t % 2, q] = jnp.max(s, axis=0, keepdims=True)

    def weigh(n, t):
        r, q = piece(n, t)
        old = m_ref[0:1, q]
        new = jnp.maximum(old, jnp.ceil(m_ref[2 + t % 2:3 + t % 2, q] * SCALE_LOG2E))
        e = jnp.exp2(s_ref[t % 2] * SCALE_LOG2E - new).astype(BF)
        e_ref[r, q] = e
        m_ref[0:1, q] = new
        mb_ref[n, t // 3:t // 3 + 1, q] = new
        vT = kv_ref[r, 128:256].T
        vt = jnp.concatenate([vT[subs[t % 3]], vT[96:112]], 0)
        acc_ref[:, q] = acc_ref[:, q] * jnp.exp2(old - new) + dot(vt, e)

    score(0, 0)

    @pl.loop(0, full)
    def _(n):
        for t in range(6):
            if t < 5:
                score(n, t + 1)
            else:
                score(jnp.minimum(n + 1, last), 0)
            weigh(n, t)
        project(jnp.minimum(n + 2, last))

    @pl.when(odd == 1)
    def _():
        for t in range(3):
            if t < 2:
                score(full, t + 1)
            weigh(full, t)

    for q, hs in zip(lanes, subs):
        inv = 1.0 / acc_ref[32:33, q]
        att = (acc_ref[0:32, q] * inv).astype(BF)
        attT_ref[hs, :] = att
        gp = (gT_ref[hs, :].astype(F32) * inv).astype(BF)
        delta = -jnp.sum(gp.astype(F32) * att.astype(F32), axis=0, keepdims=True)
        d0 = delta.astype(BF).astype(F32)
        d1 = (delta - d0).astype(BF).astype(F32)
        d2 = delta - d0 - d1
        gmT_ref[hs, q] = gp
        gm_ref[q, :] = gmT_ref[:, q].T
        gmT_ref[96:112, q] = jnp.where(i16 == 0, d0, jnp.where(i16 == 1, d1, jnp.where(i16 == 2, d2, 0.0))).astype(BF)
    acc_ref[...] = jnp.zeros_like(acc_ref)

    def pass_two(n, many):
        size = many * PC
        r = pl.ds(pl.multiple_of(n * KC, KC), size)
        v = kv_ref[r, 128:256]
        kT = kv_ref[r, 0:128].T
        dk, dv = jnp.zeros((size, 128), F32), jnp.zeros((size, 128), F32)
        for h in range(3):
            q = lanes[h]
            ga = dot(v, gmT_ref[:, q]).astype(BF)
            e = e_ref[r, q]
            by = [jnp.exp2(mb_ref[n, t:t + 1, q] - m_ref[0:1, q]).astype(BF) for t in range(many)]
            es = jnp.concatenate([e[PC * t:PC * t + PC] * by[t] for t in range(many)], 0)
            ds = es * ga
            dv = dv + dot(es, gm_ref[q, :])
            dk = dk + dot(ds, qm_ref[q, :])
            acc_ref[0:32, q] += dot(kT[subs[h]], ds)
        dkv_ref[0:size, 0:128] = (dk * SCALE).astype(BF)
        dkv_ref[0:size, 128:256] = dv.astype(BF)
        for t in range(many):
            p = half_packs(2 * n + t)
            pT = pk_ref[p, :].T
            da, db = dkv_ref[PC * t:PC * t + ROWS, :], dkv_ref[PC * t + ROWS:PC * t + PC, :]
            g_ref[p, :] = (dot(da, ua[0:256, :]) + dot(db, ub[0:256, :])).astype(BF)
            wacc_ref[...] += dot(pT[0:E], da) + dot(pT[E:2 * E], db)

    @pl.loop(0, full)
    def _(n):
        pass_two(n, 2)

    @pl.when(odd == 1)
    def _():
        pass_two(full, 1)

    for q, hs in zip(lanes, subs):
        dqT_ref[hs, :] = (acc_ref[0:32, q] * SCALE).astype(BF)

    dq, at = dqT_ref[...].T, attT_ref[...].T
    gq_ref[...] = dot(dq[0:PC], ua[256:384, :]) + dot(dq[PC:NQ], ub[256:384, :])
    poT, goT = po.T, go.T
    w_q = dot(poT[0:E], dq[0:PC]) + dot(poT[E:2 * E], dq[PC:NQ])
    w_o = dot(goT[0:E], at[0:PC]) + dot(goT[E:2 * E], at[PC:NQ])
    w_ref[...] = (
        dot(w_q.astype(BF), shifted((128, 384), 0, HALF))
        + dot(w_o.astype(BF), shifted((128, 384), HALF, HALF))
        + dot(wacc_ref[:, 0:128].astype(BF), shifted((128, 384), 2 * HALF, HALF))
        + dot(wacc_ref[:, 128:256].astype(BF), shifted((128, 384), 3 * HALF, HALF))
    ).astype(BF)


def reduce_kernel(g_ref, gq_ref, w_ref, ret_ref, wf_ref,
                  tw, part, hp, hn, fp, fn, fin, rs, p2,
                  ts, tr, hs_, hr, fs, fr, ks, kr, as_, ar, bs, br, cs, cr):
    z, x, yl, yh, c = place()
    mine = x // 2 == c
    own = jnp.where(mine, 1, 0)
    zp, zo, zn = (z + 1) % 4, (z + 2) % 4, (z + 3) % 4
    up, down, twin = device(zp, x, yl, yh, c), device(zn, x, yl, yh, c), device(z, x, yl, yh, 1 - c)
    slot = (x % 2) * 2 + yl
    i16 = z * 4 + x
    i8 = (yh * 2 + yl) * 2 + c
    owner = i16 < SLABS
    owns = jnp.where(owner, 1, 0)

    barrier = pltpu.get_barrier_semaphore()

    def greet(to):
        pl.semaphore_signal(barrier, inc=1, device_id=to, device_id_type=MESH)

    for to in (twin, up, down):
        greet(to)
    for j in range(4):
        @pl.when(jnp.logical_not(jnp.logical_and(mine, slot == j)))
        def _():
            greet(device(z, 2 * c + j // 2, j % 2, yh, x // 2))

    zs_, xs_ = [z, zp, zo, zn], [x, (x + 1) % 4, (x + 2) % 4, (x + 3) % 4]
    around = [(zs_[n // 4], xs_[n % 4]) for n in range(16)]
    beside = [((yl + n // 2 % 2) % 2, (yh + n // 4) % 2, (c + n % 2) % 2) for n in range(8)]
    for n in range(1, 16):
        greet(device(*around[n], yl, yh, c))
    for n in range(1, 8):
        greet(device(z, x, *beside[n]))

    pl.semaphore_wait(barrier, 3 + 4 - own + 15 + 7)

    sent = []

    def go(copy):
        copy.start()
        sent.append(copy)

    def block(zz, cc):
        return pl.ds(pl.multiple_of((zz * 2 + cc) * PC, PC), PC)

    for n, zz in enumerate((zo, zp, zn, z)):
        go(rcopy(g_ref.at[block(zz, 1 - c), :], tw.at[n], ts.at[n], tr.at[n], twin))

    def slab(n):
        return pl.ds(pl.multiple_of(n * 16, 16), 16)

    def one(n):
        zz, xx = around[n]
        to = zz * 4 + xx
        ok = to < SLABS
        r = slab(jnp.minimum(to, SLABS - 1))
        return ok, rcopy(w_ref.at[r, :], rs.at[i16], as_.at[n], ar.at[i16], device(zz, xx, yl, yh, c))

    def two(n):
        return rcopy(p2.at[i8], p2.at[i8], bs.at[n], br.at[i8], device(z, x, *beside[n]))

    my_slab = slab(jnp.minimum(i16, SLABS - 1))

    def three(n):
        mine_ = wf_ref.at[:, my_slab, :]
        return rcopy(mine_, mine_, cs.at[n], cr.at[i16], device(*around[n], yl, yh, c))

    for n in range(1, 16):
        ok, copy = one(n)

        @pl.when(ok)
        def _():
            copy.start()

    def with_twin(n, zz):
        wait_for(tw.at[n], tr.at[n])
        return g_ref[block(zz, c), :].astype(F32) + tw[n].astype(F32)

    lo, hi = pl.ds(0, 192), pl.ds(192, 192)
    part[0] = with_twin(0, zo).astype(BF)
    go(rcopy(part.at[0, lo, :], hp, hs_.at[0], hr.at[0], up))
    go(rcopy(part.at[0, hi, :], hn, hs_.at[1], hr.at[1], down))
    part[1] = with_twin(1, zp).astype(BF)
    go(rcopy(part.at[1, hi, :], fp.at[hi, :], fs.at[0], fr.at[0], up))
    part[2] = with_twin(2, zn).astype(BF)
    go(rcopy(part.at[2, lo, :], fn.at[lo, :], fs.at[1], fr.at[1], down))

    @pl.when(owner)
    def _():
        rs[i16] = w_ref[slab(jnp.minimum(i16, SLABS - 1)), :]

        for n in range(1, 16):
            m = around[n][0] * 4 + around[n][1]
            wait_for(rs.at[m], ar.at[m])

        acc = rs[0].astype(F32)
        for n in range(1, 16):
            acc = acc + rs[n].astype(F32)
        p2[i8] = acc.astype(BF)

        for n in range(1, 8):
            two(n).start()

    wait_for(hp, hr.at[0])
    part[1, 0:192, :] = (part[1, 0:192, :].astype(F32) + hp[...].astype(F32)).astype(BF)
    go(rcopy(part.at[1, lo, :], fp.at[lo, :], fs.at[2], fr.at[2], up))
    wait_for(hn, hr.at[1])
    part[2, 192:384, :] = (part[2, 192:384, :].astype(F32) + hn[...].astype(F32)).astype(BF)
    go(rcopy(part.at[2, hi, :], fn.at[hi, :], fs.at[3], fr.at[3], down))

    @pl.when(owner)
    def _():
        for yl_, yh_, c_ in beside[1:]:
            m = (yh_ * 2 + yl_) * 2 + c_
            wait_for(p2.at[m], br.at[m])

        for half in range(2):
            n = 2 * half
            acc = p2[n].astype(F32) + p2[n + 1].astype(F32) + p2[n + 4].astype(F32) + p2[n + 5].astype(F32)
            wf_ref[half, slab(jnp.minimum(i16, SLABS - 1)), :] = acc.astype(BF)

        for n in range(1, 16):
            three(n).start()

    total = with_twin(3, z) + gq_ref[...]
    wait_for(fp.at[hi, :], fr.at[0])
    wait_for(fn.at[lo, :], fr.at[1])
    wait_for(fp.at[lo, :], fr.at[2])
    wait_for(fn.at[hi, :], fr.at[3])
    fin[...] = (total + fp[...].astype(F32) + fn[...].astype(F32)).astype(BF)

    def back(s):
        to = device(z, 2 * c + s // 2, s % 2, yh, x // 2)
        return rcopy(fin.at[pl.ds(s * HALF, HALF), :], ret_ref.at[slot], ks.at[s], kr.at[slot], to)

    for s in range(4):
        keep = jnp.logical_and(mine, slot == s)

        @pl.when(keep)
        def _():
            pltpu.make_async_copy(fin.at[pl.ds(s * HALF, HALF), :], ret_ref.at[slot], kr.at[slot]).start()

        @pl.when(jnp.logical_not(keep))
        def _():
            back(s).start()

    for n in range(4):
        wait_for(ret_ref.at[n], kr.at[n])

    for n in range(1, 16):
        m = around[n][0] * 4 + around[n][1]

        @pl.when(m < SLABS)
        def _():
            r = slab(jnp.minimum(m, SLABS - 1))
            wait_for(wf_ref.at[:, r, :], cr.at[m])

    for copy in sent:
        copy.wait_send()
    for s in range(4):
        @pl.when(jnp.logical_not(jnp.logical_and(mine, slot == s)))
        def _():
            back(s).wait_send()

    for n in range(1, 16):
        ok, copy = one(n)

        @pl.when(ok)
        def _():
            copy.wait_send()

    @pl.when(owner)
    def _():
        for n in range(1, 16):
            three(n).wait_send()
        for n in range(1, 8):
            two(n).wait_send()


def final_kernel(ret_ref, wf_ref, grad_ref, gc_ref, gwq_ref, gwk_ref, gwv_ref, gwo_ref):
    sort = by_feature()
    i, j = iotas((256, E))
    right = ones_where(i == j + 64)
    total = grad_ref[...].reshape(2 * ROWS, E).astype(F32)
    for half in range(2):
        parts = []
        for f in range(2):
            r = ret_ref[2 * f + half]
            parts += [r[:, 0:E], dot(r[:, 128:384], right).astype(BF)]
        total = total + t_dot(sort, jnp.concatenate(parts, 0))
    gc_ref[...] = total.astype(BF).reshape(ROWS, 2, E)

    i, j = iotas((384, E))

    def weight(first):
        low = ones_where((i == j + first) & (j < HALF))
        high = ones_where((i == j - HALF + first) & (j >= HALF))
        return dot(wf_ref[0], low) + dot(wf_ref[1], high)

    gwq_ref[...] = weight(0)
    gwo_ref[...] = weight(HALF).T
    gwk_ref[...] = weight(2 * HALF)
    gwv_ref[...] = weight(3 * HALF)


SLABS = 12
VM = pl.BlockSpec(memory_space=pltpu.VMEM)
DMA = pltpu.SemaphoreType.DMA


def sds(shape, dtype=BF):
    return jax.ShapeDtypeStruct(shape, dtype)


def share(*args):
    return pl.pallas_call(
        share_kernel,
        out_shape=[sds((NR // 2, 384)), sds((PC, 384)), sds((8, 128), F32)],
        in_specs=[VM],
        out_specs=[VM] * 3,
        scratch_shapes=[
            pltpu.VMEM((2, HALF, 384), BF), pltpu.VMEM((2, HALF, 384), BF),
            pltpu.VMEM((8, 128), F32), pltpu.VMEM((4, 8, 128), F32), pltpu.VMEM((2, 8, 128), F32), pltpu.VMEM((4, 8, 128), F32),
            DMA((4,)), DMA((4,)), DMA((4,)), DMA((4,)), DMA((8,)), DMA((8,)), DMA((4,)), DMA((4,)), DMA((16,)), DMA((16,)),
            DMA((4,)), DMA((4,)), DMA((4,)), DMA((4,)),
        ],
        compiler_params=pltpu.CompilerParams(collective_id=1, has_side_effects=True, vmem_limit_bytes=24 * 2**20),
        cost_estimate=pl.CostEstimate(flops=10**8, bytes_accessed=60 * 10**6, transcendentals=0),
        name="share",
    )(*args)


def attention(*args):
    return pl.pallas_call(
        attention_kernel,
        out_shape=[sds((NR // 2, 384)), sds((PC, 384), F32), sds((E, 384))],
        in_specs=[VM] * 4,
        out_specs=[VM] * 3,
        scratch_shapes=[
            pltpu.VMEM((NR, 3 * NQ), BF), pltpu.VMEM((BLOCKS, 8, 3 * NQ), F32), pltpu.VMEM((NR, 256), BF),
            pltpu.VMEM((128, NQ), BF), pltpu.VMEM((128, NQ), BF),
            pltpu.VMEM((3 * NQ, 128), BF), pltpu.VMEM((3 * NQ, 128), BF),
            pltpu.VMEM((128, 3 * NQ), BF), pltpu.VMEM((128, 3 * NQ), BF),
            pltpu.VMEM((48, 3 * NQ), F32), pltpu.VMEM((8, 3 * NQ), F32),
            pltpu.VMEM((2, PC, NQ), F32), pltpu.VMEM((KC, 256), BF),
            pltpu.VMEM((128, NQ), BF), pltpu.VMEM((128, NQ), BF), pltpu.VMEM((E, 256), F32),
            pltpu.VMEM((256, 256), BF), pltpu.VMEM((256, 256), BF), pltpu.VMEM((256, 128), BF), pltpu.VMEM((256, 128), BF),
            pltpu.VMEM((256, 128), BF), pltpu.VMEM((256, 128), BF), pltpu.VMEM((384, 384), BF), pltpu.VMEM((384, 384), BF),
        ],
        compiler_params=pltpu.CompilerParams(vmem_limit_bytes=VLIM * 2**20),
        cost_estimate=pl.CostEstimate(flops=3 * 10**10, bytes_accessed=10**7, transcendentals=14 * 10**6),
        name="attention",
    )(*args)


VLIM = 48


def reduce(*args):
    return pl.pallas_call(
        reduce_kernel,
        out_shape=[sds((4, HALF, 384)), sds((2, E, 384))],
        in_specs=[VM] * 3,
        out_specs=[VM] * 2,
        scratch_shapes=[
            pltpu.VMEM((4, PC, 384), BF), pltpu.VMEM((3, PC, 384), BF),
            pltpu.VMEM((192, 384), BF), pltpu.VMEM((192, 384), BF),
            pltpu.VMEM((PC, 384), BF), pltpu.VMEM((PC, 384), BF), pltpu.VMEM((PC, 384), BF),
            pltpu.VMEM((16, 16, 384), BF), pltpu.VMEM((8, 16, 384), BF),
            DMA((4,)), DMA((4,)), DMA((2,)), DMA((2,)), DMA((4,)), DMA((4,)), DMA((4,)), DMA((4,)),
            DMA((16,)), DMA((16,)), DMA((8,)), DMA((8,)), DMA((16,)), DMA((16,)),
        ],
        compiler_params=pltpu.CompilerParams(collective_id=2, has_side_effects=True, vmem_limit_bytes=24 * 2**20),
        cost_estimate=pl.CostEstimate(flops=10**8, bytes_accessed=60 * 10**6, transcendentals=0),
        name="reduce",
    )(*args)


def final(*args):
    w = sds((E, E), F32)
    return pl.pallas_call(
        final_kernel,
        out_shape=[sds((ROWS, 2, E)), w, w, w, w],
        in_specs=[VM] * 3,
        out_specs=[VM] * 5,
        compiler_params=pltpu.CompilerParams(vmem_limit_bytes=24 * 2**20),
        name="final",
    )(*args)


def body(cells, w_query, w_key, w_value, w_out, train_flag, grad_out):
    flags = jnp.broadcast_to(train_flag.astype(BF), (1, 2, ROWS))
    packs, grads, count = share(jnp.concatenate([cells, grad_out, flags], 0))
    g, gq, w = attention(packs, grads, count, jnp.concatenate([w_query, w_key, w_value, w_out], 0))
    ret, wf = reduce(g, gq, w)
    return final(ret, wf, grad_out)


def solution(mesh):
    return jax.shard_map(
        body,
        mesh=mesh,
        in_specs=(P("row", "feat", None), P(), P(), P(), P(), P("row"), P("row", "feat", None)),
        out_specs=(P("row", "feat", None), P(), P(), P(), P()),
        check_vma=False,
    )
```

```python
import jax
import jax.numpy as jnp
from jax import lax
from jax.experimental import pallas as pl
from jax.experimental.pallas import tpu as pltpu
from jax.sharding import PartitionSpec as P


HD = 32
SCALE = float(HD) ** -0.5
SCALE_LOG2E = SCALE * 1.4426950408889634
BIAS = -1e30
F32 = jnp.float32
BF = jnp.bfloat16
MESH = pl.DeviceIdType.MESH

E = 192
HALF = 96
ROWS = 192
NQ = 768
NR = 6144
KC = 768
PC = 384
BLOCKS = 8


def dot(a, b):
    return jnp.dot(a, b, preferred_element_type=F32)


def t_dot(a, b):
    return lax.dot_general(a, b, (((0,), (0,)), ((), ())), preferred_element_type=F32)


def place():
    row = lax.axis_index("row")
    feat = lax.axis_index("feat")
    return row // 8, (row // 2) % 4, row % 2, feat // 2, feat % 2


def device(z, x, yl, yh, c):
    return ((z * 4 + x) * 2 + yl, yh * 2 + c)


def iotas(shape):
    return lax.broadcasted_iota(jnp.int32, shape, 0), lax.broadcasted_iota(jnp.int32, shape, 1)


def ones_where(mask):
    return mask.astype(F32).astype(BF)


def shifted(shape, by, most=None):
    i, j = iotas(shape)
    mask = j == i + by
    if most is not None:
        mask = mask & (i < most)
    return ones_where(mask)


def by_feature():
    i, j = iotas((2 * ROWS, 2 * ROWS))
    second = i >= ROWS
    return ones_where(j == jnp.where(second, 2 * (i - ROWS) + 1, 2 * i))


def rcopy(src, dst, send, recv, to):
    return pltpu.make_async_remote_copy(
        src_ref=src, dst_ref=dst, send_sem=send, recv_sem=recv, device_id=to, device_id_type=MESH
    )


def wait_for(ref, sem):
    pltpu.make_async_copy(ref, ref, sem).wait()


def share_kernel(in_ref, weights, pk_ref, cnt_ref, wkv_ref, u_ref, qT_ref, gT_ref, poT_ref, goT_ref, gp_ref, wqg, cs, gs, cf, cb, four, zb, s1, r1, s2, r2, zs, zr, fs, fr, ts, tr, ns, nr, ms, mr):
    z, x, yl, yh, c = place()
    mine = x // 2 == c
    own = jnp.where(mine, 1, 0)
    zp, zo, zn = (z + 1) % 4, (z + 2) % 4, (z + 3) % 4
    up, down, twin = device(zp, x, yl, yh, c), device(zn, x, yl, yh, c), device(z, x, yl, yh, 1 - c)
    far = device(zo, x, yl, yh, c)
    slot = (x % 2) * 2 + yl

    barrier = pltpu.get_barrier_semaphore()

    def greet(to):
        pl.semaphore_signal(barrier, inc=1, device_id=to, device_id_type=MESH)

    for s in range(4):
        @pl.when(jnp.logical_not(jnp.logical_and(mine, slot == s)))
        def _():
            greet(device(z, 2 * c + s // 2, s % 2, yh, x // 2))
    for to in (up, down, twin):
        greet(to)
    greet(far)

    sort = by_feature()
    left, right = shifted((ROWS, 2 * E), 0), shifted((ROWS, 2 * E), E)

    def pack(first, out):
        rows = dot(sort, in_ref[first:first + ROWS].reshape(2 * ROWS, E)).astype(BF)
        for f in range(2):
            r = f * ROWS
            out[f] = (dot(rows[r:r + HALF], left) + dot(rows[r + HALF:r + ROWS], right)).astype(BF)

    flags = jnp.sum(in_ref[2 * ROWS, 0:1, :].astype(F32), axis=1, keepdims=True)
    cf[...] = jnp.broadcast_to(flags, (8, 128))
    pack(0, cs)
    pl.semaphore_wait(barrier, 4 - own + 4)

    my_rows = pl.ds(pl.multiple_of(((z * 4 + x) * 2 + yl) * HALF, HALF), HALF)
    my_slot = pl.ds(pl.multiple_of(slot * HALF, HALF), HALF)

    def first(j):
        to = device(z, 2 * c + j // 2, j % 2, yh, x // 2)
        a = rcopy(cs.at[j // 2], pk_ref.at[my_rows, :], s1.at[j], r1.at[slot], to)
        b = rcopy(gs.at[j // 2], gp_ref.at[my_slot, :], s2.at[j], r2.at[slot], to)
        return a, b

    for j in range(4):
        keep = jnp.logical_and(mine, slot == j)

        @pl.when(keep)
        def _():
            pltpu.make_async_copy(cs.at[j // 2], pk_ref.at[my_rows, :], r1.at[slot]).start()

        @pl.when(jnp.logical_not(keep))
        def _():
            first(j)[0].start()

    def count(j):
        return rcopy(cf, cb.at[slot], ns.at[j], nr.at[slot], device(z, 2 * c + j // 2, j % 2, yh, x // 2))

    for j in range(4):
        keep = jnp.logical_and(mine, slot == j)

        @pl.when(keep)
        def _():
            pltpu.make_async_copy(cf, cb.at[slot], nr.at[slot]).start()

        @pl.when(jnp.logical_not(keep))
        def _():
            count(j).start()

    def rows_of(zz, cc, s):
        return pl.ds(pl.multiple_of((zz * 2 + cc) * PC + s * HALF, HALF), HALF)

    def move(zz, s, send, recv, to):
        r = rows_of(zz, c, s)
        return rcopy(pk_ref.at[r, :], pk_ref.at[r, :], send, recv, to)

    def landed(zz, cc, s, recv):
        wait_for(pk_ref.at[rows_of(zz, cc, s), :], recv)

    sent = []

    def go(copy):
        copy.start()
        sent.append(copy)

    i, j = iotas((E, 128))
    heads = ones_where((i == j + HALF * yl) & (j < HALF))
    wq = dot(weights[0:192, :], heads).astype(BF)
    wk = dot(weights[192:384, :], heads).astype(BF)
    wv = dot(weights[384:576, :], heads).astype(BF)
    wo = t_dot(weights[576:768, :], heads).astype(BF)
    for out, w in ((wkv_ref, jnp.concatenate([wk, wv], 1)), (wqg.at[0], wq), (wqg.at[1], wo)):
        none = jnp.zeros((64, w.shape[1]), BF)
        out[0, 0:192, :] = w
        out[0, 192:256, :] = none
        out[1, 64:256, :] = w
        out[1, 0:64, :] = none
    for n, w in enumerate((wk, wv, wq)):
        u_ref[0, 128 * n:128 * n + 128, :] = t_dot(w, left).astype(BF)
        u_ref[1, 128 * n:128 * n + 128, :] = t_dot(w, right).astype(BF)

    def own_rows(src, w, out, turned):
        turned[...] = src.T
        out[:, 0:PC] = dot(src[:, 0:256], w[0]).astype(BF).T
        out[:, PC:NQ] = dot(src[:, 128:384], w[1]).astype(BF).T

    for s in range(4):
        landed(z, c, s, r1.at[s])
        go(move(z, s, zs.at[s], zr.at[s], up))
        go(move(z, s, zs.at[4 + s], zr.at[4 + s], down))
        go(move(z, s, ts.at[s], tr.at[s], twin))

    for s in range(4):
        wait_for(cb.at[s], nr.at[s])
    four[0] = cb[0] + cb[1] + cb[2] + cb[3]
    go(rcopy(four.at[0], four.at[1], ms.at[0], mr.at[0], twin))
    pack(ROWS, gs)
    for j in range(4):
        keep = jnp.logical_and(mine, slot == j)

        @pl.when(keep)
        def _():
            pltpu.make_async_copy(gs.at[j // 2], gp_ref.at[my_slot, :], r2.at[slot]).start()

        @pl.when(jnp.logical_not(keep))
        def _():
            first(j)[1].start()

    own_rows(pk_ref[pl.ds(pl.multiple_of((z * 2 + c) * PC, PC), PC), :], wqg.at[0], qT_ref, poT_ref)
    wait_for(four.at[1], mr.at[0])
    zb[0] = four[0] + four[1]
    for n, to in ((1, up), (2, far), (3, down)):
        go(rcopy(zb.at[0], zb.at[n], ms.at[n], mr.at[n], to))

    for i in range(4):
        s = i
        landed(zn, c, s, zr.at[s])
        if s < 2:
            go(move(zn, s, fs.at[s], fr.at[s], up))
        go(move(zn, s, ts.at[4 + s], tr.at[4 + s], twin))
        s = (i + 2) % 4
        landed(zp, c, s, zr.at[4 + s])
        if s >= 2:
            go(move(zp, s, fs.at[s], fr.at[s], down))
        go(move(zp, s, ts.at[8 + s], tr.at[8 + s], twin))

    for s in (0, 2, 1, 3):
        landed(zo, c, s, fr.at[s])
        go(move(zo, s, ts.at[12 + s], tr.at[12 + s], twin))

    for n in range(1, 4):
        wait_for(zb.at[n], mr.at[n])
    cnt_ref[...] = zb[0] + zb[1] + zb[2] + zb[3]

    for s in range(4):
        wait_for(gp_ref.at[pl.ds(s * HALF, HALF), :], r2.at[s])
    own_rows(gp_ref[...], wqg.at[1], gT_ref, goT_ref)
    for n, zz in ((0, z), (1, zn), (2, zp), (3, zo)):
        for s in range(4):
            landed(zz, 1 - c, s, tr.at[4 * n + s])
    for copy in sent:
        copy.wait_send()
    for j in range(4):
        @pl.when(jnp.logical_not(jnp.logical_and(mine, slot == j)))
        def _():
            a, b = first(j)
            a.wait_send()
            b.wait_send()
            count(j).wait_send()


def attention_kernel(pk_ref, cnt_ref, wkv_ref, u_ref, qT_ref, gT_ref, poT_ref, goT_ref, g_ref, gq_ref, w_ref, e_ref, mb_ref, kv_ref, qm_ref, gm_ref,
                     qmT_ref, gmT_ref, acc_ref, m_ref, s_ref, dkv_ref, attT_ref, dqT_ref, wacc_ref):
    train = jnp.max(cnt_ref[...]).astype(jnp.int32)
    halves = lax.div(train + PC - 1, PC)
    full, odd = lax.div(halves, 2), lax.rem(halves, 2)
    last = lax.div(halves - 1, 2)

    def rows(n):
        return pl.ds(pl.multiple_of(n * KC, KC), KC)

    def packs(n):
        return pl.ds(pl.multiple_of(n * PC, PC), PC)

    def half_packs(n):
        return pl.ds(pl.multiple_of(n * ROWS, ROWS), ROWS)

    @pl.loop(halves, 2 * BLOCKS)
    def _(n):
        g_ref[half_packs(n), :] = jnp.zeros((ROWS, 384), BF)

    lane = lax.broadcasted_iota(jnp.int32, (ROWS, 128), 1)
    sub = lax.broadcasted_iota(jnp.int32, (ROWS, 128), 0)
    real = sub + HALF * (sub >= HALF).astype(jnp.int32)
    v_extra = jnp.where((lane >= HALF) & (lane < HALF + 3), 1.0, 0.0)

    def project(n):
        p = pk_ref[packs(n), :]
        for side, (cells, w) in enumerate(((p[:, 0:256], wkv_ref[0]), (p[:, 128:384], wkv_ref[1]))):
            kv = dot(cells, w)
            for half in range(2):
                first = n * KC + PC * half
                bias = jnp.where((lane == HALF) & (real + (first + HALF * side) >= train), BIAS, 0.0)
                r = pl.ds(pl.multiple_of(first + ROWS * side, ROWS), ROWS)
                own = slice(ROWS * half, ROWS * half + ROWS)
                kv_ref[r, 0:128] = (kv[own, 0:128] + bias).astype(BF)
                kv_ref[r, 128:256] = (kv[own, 128:256] + v_extra).astype(BF)

    project(0)
    project(jnp.minimum(1, last))

    attT_ref[...] = jnp.zeros_like(attT_ref)
    dqT_ref[...] = jnp.zeros_like(dqT_ref)
    wacc_ref[...] = jnp.zeros_like(wacc_ref)
    i16 = lax.broadcasted_iota(jnp.int32, (16, NQ), 0)
    lanes = [slice(NQ * h, NQ * h + NQ) for h in range(3)]
    subs = [slice(32 * h, 32 * h + 32) for h in range(3)]

    qmT_ref[...] = jnp.zeros_like(qmT_ref)
    gmT_ref[...] = jnp.zeros_like(gmT_ref)
    for q, hs in zip(lanes, subs):
        qmT_ref[hs, q] = qT_ref[hs, :]
        qm_ref[q, :] = qmT_ref[:, q].T
        qmT_ref[96:112, q] = jnp.where(i16 == 0, 1.0, 0.0).astype(BF)
    acc_ref[...] = jnp.zeros_like(acc_ref)
    m_ref[...] = jnp.full_like(m_ref, BIAS)

    def piece(n, t):
        return pl.ds(pl.multiple_of(n * KC + (t // 3) * PC, PC), PC), lanes[t % 3]

    def score(n, t):
        r, q = piece(n, t)
        s = dot(kv_ref[r, 0:128], qmT_ref[:, q])
        s_ref[t % 2] = s
        m_ref[2 + t % 2:3 + t % 2, q] = jnp.max(s, axis=0, keepdims=True)

    def weigh(n, t):
        r, q = piece(n, t)
        old = m_ref[0:1, q]
        new = jnp.maximum(old, jnp.ceil(m_ref[2 + t % 2:3 + t % 2, q] * SCALE_LOG2E))
        e = jnp.exp2(s_ref[t % 2] * SCALE_LOG2E - new).astype(BF)
        e_ref[r, q] = e
        m_ref[0:1, q] = new
        mb_ref[n, t // 3:t // 3 + 1, q] = new
        vT = kv_ref[r, 128:256].T
        vt = jnp.concatenate([vT[subs[t % 3]], vT[96:112]], 0)
        acc_ref[:, q] = acc_ref[:, q] * jnp.exp2(old - new) + dot(vt, e)

    score(0, 0)

    @pl.loop(0, full)
    def _(n):
        for t in range(6):
            if t < 5:
                score(n, t + 1)
            else:
                score(jnp.minimum(n + 1, last), 0)
            weigh(n, t)
        project(jnp.minimum(n + 2, last))

    @pl.when(odd == 1)
    def _():
        for t in range(3):
            if t < 2:
                score(full, t + 1)
            weigh(full, t)

    for q, hs in zip(lanes, subs):
        inv = 1.0 / acc_ref[32:33, q]
        att = (acc_ref[0:32, q] * inv).astype(BF)
        attT_ref[hs, :] = att
        gp = (gT_ref[hs, :].astype(F32) * inv).astype(BF)
        delta = -jnp.sum(gp.astype(F32) * att.astype(F32), axis=0, keepdims=True)
        d0 = delta.astype(BF).astype(F32)
        d1 = (delta - d0).astype(BF).astype(F32)
        d2 = delta - d0 - d1
        gmT_ref[hs, q] = gp
        gm_ref[q, :] = gmT_ref[:, q].T
        gmT_ref[96:112, q] = jnp.where(i16 == 0, d0, jnp.where(i16 == 1, d1, jnp.where(i16 == 2, d2, 0.0))).astype(BF)
    acc_ref[...] = jnp.zeros_like(acc_ref)

    def pass_two(n, many):
        size = many * PC
        r = pl.ds(pl.multiple_of(n * KC, KC), size)
        v = kv_ref[r, 128:256]
        kT = kv_ref[r, 0:128].T
        dk, dv = jnp.zeros((size, 128), F32), jnp.zeros((size, 128), F32)
        for h in range(3):
            q = lanes[h]
            ga = dot(v, gmT_ref[:, q]).astype(BF)
            e = e_ref[r, q]
            by = [jnp.exp2(mb_ref[n, t:t + 1, q] - m_ref[0:1, q]).astype(BF) for t in range(many)]
            es = jnp.concatenate([e[PC * t:PC * t + PC] * by[t] for t in range(many)], 0)
            ds = es * ga
            dv = dv + dot(es, gm_ref[q, :])
            dk = dk + dot(ds, qm_ref[q, :])
            acc_ref[0:32, q] += dot(kT[subs[h]], ds)
        dkv_ref[0:size, 0:128] = (dk * SCALE).astype(BF)
        dkv_ref[0:size, 128:256] = dv.astype(BF)
        for t in range(many):
            p = half_packs(2 * n + t)
            pT = pk_ref[p, :].T
            da, db = dkv_ref[PC * t:PC * t + ROWS, :], dkv_ref[PC * t + ROWS:PC * t + PC, :]
            g_ref[p, :] = (dot(da, u_ref[0, 0:256, :]) + dot(db, u_ref[1, 0:256, :])).astype(BF)
            wacc_ref[...] += dot(pT[0:E], da) + dot(pT[E:2 * E], db)

    @pl.loop(0, full)
    def _(n):
        pass_two(n, 2)

    @pl.when(odd == 1)
    def _():
        pass_two(full, 1)

    for q, hs in zip(lanes, subs):
        dqT_ref[hs, :] = (acc_ref[0:32, q] * SCALE).astype(BF)

    dq, at = dqT_ref[...].T, attT_ref[...].T
    gq_ref[...] = dot(dq[0:PC], u_ref[0, 256:384, :]) + dot(dq[PC:NQ], u_ref[1, 256:384, :])
    poT, goT = poT_ref[...], goT_ref[...]
    w_q = dot(poT[0:E], dq[0:PC]) + dot(poT[E:2 * E], dq[PC:NQ])
    w_o = dot(goT[0:E], at[0:PC]) + dot(goT[E:2 * E], at[PC:NQ])
    w_ref[...] = (
        dot(w_q.astype(BF), shifted((128, 384), 0, HALF))
        + dot(w_o.astype(BF), shifted((128, 384), HALF, HALF))
        + dot(wacc_ref[:, 0:128].astype(BF), shifted((128, 384), 2 * HALF, HALF))
        + dot(wacc_ref[:, 128:256].astype(BF), shifted((128, 384), 3 * HALF, HALF))
    ).astype(BF)


def reduce_kernel(g_ref, gq_ref, w_ref, ret_ref, wf_ref,
                  tw, part, hp, hn, fp, fn, fin, rs, p2,
                  ts, tr, hs_, hr, fs, fr, ks, kr, as_, ar, bs, br, cs, cr):
    z, x, yl, yh, c = place()
    mine = x // 2 == c
    own = jnp.where(mine, 1, 0)
    zp, zo, zn = (z + 1) % 4, (z + 2) % 4, (z + 3) % 4
    up, down, twin = device(zp, x, yl, yh, c), device(zn, x, yl, yh, c), device(z, x, yl, yh, 1 - c)
    slot = (x % 2) * 2 + yl
    i16 = z * 4 + x
    i8 = (yh * 2 + yl) * 2 + c
    owner = i16 < SLABS
    owns = jnp.where(owner, 1, 0)

    barrier = pltpu.get_barrier_semaphore()

    def greet(to):
        pl.semaphore_signal(barrier, inc=1, device_id=to, device_id_type=MESH)

    for to in (twin, up, down):
        greet(to)
    for j in range(4):
        @pl.when(jnp.logical_not(jnp.logical_and(mine, slot == j)))
        def _():
            greet(device(z, 2 * c + j // 2, j % 2, yh, x // 2))

    zs_, xs_ = [z, zp, zo, zn], [x, (x + 1) % 4, (x + 2) % 4, (x + 3) % 4]
    around = [(zs_[n // 4], xs_[n % 4]) for n in range(16)]
    beside = [((yl + n // 2 % 2) % 2, (yh + n // 4) % 2, (c + n % 2) % 2) for n in range(8)]
    for n in range(1, 16):
        greet(device(*around[n], yl, yh, c))
    for n in range(1, 8):
        greet(device(z, x, *beside[n]))

    pl.semaphore_wait(barrier, 3 + 4 - own + 15 + 7)

    sent = []

    def go(copy):
        copy.start()
        sent.append(copy)

    def block(zz, cc):
        return pl.ds(pl.multiple_of((zz * 2 + cc) * PC, PC), PC)

    for n, zz in enumerate((zo, zp, zn, z)):
        go(rcopy(g_ref.at[block(zz, 1 - c), :], tw.at[n], ts.at[n], tr.at[n], twin))

    def slab(n):
        return pl.ds(pl.multiple_of(n * 16, 16), 16)

    def one(n):
        zz, xx = around[n]
        to = zz * 4 + xx
        ok = to < SLABS
        r = slab(jnp.minimum(to, SLABS - 1))
        return ok, rcopy(w_ref.at[r, :], rs.at[i16], as_.at[n], ar.at[i16], device(zz, xx, yl, yh, c))

    def two(n):
        return rcopy(p2.at[i8], p2.at[i8], bs.at[n], br.at[i8], device(z, x, *beside[n]))

    my_slab = slab(jnp.minimum(i16, SLABS - 1))

    def three(n):
        mine_ = wf_ref.at[:, my_slab, :]
        return rcopy(mine_, mine_, cs.at[n], cr.at[i16], device(*around[n], yl, yh, c))

    for n in range(1, 16):
        ok, copy = one(n)

        @pl.when(ok)
        def _():
            copy.start()

    def with_twin(n, zz):
        wait_for(tw.at[n], tr.at[n])
        return g_ref[block(zz, c), :].astype(F32) + tw[n].astype(F32)

    lo, hi = pl.ds(0, 192), pl.ds(192, 192)
    part[0] = with_twin(0, zo).astype(BF)
    go(rcopy(part.at[0, lo, :], hp, hs_.at[0], hr.at[0], up))
    go(rcopy(part.at[0, hi, :], hn, hs_.at[1], hr.at[1], down))
    part[1] = with_twin(1, zp).astype(BF)
    go(rcopy(part.at[1, hi, :], fp.at[hi, :], fs.at[0], fr.at[0], up))
    part[2] = with_twin(2, zn).astype(BF)
    go(rcopy(part.at[2, lo, :], fn.at[lo, :], fs.at[1], fr.at[1], down))

    @pl.when(owner)
    def _():
        rs[i16] = w_ref[slab(jnp.minimum(i16, SLABS - 1)), :]

        for n in range(1, 16):
            m = around[n][0] * 4 + around[n][1]
            wait_for(rs.at[m], ar.at[m])

        acc = rs[0].astype(F32)
        for n in range(1, 16):
            acc = acc + rs[n].astype(F32)
        p2[i8] = acc.astype(BF)

        for n in range(1, 8):
            two(n).start()

    wait_for(hp, hr.at[0])
    part[1, 0:192, :] = (part[1, 0:192, :].astype(F32) + hp[...].astype(F32)).astype(BF)
    go(rcopy(part.at[1, lo, :], fp.at[lo, :], fs.at[2], fr.at[2], up))
    wait_for(hn, hr.at[1])
    part[2, 192:384, :] = (part[2, 192:384, :].astype(F32) + hn[...].astype(F32)).astype(BF)
    go(rcopy(part.at[2, hi, :], fn.at[hi, :], fs.at[3], fr.at[3], down))

    @pl.when(owner)
    def _():
        for yl_, yh_, c_ in beside[1:]:
            m = (yh_ * 2 + yl_) * 2 + c_
            wait_for(p2.at[m], br.at[m])

        for half in range(2):
            n = 2 * half
            acc = p2[n].astype(F32) + p2[n + 1].astype(F32) + p2[n + 4].astype(F32) + p2[n + 5].astype(F32)
            wf_ref[half, slab(jnp.minimum(i16, SLABS - 1)), :] = acc.astype(BF)

        for n in range(1, 16):
            three(n).start()

    total = with_twin(3, z) + gq_ref[...]
    wait_for(fp.at[hi, :], fr.at[0])
    wait_for(fn.at[lo, :], fr.at[1])
    wait_for(fp.at[lo, :], fr.at[2])
    wait_for(fn.at[hi, :], fr.at[3])
    fin[...] = (total + fp[...].astype(F32) + fn[...].astype(F32)).astype(BF)

    def back(s):
        to = device(z, 2 * c + s // 2, s % 2, yh, x // 2)
        return rcopy(fin.at[pl.ds(s * HALF, HALF), :], ret_ref.at[slot], ks.at[s], kr.at[slot], to)

    for s in range(4):
        keep = jnp.logical_and(mine, slot == s)

        @pl.when(keep)
        def _():
            pltpu.make_async_copy(fin.at[pl.ds(s * HALF, HALF), :], ret_ref.at[slot], kr.at[slot]).start()

        @pl.when(jnp.logical_not(keep))
        def _():
            back(s).start()

    for n in range(4):
        wait_for(ret_ref.at[n], kr.at[n])

    for n in range(1, 16):
        m = around[n][0] * 4 + around[n][1]

        @pl.when(m < SLABS)
        def _():
            r = slab(jnp.minimum(m, SLABS - 1))
            wait_for(wf_ref.at[:, r, :], cr.at[m])

    for copy in sent:
        copy.wait_send()
    for s in range(4):
        @pl.when(jnp.logical_not(jnp.logical_and(mine, slot == s)))
        def _():
            back(s).wait_send()

    for n in range(1, 16):
        ok, copy = one(n)

        @pl.when(ok)
        def _():
            copy.wait_send()

    @pl.when(owner)
    def _():
        for n in range(1, 16):
            three(n).wait_send()
        for n in range(1, 8):
            two(n).wait_send()


def final_kernel(ret_ref, wf_ref, grad_ref, gc_ref, gwq_ref, gwk_ref, gwv_ref, gwo_ref):
    sort = by_feature()
    i, j = iotas((256, E))
    right = ones_where(i == j + 64)
    total = grad_ref[...].reshape(2 * ROWS, E).astype(F32)
    for half in range(2):
        parts = []
        for f in range(2):
            r = ret_ref[2 * f + half]
            parts += [r[:, 0:E], dot(r[:, 128:384], right).astype(BF)]
        total = total + t_dot(sort, jnp.concatenate(parts, 0))
    gc_ref[...] = total.astype(BF).reshape(ROWS, 2, E)

    i, j = iotas((384, E))

    def weight(first):
        low = ones_where((i == j + first) & (j < HALF))
        high = ones_where((i == j - HALF + first) & (j >= HALF))
        return dot(wf_ref[0], low) + dot(wf_ref[1], high)

    gwq_ref[...] = weight(0)
    gwo_ref[...] = weight(HALF).T
    gwk_ref[...] = weight(2 * HALF)
    gwv_ref[...] = weight(3 * HALF)


SLABS = 12
VM = pl.BlockSpec(memory_space=pltpu.VMEM)
DMA = pltpu.SemaphoreType.DMA


def sds(shape, dtype=BF):
    return jax.ShapeDtypeStruct(shape, dtype)


def share(*args):
    return pl.pallas_call(
        share_kernel,
        out_shape=[
            sds((NR // 2, 384)), sds((8, 128), F32), sds((2, 256, 256)), sds((2, 384, 384)), sds((128, NQ)), sds((128, NQ)),
            sds((384, PC)), sds((384, PC)),
        ],
        in_specs=[VM] * 2,
        out_specs=[VM] * 8,
        scratch_shapes=[
            pltpu.VMEM((PC, 384), BF), pltpu.VMEM((2, 2, 256, 128), BF),
            pltpu.VMEM((2, HALF, 384), BF), pltpu.VMEM((2, HALF, 384), BF),
            pltpu.VMEM((8, 128), F32), pltpu.VMEM((4, 8, 128), F32), pltpu.VMEM((2, 8, 128), F32), pltpu.VMEM((4, 8, 128), F32),
            DMA((4,)), DMA((4,)), DMA((4,)), DMA((4,)), DMA((8,)), DMA((8,)), DMA((4,)), DMA((4,)), DMA((16,)), DMA((16,)),
            DMA((4,)), DMA((4,)), DMA((4,)), DMA((4,)),
        ],
        compiler_params=pltpu.CompilerParams(collective_id=1, has_side_effects=True, vmem_limit_bytes=24 * 2**20),
        cost_estimate=pl.CostEstimate(flops=10**8, bytes_accessed=60 * 10**6, transcendentals=0),
        name="share",
    )(*args)


def attention(*args):
    return pl.pallas_call(
        attention_kernel,
        out_shape=[sds((NR // 2, 384)), sds((PC, 384), F32), sds((E, 384))],
        in_specs=[VM] * 8,
        out_specs=[VM] * 3,
        scratch_shapes=[
            pltpu.VMEM((NR, 3 * NQ), BF), pltpu.VMEM((BLOCKS, 8, 3 * NQ), F32), pltpu.VMEM((NR, 256), BF),
            pltpu.VMEM((3 * NQ, 128), BF), pltpu.VMEM((3 * NQ, 128), BF),
            pltpu.VMEM((128, 3 * NQ), BF), pltpu.VMEM((128, 3 * NQ), BF),
            pltpu.VMEM((48, 3 * NQ), F32), pltpu.VMEM((8, 3 * NQ), F32),
            pltpu.VMEM((2, PC, NQ), F32), pltpu.VMEM((KC, 256), BF),
            pltpu.VMEM((128, NQ), BF), pltpu.VMEM((128, NQ), BF), pltpu.VMEM((E, 256), F32),
        ],
        compiler_params=pltpu.CompilerParams(vmem_limit_bytes=VLIM * 2**20),
        cost_estimate=pl.CostEstimate(flops=3 * 10**10, bytes_accessed=10**7, transcendentals=14 * 10**6),
        name="attention",
    )(*args)


VLIM = 45


def reduce(*args):
    return pl.pallas_call(
        reduce_kernel,
        out_shape=[sds((4, HALF, 384)), sds((2, E, 384))],
        in_specs=[VM] * 3,
        out_specs=[VM] * 2,
        scratch_shapes=[
            pltpu.VMEM((4, PC, 384), BF), pltpu.VMEM((3, PC, 384), BF),
            pltpu.VMEM((192, 384), BF), pltpu.VMEM((192, 384), BF),
            pltpu.VMEM((PC, 384), BF), pltpu.VMEM((PC, 384), BF), pltpu.VMEM((PC, 384), BF),
            pltpu.VMEM((16, 16, 384), BF), pltpu.VMEM((8, 16, 384), BF),
            DMA((4,)), DMA((4,)), DMA((2,)), DMA((2,)), DMA((4,)), DMA((4,)), DMA((4,)), DMA((4,)),
            DMA((16,)), DMA((16,)), DMA((8,)), DMA((8,)), DMA((16,)), DMA((16,)),
        ],
        compiler_params=pltpu.CompilerParams(collective_id=2, has_side_effects=True, vmem_limit_bytes=24 * 2**20),
        cost_estimate=pl.CostEstimate(flops=10**8, bytes_accessed=60 * 10**6, transcendentals=0),
        name="reduce",
    )(*args)


def final(*args):
    w = sds((E, E), F32)
    return pl.pallas_call(
        final_kernel,
        out_shape=[sds((ROWS, 2, E)), w, w, w, w],
        in_specs=[VM] * 3,
        out_specs=[VM] * 5,
        compiler_params=pltpu.CompilerParams(vmem_limit_bytes=24 * 2**20),
        name="final",
    )(*args)


def body(cells, w_query, w_key, w_value, w_out, train_flag, grad_out):
    flags = jnp.broadcast_to(train_flag.astype(BF), (1, 2, ROWS))
    parts = share(jnp.concatenate([cells, grad_out, flags], 0), jnp.concatenate([w_query, w_key, w_value, w_out], 0))
    g, gq, w = attention(*parts)
    ret, wf = reduce(g, gq, w)
    return final(ret, wf, grad_out)


def solution(mesh):
    return jax.shard_map(
        body,
        mesh=mesh,
        in_specs=(P("row", "feat", None), P(), P(), P(), P(), P("row"), P("row", "feat", None)),
        out_specs=(P("row", "feat", None), P(), P(), P(), P()),
        check_vma=False,
    )
```

```python
import jax
import jax.numpy as jnp
from jax import lax
from jax.experimental import pallas as pl
from jax.experimental.pallas import tpu as pltpu
from jax.sharding import PartitionSpec as P


HD = 32
SCALE = float(HD) ** -0.5
SCALE_LOG2E = SCALE * 1.4426950408889634
BIAS = -1e30
F32 = jnp.float32
BF = jnp.bfloat16
MESH = pl.DeviceIdType.MESH

E = 192
HALF = 96
ROWS = 192
NQ = 768
NR = 6144
KC = 768
PC = 384
BLOCKS = 8


def dot(a, b):
    return jnp.dot(a, b, preferred_element_type=F32)


def t_dot(a, b):
    return lax.dot_general(a, b, (((0,), (0,)), ((), ())), preferred_element_type=F32)


def place():
    row = lax.axis_index("row")
    feat = lax.axis_index("feat")
    return row // 8, (row // 2) % 4, row % 2, feat // 2, feat % 2


def device(z, x, yl, yh, c):
    return ((z * 4 + x) * 2 + yl, yh * 2 + c)


def iotas(shape):
    return lax.broadcasted_iota(jnp.int32, shape, 0), lax.broadcasted_iota(jnp.int32, shape, 1)


def ones_where(mask):
    return mask.astype(F32).astype(BF)


def shifted(shape, by, most=None):
    i, j = iotas(shape)
    mask = j == i + by
    if most is not None:
        mask = mask & (i < most)
    return ones_where(mask)


def by_feature():
    i, j = iotas((2 * ROWS, 2 * ROWS))
    second = i >= ROWS
    return ones_where(j == jnp.where(second, 2 * (i - ROWS) + 1, 2 * i))


def rcopy(src, dst, send, recv, to):
    return pltpu.make_async_remote_copy(
        src_ref=src, dst_ref=dst, send_sem=send, recv_sem=recv, device_id=to, device_id_type=MESH
    )


def wait_for(ref, sem):
    pltpu.make_async_copy(ref, ref, sem).wait()


def share_kernel(in_ref, weights, pk_ref, cnt_ref, wkv_ref, u_ref, qT_ref, gT_ref, poT_ref, goT_ref, gp_ref, wqg, cs, gs, cf, cb, four, zb, s1, r1, s2, r2, zs, zr, fs, fr, ts, tr, ns, nr, ms, mr):
    z, x, yl, yh, c = place()
    mine = x // 2 == c
    own = jnp.where(mine, 1, 0)
    zp, zo, zn = (z + 1) % 4, (z + 2) % 4, (z + 3) % 4
    up, down, twin = device(zp, x, yl, yh, c), device(zn, x, yl, yh, c), device(z, x, yl, yh, 1 - c)
    far = device(zo, x, yl, yh, c)
    slot = (x % 2) * 2 + yl

    barrier = pltpu.get_barrier_semaphore()

    def greet(to):
        pl.semaphore_signal(barrier, inc=1, device_id=to, device_id_type=MESH)

    for s in range(4):
        @pl.when(jnp.logical_not(jnp.logical_and(mine, slot == s)))
        def _():
            greet(device(z, 2 * c + s // 2, s % 2, yh, x // 2))
    for to in (up, down, twin):
        greet(to)
    greet(far)

    sort = by_feature()
    left, right = shifted((ROWS, 2 * E), 0), shifted((ROWS, 2 * E), E)

    def pack(first, out):
        rows = dot(sort, in_ref[first:first + ROWS].reshape(2 * ROWS, E)).astype(BF)
        for f in range(2):
            r = f * ROWS
            out[f] = (dot(rows[r:r + HALF], left) + dot(rows[r + HALF:r + ROWS], right)).astype(BF)

    flags = jnp.sum(in_ref[2 * ROWS, 0:1, :].astype(F32), axis=1, keepdims=True)
    cf[...] = jnp.broadcast_to(flags, (8, 128))
    pack(0, cs)
    pl.semaphore_wait(barrier, 4 - own + 4)

    my_rows = pl.ds(pl.multiple_of(((z * 4 + x) * 2 + yl) * HALF, HALF), HALF)
    my_slot = pl.ds(pl.multiple_of(slot * HALF, HALF), HALF)

    def first(j):
        to = device(z, 2 * c + j // 2, j % 2, yh, x // 2)
        a = rcopy(cs.at[j // 2], pk_ref.at[my_rows, :], s1.at[j], r1.at[slot], to)
        b = rcopy(gs.at[j // 2], gp_ref.at[my_slot, :], s2.at[j], r2.at[slot], to)
        return a, b

    for j in range(4):
        keep = jnp.logical_and(mine, slot == j)

        @pl.when(keep)
        def _():
            pltpu.make_async_copy(cs.at[j // 2], pk_ref.at[my_rows, :], r1.at[slot]).start()

        @pl.when(jnp.logical_not(keep))
        def _():
            first(j)[0].start()

    def count(j):
        return rcopy(cf, cb.at[slot], ns.at[j], nr.at[slot], device(z, 2 * c + j // 2, j % 2, yh, x // 2))

    for j in range(4):
        keep = jnp.logical_and(mine, slot == j)

        @pl.when(keep)
        def _():
            pltpu.make_async_copy(cf, cb.at[slot], nr.at[slot]).start()

        @pl.when(jnp.logical_not(keep))
        def _():
            count(j).start()

    def rows_of(zz, cc, s):
        return pl.ds(pl.multiple_of((zz * 2 + cc) * PC + s * HALF, HALF), HALF)

    def move(zz, s, send, recv, to):
        r = rows_of(zz, c, s)
        return rcopy(pk_ref.at[r, :], pk_ref.at[r, :], send, recv, to)

    def landed(zz, cc, s, recv):
        wait_for(pk_ref.at[rows_of(zz, cc, s), :], recv)

    sent = []

    def go(copy):
        copy.start()
        sent.append(copy)

    i, j = iotas((E, 128))
    heads = ones_where((i == j + HALF * yl) & (j < HALF))
    wq = dot(weights[0:192, :], heads).astype(BF)
    wk = dot(weights[192:384, :], heads).astype(BF)
    wv = dot(weights[384:576, :], heads).astype(BF)
    wo = t_dot(weights[576:768, :], heads).astype(BF)
    for out, w in ((wkv_ref, jnp.concatenate([wk, wv], 1)), (wqg.at[0], wq), (wqg.at[1], wo)):
        none = jnp.zeros((64, w.shape[1]), BF)
        out[0, 0:192, :] = w
        out[0, 192:256, :] = none
        out[1, 64:256, :] = w
        out[1, 0:64, :] = none
    for n, w in enumerate((wk, wv, wq)):
        u_ref[0, 128 * n:128 * n + 128, :] = t_dot(w, left).astype(BF)
        u_ref[1, 128 * n:128 * n + 128, :] = t_dot(w, right).astype(BF)

    def own_rows(src, w, out, turned):
        turned[...] = src.T
        out[:, 0:PC] = dot(src[:, 0:256], w[0]).astype(BF).T
        out[:, PC:NQ] = dot(src[:, 128:384], w[1]).astype(BF).T

    for i in range(4):
        s, t = i, (i + 2) % 4
        if i < 2:
            landed(z, c, s, r1.at[s])
            landed(z, c, t, r1.at[t])
        go(move(z, s, zs.at[s], zr.at[s], up))
        go(move(z, t, zs.at[4 + t], zr.at[4 + t], down))
        go(move(z, s, ts.at[s], tr.at[s], twin))

    for s in range(4):
        wait_for(cb.at[s], nr.at[s])
    four[0] = cb[0] + cb[1] + cb[2] + cb[3]
    go(rcopy(four.at[0], four.at[1], ms.at[0], mr.at[0], twin))
    pack(ROWS, gs)
    for j in range(4):
        keep = jnp.logical_and(mine, slot == j)

        @pl.when(keep)
        def _():
            pltpu.make_async_copy(gs.at[j // 2], gp_ref.at[my_slot, :], r2.at[slot]).start()

        @pl.when(jnp.logical_not(keep))
        def _():
            first(j)[1].start()

    own_rows(pk_ref[pl.ds(pl.multiple_of((z * 2 + c) * PC, PC), PC), :], wqg.at[0], qT_ref, poT_ref)
    wait_for(four.at[1], mr.at[0])
    zb[0] = four[0] + four[1]
    for n, to in ((1, up), (2, far), (3, down)):
        go(rcopy(zb.at[0], zb.at[n], ms.at[n], mr.at[n], to))

    for i in range(4):
        s = i
        landed(zn, c, s, zr.at[s])
        if s < 2:
            go(move(zn, s, fs.at[s], fr.at[s], up))
        go(move(zn, s, ts.at[4 + s], tr.at[4 + s], twin))
        s = (i + 2) % 4
        landed(zp, c, s, zr.at[4 + s])
        if s >= 2:
            go(move(zp, s, fs.at[s], fr.at[s], down))
        go(move(zp, s, ts.at[8 + s], tr.at[8 + s], twin))

    for s in (0, 2, 1, 3):
        landed(zo, c, s, fr.at[s])
        go(move(zo, s, ts.at[12 + s], tr.at[12 + s], twin))

    for n in range(1, 4):
        wait_for(zb.at[n], mr.at[n])
    cnt_ref[...] = zb[0] + zb[1] + zb[2] + zb[3]

    for s in range(4):
        wait_for(gp_ref.at[pl.ds(s * HALF, HALF), :], r2.at[s])
    own_rows(gp_ref[...], wqg.at[1], gT_ref, goT_ref)
    for n, zz in ((0, z), (1, zn), (2, zp), (3, zo)):
        for s in range(4):
            landed(zz, 1 - c, s, tr.at[4 * n + s])
    for copy in sent:
        copy.wait_send()
    for j in range(4):
        @pl.when(jnp.logical_not(jnp.logical_and(mine, slot == j)))
        def _():
            a, b = first(j)
            a.wait_send()
            b.wait_send()
            count(j).wait_send()


def attention_kernel(pk_ref, cnt_ref, wkv_ref, u_ref, qT_ref, gT_ref, poT_ref, goT_ref, g_ref, gq_ref, w_ref, e_ref, mb_ref, kv_ref, qm_ref, gm_ref,
                     qmT_ref, gmT_ref, acc_ref, m_ref, s_ref, dkv_ref, attT_ref, dqT_ref, wacc_ref):
    train = jnp.max(cnt_ref[...]).astype(jnp.int32)
    halves = lax.div(train + PC - 1, PC)
    full, odd = lax.div(halves, 2), lax.rem(halves, 2)
    last = lax.div(halves - 1, 2)

    def rows(n):
        return pl.ds(pl.multiple_of(n * KC, KC), KC)

    def packs(n):
        return pl.ds(pl.multiple_of(n * PC, PC), PC)

    def half_packs(n):
        return pl.ds(pl.multiple_of(n * ROWS, ROWS), ROWS)

    @pl.loop(halves, 2 * BLOCKS)
    def _(n):
        g_ref[half_packs(n), :] = jnp.zeros((ROWS, 384), BF)

    lane = lax.broadcasted_iota(jnp.int32, (ROWS, 128), 1)
    sub = lax.broadcasted_iota(jnp.int32, (ROWS, 128), 0)
    real = sub + HALF * (sub >= HALF).astype(jnp.int32)
    v_extra = jnp.where((lane >= HALF) & (lane < HALF + 3), 1.0, 0.0)

    def project(n):
        p = pk_ref[packs(n), :]
        for side, (cells, w) in enumerate(((p[:, 0:256], wkv_ref[0]), (p[:, 128:384], wkv_ref[1]))):
            kv = dot(cells, w)
            for half in range(2):
                first = n * KC + PC * half
                bias = jnp.where((lane == HALF) & (real + (first + HALF * side) >= train), BIAS, 0.0)
                r = pl.ds(pl.multiple_of(first + ROWS * side, ROWS), ROWS)
                own = slice(ROWS * half, ROWS * half + ROWS)
                kv_ref[r, 0:128] = (kv[own, 0:128] + bias).astype(BF)
                kv_ref[r, 128:256] = (kv[own, 128:256] + v_extra).astype(BF)

    project(0)
    project(jnp.minimum(1, last))

    attT_ref[...] = jnp.zeros_like(attT_ref)
    dqT_ref[...] = jnp.zeros_like(dqT_ref)
    wacc_ref[...] = jnp.zeros_like(wacc_ref)
    i16 = lax.broadcasted_iota(jnp.int32, (16, NQ), 0)
    lanes = [slice(NQ * h, NQ * h + NQ) for h in range(3)]
    subs = [slice(32 * h, 32 * h + 32) for h in range(3)]

    qmT_ref[...] = jnp.zeros_like(qmT_ref)
    gmT_ref[...] = jnp.zeros_like(gmT_ref)
    for q, hs in zip(lanes, subs):
        qmT_ref[hs, q] = qT_ref[hs, :]
        qm_ref[q, :] = qmT_ref[:, q].T
        qmT_ref[96:112, q] = jnp.where(i16 == 0, 1.0, 0.0).astype(BF)
    acc_ref[...] = jnp.zeros_like(acc_ref)
    m_ref[...] = jnp.full_like(m_ref, BIAS)

    def piece(n, t):
        return pl.ds(pl.multiple_of(n * KC + (t // 3) * PC, PC), PC), lanes[t % 3]

    def score(n, t):
        r, q = piece(n, t)
        s = dot(kv_ref[r, 0:128], qmT_ref[:, q])
        s_ref[t % 2] = s
        m_ref[2 + t % 2:3 + t % 2, q] = jnp.max(s, axis=0, keepdims=True)

    def weigh(n, t):
        r, q = piece(n, t)
        old = m_ref[0:1, q]
        new = jnp.maximum(old, jnp.ceil(m_ref[2 + t % 2:3 + t % 2, q] * SCALE_LOG2E))
        e = jnp.exp2(s_ref[t % 2] * SCALE_LOG2E - new).astype(BF)
        e_ref[r, q] = e
        m_ref[0:1, q] = new
        mb_ref[n, t // 3:t // 3 + 1, q] = new
        vT = kv_ref[r, 128:256].T
        vt = jnp.concatenate([vT[subs[t % 3]], vT[96:112]], 0)
        acc_ref[:, q] = acc_ref[:, q] * jnp.exp2(old - new) + dot(vt, e)

    score(0, 0)

    @pl.loop(0, full)
    def _(n):
        for t in range(6):
            if t < 5:
                score(n, t + 1)
            else:
                score(jnp.minimum(n + 1, last), 0)
            weigh(n, t)
        project(jnp.minimum(n + 2, last))

    @pl.when(odd == 1)
    def _():
        for t in range(3):
            if t < 2:
                score(full, t + 1)
            weigh(full, t)

    for q, hs in zip(lanes, subs):
        inv = 1.0 / acc_ref[32:33, q]
        att = (acc_ref[0:32, q] * inv).astype(BF)
        attT_ref[hs, :] = att
        gp = (gT_ref[hs, :].astype(F32) * inv).astype(BF)
        delta = -jnp.sum(gp.astype(F32) * att.astype(F32), axis=0, keepdims=True)
        d0 = delta.astype(BF).astype(F32)
        d1 = (delta - d0).astype(BF).astype(F32)
        d2 = delta - d0 - d1
        gmT_ref[hs, q] = gp
        gm_ref[q, :] = gmT_ref[:, q].T
        gmT_ref[96:112, q] = jnp.where(i16 == 0, d0, jnp.where(i16 == 1, d1, jnp.where(i16 == 2, d2, 0.0))).astype(BF)
    acc_ref[...] = jnp.zeros_like(acc_ref)

    def pass_two(n, many):
        size = many * PC
        r = pl.ds(pl.multiple_of(n * KC, KC), size)
        v = kv_ref[r, 128:256]
        kT = kv_ref[r, 0:128].T
        dk, dv = jnp.zeros((size, 128), F32), jnp.zeros((size, 128), F32)
        for h in range(3):
            q = lanes[h]
            ga = dot(v, gmT_ref[:, q]).astype(BF)
            e = e_ref[r, q]
            by = [jnp.exp2(mb_ref[n, t:t + 1, q] - m_ref[0:1, q]).astype(BF) for t in range(many)]
            es = jnp.concatenate([e[PC * t:PC * t + PC] * by[t] for t in range(many)], 0)
            ds = es * ga
            dv = dv + dot(es, gm_ref[q, :])
            dk = dk + dot(ds, qm_ref[q, :])
            acc_ref[0:32, q] += dot(kT[subs[h]], ds)
        dkv_ref[0:size, 0:128] = (dk * SCALE).astype(BF)
        dkv_ref[0:size, 128:256] = dv.astype(BF)
        for t in range(many):
            p = half_packs(2 * n + t)
            pT = pk_ref[p, :].T
            da, db = dkv_ref[PC * t:PC * t + ROWS, :], dkv_ref[PC * t + ROWS:PC * t + PC, :]
            g_ref[p, :] = (dot(da, u_ref[0, 0:256, :]) + dot(db, u_ref[1, 0:256, :])).astype(BF)
            wacc_ref[...] += dot(pT[0:E], da) + dot(pT[E:2 * E], db)

    @pl.loop(0, full)
    def _(n):
        pass_two(n, 2)

    @pl.when(odd == 1)
    def _():
        pass_two(full, 1)

    for q, hs in zip(lanes, subs):
        dqT_ref[hs, :] = (acc_ref[0:32, q] * SCALE).astype(BF)

    dq, at = dqT_ref[...].T, attT_ref[...].T
    gq_ref[...] = dot(dq[0:PC], u_ref[0, 256:384, :]) + dot(dq[PC:NQ], u_ref[1, 256:384, :])
    poT, goT = poT_ref[...], goT_ref[...]
    w_q = dot(poT[0:E], dq[0:PC]) + dot(poT[E:2 * E], dq[PC:NQ])
    w_o = dot(goT[0:E], at[0:PC]) + dot(goT[E:2 * E], at[PC:NQ])
    w_ref[...] = (
        dot(w_q.astype(BF), shifted((128, 384), 0, HALF))
        + dot(w_o.astype(BF), shifted((128, 384), HALF, HALF))
        + dot(wacc_ref[:, 0:128].astype(BF), shifted((128, 384), 2 * HALF, HALF))
        + dot(wacc_ref[:, 128:256].astype(BF), shifted((128, 384), 3 * HALF, HALF))
    ).astype(BF)


def reduce_kernel(g_ref, gq_ref, w_ref, ret_ref, wf_ref,
                  tw, part, hp, hn, fp, fn, fin, rs, p2,
                  ts, tr, hs_, hr, fs, fr, ks, kr, as_, ar, bs, br, cs, cr):
    z, x, yl, yh, c = place()
    mine = x // 2 == c
    own = jnp.where(mine, 1, 0)
    zp, zo, zn = (z + 1) % 4, (z + 2) % 4, (z + 3) % 4
    up, down, twin = device(zp, x, yl, yh, c), device(zn, x, yl, yh, c), device(z, x, yl, yh, 1 - c)
    slot = (x % 2) * 2 + yl
    i16 = z * 4 + x
    i8 = (yh * 2 + yl) * 2 + c
    owner = i16 < SLABS
    owns = jnp.where(owner, 1, 0)

    barrier = pltpu.get_barrier_semaphore()

    def greet(to):
        pl.semaphore_signal(barrier, inc=1, device_id=to, device_id_type=MESH)

    for to in (twin, up, down):
        greet(to)
    for j in range(4):
        @pl.when(jnp.logical_not(jnp.logical_and(mine, slot == j)))
        def _():
            greet(device(z, 2 * c + j // 2, j % 2, yh, x // 2))

    zs_, xs_ = [z, zp, zo, zn], [x, (x + 1) % 4, (x + 2) % 4, (x + 3) % 4]
    around = [(zs_[n // 4], xs_[n % 4]) for n in range(16)]
    beside = [((yl + n // 2 % 2) % 2, (yh + n // 4) % 2, (c + n % 2) % 2) for n in range(8)]
    for n in range(1, 16):
        greet(device(*around[n], yl, yh, c))
    for n in range(1, 8):
        greet(device(z, x, *beside[n]))

    pl.semaphore_wait(barrier, 3 + 4 - own + 15 + 7)

    sent = []

    def go(copy):
        copy.start()
        sent.append(copy)

    def block(zz, cc):
        return pl.ds(pl.multiple_of((zz * 2 + cc) * PC, PC), PC)

    for n, zz in enumerate((zo, zp, zn, z)):
        go(rcopy(g_ref.at[block(zz, 1 - c), :], tw.at[n], ts.at[n], tr.at[n], twin))

    def slab(n):
        return pl.ds(pl.multiple_of(n * 16, 16), 16)

    def one(n):
        zz, xx = around[n]
        to = zz * 4 + xx
        ok = to < SLABS
        r = slab(jnp.minimum(to, SLABS - 1))
        return ok, rcopy(w_ref.at[r, :], rs.at[i16], as_.at[n], ar.at[i16], device(zz, xx, yl, yh, c))

    def two(n):
        return rcopy(p2.at[i8], p2.at[i8], bs.at[n], br.at[i8], device(z, x, *beside[n]))

    my_slab = slab(jnp.minimum(i16, SLABS - 1))

    def three(n):
        mine_ = wf_ref.at[:, my_slab, :]
        return rcopy(mine_, mine_, cs.at[n], cr.at[i16], device(*around[n], yl, yh, c))

    for n in range(1, 16):
        ok, copy = one(n)

        @pl.when(ok)
        def _():
            copy.start()

    def with_twin(n, zz):
        wait_for(tw.at[n], tr.at[n])
        return g_ref[block(zz, c), :].astype(F32) + tw[n].astype(F32)

    lo, hi = pl.ds(0, 192), pl.ds(192, 192)
    part[0] = with_twin(0, zo).astype(BF)
    go(rcopy(part.at[0, lo, :], hp, hs_.at[0], hr.at[0], up))
    go(rcopy(part.at[0, hi, :], hn, hs_.at[1], hr.at[1], down))
    part[1] = with_twin(1, zp).astype(BF)
    go(rcopy(part.at[1, hi, :], fp.at[hi, :], fs.at[0], fr.at[0], up))
    part[2] = with_twin(2, zn).astype(BF)
    go(rcopy(part.at[2, lo, :], fn.at[lo, :], fs.at[1], fr.at[1], down))

    @pl.when(owner)
    def _():
        rs[i16] = w_ref[slab(jnp.minimum(i16, SLABS - 1)), :]

        for n in range(1, 16):
            m = around[n][0] * 4 + around[n][1]
            wait_for(rs.at[m], ar.at[m])

        acc = rs[0].astype(F32)
        for n in range(1, 16):
            acc = acc + rs[n].astype(F32)
        p2[i8] = acc.astype(BF)

        for n in range(1, 8):
            two(n).start()

    wait_for(hp, hr.at[0])
    part[1, 0:192, :] = (part[1, 0:192, :].astype(F32) + hp[...].astype(F32)).astype(BF)
    go(rcopy(part.at[1, lo, :], fp.at[lo, :], fs.at[2], fr.at[2], up))
    wait_for(hn, hr.at[1])
    part[2, 192:384, :] = (part[2, 192:384, :].astype(F32) + hn[...].astype(F32)).astype(BF)
    go(rcopy(part.at[2, hi, :], fn.at[hi, :], fs.at[3], fr.at[3], down))

    @pl.when(owner)
    def _():
        for yl_, yh_, c_ in beside[1:]:
            m = (yh_ * 2 + yl_) * 2 + c_
            wait_for(p2.at[m], br.at[m])

        for half in range(2):
            n = 2 * half
            acc = p2[n].astype(F32) + p2[n + 1].astype(F32) + p2[n + 4].astype(F32) + p2[n + 5].astype(F32)
            wf_ref[half, slab(jnp.minimum(i16, SLABS - 1)), :] = acc.astype(BF)

        for n in range(1, 16):
            three(n).start()

    total = with_twin(3, z) + gq_ref[...]
    wait_for(fp.at[hi, :], fr.at[0])
    wait_for(fn.at[lo, :], fr.at[1])
    wait_for(fp.at[lo, :], fr.at[2])
    wait_for(fn.at[hi, :], fr.at[3])
    fin[...] = (total + fp[...].astype(F32) + fn[...].astype(F32)).astype(BF)

    def back(s):
        to = device(z, 2 * c + s // 2, s % 2, yh, x // 2)
        return rcopy(fin.at[pl.ds(s * HALF, HALF), :], ret_ref.at[slot], ks.at[s], kr.at[slot], to)

    for s in range(4):
        keep = jnp.logical_and(mine, slot == s)

        @pl.when(keep)
        def _():
            pltpu.make_async_copy(fin.at[pl.ds(s * HALF, HALF), :], ret_ref.at[slot], kr.at[slot]).start()

        @pl.when(jnp.logical_not(keep))
        def _():
            back(s).start()

    for n in range(4):
        wait_for(ret_ref.at[n], kr.at[n])

    for n in range(1, 16):
        m = around[n][0] * 4 + around[n][1]

        @pl.when(m < SLABS)
        def _():
            r = slab(jnp.minimum(m, SLABS - 1))
            wait_for(wf_ref.at[:, r, :], cr.at[m])

    for copy in sent:
        copy.wait_send()
    for s in range(4):
        @pl.when(jnp.logical_not(jnp.logical_and(mine, slot == s)))
        def _():
            back(s).wait_send()

    for n in range(1, 16):
        ok, copy = one(n)

        @pl.when(ok)
        def _():
            copy.wait_send()

    @pl.when(owner)
    def _():
        for n in range(1, 16):
            three(n).wait_send()
        for n in range(1, 8):
            two(n).wait_send()


def final_kernel(ret_ref, wf_ref, grad_ref, gc_ref, gwq_ref, gwk_ref, gwv_ref, gwo_ref):
    sort = by_feature()
    i, j = iotas((256, E))
    right = ones_where(i == j + 64)
    total = grad_ref[...].reshape(2 * ROWS, E).astype(F32)
    for half in range(2):
        parts = []
        for f in range(2):
            r = ret_ref[2 * f + half]
            parts += [r[:, 0:E], dot(r[:, 128:384], right).astype(BF)]
        total = total + t_dot(sort, jnp.concatenate(parts, 0))
    gc_ref[...] = total.astype(BF).reshape(ROWS, 2, E)

    i, j = iotas((384, E))

    def weight(first):
        low = ones_where((i == j + first) & (j < HALF))
        high = ones_where((i == j - HALF + first) & (j >= HALF))
        return dot(wf_ref[0], low) + dot(wf_ref[1], high)

    gwq_ref[...] = weight(0)
    gwo_ref[...] = weight(HALF).T
    gwk_ref[...] = weight(2 * HALF)
    gwv_ref[...] = weight(3 * HALF)


SLABS = 12
VM = pl.BlockSpec(memory_space=pltpu.VMEM)
DMA = pltpu.SemaphoreType.DMA


def sds(shape, dtype=BF):
    return jax.ShapeDtypeStruct(shape, dtype)


def share(*args):
    return pl.pallas_call(
        share_kernel,
        out_shape=[
            sds((NR // 2, 384)), sds((8, 128), F32), sds((2, 256, 256)), sds((2, 384, 384)), sds((128, NQ)), sds((128, NQ)),
            sds((384, PC)), sds((384, PC)),
        ],
        in_specs=[VM] * 2,
        out_specs=[VM] * 8,
        scratch_shapes=[
            pltpu.VMEM((PC, 384), BF), pltpu.VMEM((2, 2, 256, 128), BF),
            pltpu.VMEM((2, HALF, 384), BF), pltpu.VMEM((2, HALF, 384), BF),
            pltpu.VMEM((8, 128), F32), pltpu.VMEM((4, 8, 128), F32), pltpu.VMEM((2, 8, 128), F32), pltpu.VMEM((4, 8, 128), F32),
            DMA((4,)), DMA((4,)), DMA((4,)), DMA((4,)), DMA((8,)), DMA((8,)), DMA((4,)), DMA((4,)), DMA((16,)), DMA((16,)),
            DMA((4,)), DMA((4,)), DMA((4,)), DMA((4,)),
        ],
        compiler_params=pltpu.CompilerParams(collective_id=1, has_side_effects=True, vmem_limit_bytes=24 * 2**20),
        cost_estimate=pl.CostEstimate(flops=10**8, bytes_accessed=60 * 10**6, transcendentals=0),
        name="share",
    )(*args)


def attention(*args):
    return pl.pallas_call(
        attention_kernel,
        out_shape=[sds((NR // 2, 384)), sds((PC, 384), F32), sds((E, 384))],
        in_specs=[VM] * 8,
        out_specs=[VM] * 3,
        scratch_shapes=[
            pltpu.VMEM((NR, 3 * NQ), BF), pltpu.VMEM((BLOCKS, 8, 3 * NQ), F32), pltpu.VMEM((NR, 256), BF),
            pltpu.VMEM((3 * NQ, 128), BF), pltpu.VMEM((3 * NQ, 128), BF),
            pltpu.VMEM((128, 3 * NQ), BF), pltpu.VMEM((128, 3 * NQ), BF),
            pltpu.VMEM((48, 3 * NQ), F32), pltpu.VMEM((8, 3 * NQ), F32),
            pltpu.VMEM((2, PC, NQ), F32), pltpu.VMEM((KC, 256), BF),
            pltpu.VMEM((128, NQ), BF), pltpu.VMEM((128, NQ), BF), pltpu.VMEM((E, 256), F32),
        ],
        compiler_params=pltpu.CompilerParams(vmem_limit_bytes=VLIM * 2**20),
        cost_estimate=pl.CostEstimate(flops=3 * 10**10, bytes_accessed=10**7, transcendentals=14 * 10**6),
        name="attention",
    )(*args)


VLIM = 45


def reduce(*args):
    return pl.pallas_call(
        reduce_kernel,
        out_shape=[sds((4, HALF, 384)), sds((2, E, 384))],
        in_specs=[VM] * 3,
        out_specs=[VM] * 2,
        scratch_shapes=[
            pltpu.VMEM((4, PC, 384), BF), pltpu.VMEM((3, PC, 384), BF),
            pltpu.VMEM((192, 384), BF), pltpu.VMEM((192, 384), BF),
            pltpu.VMEM((PC, 384), BF), pltpu.VMEM((PC, 384), BF), pltpu.VMEM((PC, 384), BF),
            pltpu.VMEM((16, 16, 384), BF), pltpu.VMEM((8, 16, 384), BF),
            DMA((4,)), DMA((4,)), DMA((2,)), DMA((2,)), DMA((4,)), DMA((4,)), DMA((4,)), DMA((4,)),
            DMA((16,)), DMA((16,)), DMA((8,)), DMA((8,)), DMA((16,)), DMA((16,)),
        ],
        compiler_params=pltpu.CompilerParams(collective_id=2, has_side_effects=True, vmem_limit_bytes=24 * 2**20),
        cost_estimate=pl.CostEstimate(flops=10**8, bytes_accessed=60 * 10**6, transcendentals=0),
        name="reduce",
    )(*args)


def final(*args):
    w = sds((E, E), F32)
    return pl.pallas_call(
        final_kernel,
        out_shape=[sds((ROWS, 2, E)), w, w, w, w],
        in_specs=[VM] * 3,
        out_specs=[VM] * 5,
        compiler_params=pltpu.CompilerParams(vmem_limit_bytes=24 * 2**20),
        name="final",
    )(*args)


def body(cells, w_query, w_key, w_value, w_out, train_flag, grad_out):
    flags = jnp.broadcast_to(train_flag.astype(BF), (1, 2, ROWS))
    parts = share(jnp.concatenate([cells, grad_out, flags], 0), jnp.concatenate([w_query, w_key, w_value, w_out], 0))
    g, gq, w = attention(*parts)
    ret, wf = reduce(g, gq, w)
    return final(ret, wf, grad_out)


def solution(mesh):
    return jax.shard_map(
        body,
        mesh=mesh,
        in_specs=(P("row", "feat", None), P(), P(), P(), P(), P("row"), P("row", "feat", None)),
        out_specs=(P("row", "feat", None), P(), P(), P(), P()),
        check_vma=False,
    )
```

```python
import jax
import jax.numpy as jnp
from jax import lax
from jax.experimental import pallas as pl
from jax.experimental.pallas import tpu as pltpu
from jax.sharding import PartitionSpec as P


HD = 32
SCALE = float(HD) ** -0.5
SCALE_LOG2E = SCALE * 1.4426950408889634
BIAS = -1e30
F32 = jnp.float32
BF = jnp.bfloat16
MESH = pl.DeviceIdType.MESH

E = 192
HALF = 96
ROWS = 192
NQ = 768
NR = 6144
KC = 768
PC = 384
BLOCKS = 8


def dot(a, b):
    return jnp.dot(a, b, preferred_element_type=F32)


def t_dot(a, b):
    return lax.dot_general(a, b, (((0,), (0,)), ((), ())), preferred_element_type=F32)


def place():
    row = lax.axis_index("row")
    feat = lax.axis_index("feat")
    return row // 8, (row // 2) % 4, row % 2, feat // 2, feat % 2


def device(z, x, yl, yh, c):
    return ((z * 4 + x) * 2 + yl, yh * 2 + c)


def iotas(shape):
    return lax.broadcasted_iota(jnp.int32, shape, 0), lax.broadcasted_iota(jnp.int32, shape, 1)


def ones_where(mask):
    return mask.astype(F32).astype(BF)


def shifted(shape, by, most=None):
    i, j = iotas(shape)
    mask = j == i + by
    if most is not None:
        mask = mask & (i < most)
    return ones_where(mask)


def by_feature():
    i, j = iotas((2 * ROWS, 2 * ROWS))
    second = i >= ROWS
    return ones_where(j == jnp.where(second, 2 * (i - ROWS) + 1, 2 * i))


def rcopy(src, dst, send, recv, to):
    return pltpu.make_async_remote_copy(
        src_ref=src, dst_ref=dst, send_sem=send, recv_sem=recv, device_id=to, device_id_type=MESH
    )


def wait_for(ref, sem):
    pltpu.make_async_copy(ref, ref, sem).wait()


def share_kernel(in_ref, weights, pk_ref, cnt_ref, wkv_ref, u_ref, qT_ref, gT_ref, poT_ref, goT_ref, gp_ref, wqg, cs, gs, cf, cb, four, zb, s1, r1, s2, r2, zs, zr, fs, fr, ts, tr, ns, nr, ms, mr):
    z, x, yl, yh, c = place()
    mine = x // 2 == c
    own = jnp.where(mine, 1, 0)
    zp, zo, zn = (z + 1) % 4, (z + 2) % 4, (z + 3) % 4
    up, down, twin = device(zp, x, yl, yh, c), device(zn, x, yl, yh, c), device(z, x, yl, yh, 1 - c)
    far = device(zo, x, yl, yh, c)
    slot = (x % 2) * 2 + yl

    barrier = pltpu.get_barrier_semaphore()

    def greet(to):
        pl.semaphore_signal(barrier, inc=1, device_id=to, device_id_type=MESH)

    for s in range(4):
        @pl.when(jnp.logical_not(jnp.logical_and(mine, slot == s)))
        def _():
            greet(device(z, 2 * c + s // 2, s % 2, yh, x // 2))
    for to in (up, down, twin):
        greet(to)
    greet(far)

    sort = by_feature()
    left, right = shifted((ROWS, 2 * E), 0), shifted((ROWS, 2 * E), E)

    def pack(first, out):
        rows = dot(sort, in_ref[first:first + ROWS].reshape(2 * ROWS, E)).astype(BF)
        for f in range(2):
            r = f * ROWS
            out[f] = (dot(rows[r:r + HALF], left) + dot(rows[r + HALF:r + ROWS], right)).astype(BF)

    flags = jnp.sum(in_ref[2 * ROWS, 0:1, :].astype(F32), axis=1, keepdims=True)
    cf[...] = jnp.broadcast_to(flags, (8, 128))
    pack(0, cs)
    pl.semaphore_wait(barrier, 4 - own + 4)

    my_rows = pl.ds(pl.multiple_of(((z * 4 + x) * 2 + yl) * HALF, HALF), HALF)
    my_slot = pl.ds(pl.multiple_of(slot * HALF, HALF), HALF)

    def first(j):
        to = device(z, 2 * c + j // 2, j % 2, yh, x // 2)
        a = rcopy(cs.at[j // 2], pk_ref.at[my_rows, :], s1.at[j], r1.at[slot], to)
        b = rcopy(gs.at[j // 2], gp_ref.at[my_slot, :], s2.at[j], r2.at[slot], to)
        return a, b

    for j in range(4):
        keep = jnp.logical_and(mine, slot == j)

        @pl.when(keep)
        def _():
            pltpu.make_async_copy(cs.at[j // 2], pk_ref.at[my_rows, :], r1.at[slot]).start()

        @pl.when(jnp.logical_not(keep))
        def _():
            first(j)[0].start()

    def count(j):
        return rcopy(cf, cb.at[slot], ns.at[j], nr.at[slot], device(z, 2 * c + j // 2, j % 2, yh, x // 2))

    for j in range(4):
        keep = jnp.logical_and(mine, slot == j)

        @pl.when(keep)
        def _():
            pltpu.make_async_copy(cf, cb.at[slot], nr.at[slot]).start()

        @pl.when(jnp.logical_not(keep))
        def _():
            count(j).start()

    def rows_of(zz, cc, s):
        return pl.ds(pl.multiple_of((zz * 2 + cc) * PC + s * HALF, HALF), HALF)

    def move(zz, s, send, recv, to):
        r = rows_of(zz, c, s)
        return rcopy(pk_ref.at[r, :], pk_ref.at[r, :], send, recv, to)

    def landed(zz, cc, s, recv):
        wait_for(pk_ref.at[rows_of(zz, cc, s), :], recv)

    sent = []

    def go(copy):
        copy.start()
        sent.append(copy)

    i, j = iotas((E, 128))
    heads = ones_where((i == j + HALF * yl) & (j < HALF))
    wq = dot(weights[0:192, :], heads).astype(BF)
    wk = dot(weights[192:384, :], heads).astype(BF)
    wv = dot(weights[384:576, :], heads).astype(BF)
    wo = t_dot(weights[576:768, :], heads).astype(BF)
    for out, w in ((wkv_ref, jnp.concatenate([wk, wv], 1)), (wqg.at[0], wq), (wqg.at[1], wo)):
        none = jnp.zeros((64, w.shape[1]), BF)
        out[0, 0:192, :] = w
        out[0, 192:256, :] = none
        out[1, 64:256, :] = w
        out[1, 0:64, :] = none
    for n, w in enumerate((wk, wv, wq)):
        u_ref[0, 128 * n:128 * n + 128, :] = t_dot(w, left).astype(BF)
        u_ref[1, 128 * n:128 * n + 128, :] = t_dot(w, right).astype(BF)

    def own_rows(src, w, out, turned):
        turned[...] = src.T
        out[:, 0:PC] = dot(src[:, 0:256], w[0]).astype(BF).T
        out[:, PC:NQ] = dot(src[:, 128:384], w[1]).astype(BF).T

    for i in range(4):
        s, t = i, (i + 2) % 4
        if i < 2:
            landed(z, c, s, r1.at[s])
            landed(z, c, t, r1.at[t])
        go(move(z, s, zs.at[s], zr.at[s], up))
        go(move(z, t, zs.at[4 + t], zr.at[4 + t], down))
        go(move(z, s, ts.at[s], tr.at[s], twin))

    for s in range(4):
        wait_for(cb.at[s], nr.at[s])
    four[0] = cb[0] + cb[1] + cb[2] + cb[3]
    go(rcopy(four.at[0], four.at[1], ms.at[0], mr.at[0], twin))
    pack(ROWS, gs)
    for j in range(4):
        keep = jnp.logical_and(mine, slot == j)

        @pl.when(keep)
        def _():
            pltpu.make_async_copy(gs.at[j // 2], gp_ref.at[my_slot, :], r2.at[slot]).start()

        @pl.when(jnp.logical_not(keep))
        def _():
            first(j)[1].start()

    own_rows(pk_ref[pl.ds(pl.multiple_of((z * 2 + c) * PC, PC), PC), :], wqg.at[0], qT_ref, poT_ref)
    wait_for(four.at[1], mr.at[0])
    zb[0] = four[0] + four[1]
    for n, to in ((1, up), (2, far), (3, down)):
        go(rcopy(zb.at[0], zb.at[n], ms.at[n], mr.at[n], to))

    for i in range(4):
        s = i
        landed(zn, c, s, zr.at[s])
        if s < 2:
            go(move(zn, s, fs.at[s], fr.at[s], up))
        go(move(zn, s, ts.at[4 + s], tr.at[4 + s], twin))
        s = (i + 2) % 4
        landed(zp, c, s, zr.at[4 + s])
        if s >= 2:
            go(move(zp, s, fs.at[s], fr.at[s], down))
        go(move(zp, s, ts.at[8 + s], tr.at[8 + s], twin))

    for s in (0, 2, 1, 3):
        landed(zo, c, s, fr.at[s])
        go(move(zo, s, ts.at[12 + s], tr.at[12 + s], twin))

    for n in range(1, 4):
        wait_for(zb.at[n], mr.at[n])
    cnt_ref[...] = zb[0] + zb[1] + zb[2] + zb[3]

    for s in range(4):
        wait_for(gp_ref.at[pl.ds(s * HALF, HALF), :], r2.at[s])
    own_rows(gp_ref[...], wqg.at[1], gT_ref, goT_ref)
    for n, zz in ((0, z), (1, zn), (2, zp), (3, zo)):
        for s in range(4):
            landed(zz, 1 - c, s, tr.at[4 * n + s])
    for copy in sent:
        copy.wait_send()
    for j in range(4):
        @pl.when(jnp.logical_not(jnp.logical_and(mine, slot == j)))
        def _():
            a, b = first(j)
            a.wait_send()
            b.wait_send()
            count(j).wait_send()


def attention_kernel(pk_ref, cnt_ref, wkv_ref, u_ref, qT_ref, gT_ref, poT_ref, goT_ref, g_ref, dq_ref, w_ref, e_ref, mb_ref, kv_ref, qm_ref, gm_ref,
                     qmT_ref, gmT_ref, acc_ref, m_ref, s_ref, dkv_ref, attT_ref, dqT_ref, wacc_ref):
    train = jnp.max(cnt_ref[...]).astype(jnp.int32)
    halves = lax.div(train + PC - 1, PC)
    full, odd = lax.div(halves, 2), lax.rem(halves, 2)
    last = lax.div(halves - 1, 2)

    def rows(n):
        return pl.ds(pl.multiple_of(n * KC, KC), KC)

    def packs(n):
        return pl.ds(pl.multiple_of(n * PC, PC), PC)

    def half_packs(n):
        return pl.ds(pl.multiple_of(n * ROWS, ROWS), ROWS)

    @pl.loop(halves, 2 * BLOCKS)
    def _(n):
        g_ref[half_packs(n), :] = jnp.zeros((ROWS, 384), BF)

    lane = lax.broadcasted_iota(jnp.int32, (ROWS, 128), 1)
    sub = lax.broadcasted_iota(jnp.int32, (ROWS, 128), 0)
    real = sub + HALF * (sub >= HALF).astype(jnp.int32)
    v_extra = jnp.where((lane >= HALF) & (lane < HALF + 3), 1.0, 0.0)

    def project(n):
        p = pk_ref[packs(n), :]
        for side, (cells, w) in enumerate(((p[:, 0:256], wkv_ref[0]), (p[:, 128:384], wkv_ref[1]))):
            kv = dot(cells, w)
            for half in range(2):
                first = n * KC + PC * half
                bias = jnp.where((lane == HALF) & (real + (first + HALF * side) >= train), BIAS, 0.0)
                r = pl.ds(pl.multiple_of(first + ROWS * side, ROWS), ROWS)
                own = slice(ROWS * half, ROWS * half + ROWS)
                kv_ref[r, 0:128] = (kv[own, 0:128] + bias).astype(BF)
                kv_ref[r, 128:256] = (kv[own, 128:256] + v_extra).astype(BF)

    project(0)
    project(jnp.minimum(1, last))

    attT_ref[...] = jnp.zeros_like(attT_ref)
    dqT_ref[...] = jnp.zeros_like(dqT_ref)
    wacc_ref[...] = jnp.zeros_like(wacc_ref)
    i16 = lax.broadcasted_iota(jnp.int32, (16, NQ), 0)
    lanes = [slice(NQ * h, NQ * h + NQ) for h in range(3)]
    subs = [slice(32 * h, 32 * h + 32) for h in range(3)]

    qmT_ref[...] = jnp.zeros_like(qmT_ref)
    gmT_ref[...] = jnp.zeros_like(gmT_ref)
    for q, hs in zip(lanes, subs):
        qmT_ref[hs, q] = qT_ref[hs, :]
        qm_ref[q, :] = qmT_ref[:, q].T
        qmT_ref[96:112, q] = jnp.where(i16 == 0, 1.0, 0.0).astype(BF)
    acc_ref[...] = jnp.zeros_like(acc_ref)
    m_ref[...] = jnp.full_like(m_ref, BIAS)

    def piece(n, t):
        return pl.ds(pl.multiple_of(n * KC + (t // 3) * PC, PC), PC), lanes[t % 3]

    def score(n, t):
        r, q = piece(n, t)
        s = dot(kv_ref[r, 0:128], qmT_ref[:, q])
        s_ref[t % 2] = s
        m_ref[2 + t % 2:3 + t % 2, q] = jnp.max(s, axis=0, keepdims=True)

    def weigh(n, t):
        r, q = piece(n, t)
        old = m_ref[0:1, q]
        new = jnp.maximum(old, jnp.ceil(m_ref[2 + t % 2:3 + t % 2, q] * SCALE_LOG2E))
        e = jnp.exp2(s_ref[t % 2] * SCALE_LOG2E - new).astype(BF)
        e_ref[r, q] = e
        m_ref[0:1, q] = new
        mb_ref[n, t // 3:t // 3 + 1, q] = new
        vT = kv_ref[r, 128:256].T
        vt = jnp.concatenate([vT[subs[t % 3]], vT[96:112]], 0)
        acc_ref[:, q] = acc_ref[:, q] * jnp.exp2(old - new) + dot(vt, e)

    score(0, 0)

    @pl.loop(0, full)
    def _(n):
        for t in range(6):
            if t < 5:
                score(n, t + 1)
            else:
                score(jnp.minimum(n + 1, last), 0)
            weigh(n, t)
        project(jnp.minimum(n + 2, last))

    @pl.when(odd == 1)
    def _():
        for t in range(3):
            if t < 2:
                score(full, t + 1)
            weigh(full, t)

    for q, hs in zip(lanes, subs):
        inv = 1.0 / acc_ref[32:33, q]
        att = (acc_ref[0:32, q] * inv).astype(BF)
        attT_ref[hs, :] = att
        gp = (gT_ref[hs, :].astype(F32) * inv).astype(BF)
        delta = -jnp.sum(gp.astype(F32) * att.astype(F32), axis=0, keepdims=True)
        d0 = delta.astype(BF).astype(F32)
        d1 = (delta - d0).astype(BF).astype(F32)
        d2 = delta - d0 - d1
        gmT_ref[hs, q] = gp
        gm_ref[q, :] = gmT_ref[:, q].T
        gmT_ref[96:112, q] = jnp.where(i16 == 0, d0, jnp.where(i16 == 1, d1, jnp.where(i16 == 2, d2, 0.0))).astype(BF)
    acc_ref[...] = jnp.zeros_like(acc_ref)

    def pass_two(n, many):
        size = many * PC
        r = pl.ds(pl.multiple_of(n * KC, KC), size)
        v = kv_ref[r, 128:256]
        kT = kv_ref[r, 0:128].T
        dk, dv = jnp.zeros((size, 128), F32), jnp.zeros((size, 128), F32)
        for h in range(3):
            q = lanes[h]
            ga = dot(v, gmT_ref[:, q]).astype(BF)
            e = e_ref[r, q]
            by = [jnp.exp2(mb_ref[n, t:t + 1, q] - m_ref[0:1, q]).astype(BF) for t in range(many)]
            es = jnp.concatenate([e[PC * t:PC * t + PC] * by[t] for t in range(many)], 0)
            ds = es * ga
            dv = dv + dot(es, gm_ref[q, :])
            dk = dk + dot(ds, qm_ref[q, :])
            acc_ref[0:32, q] += dot(kT[subs[h]], ds)
        dkv_ref[0:size, 0:128] = (dk * SCALE).astype(BF)
        dkv_ref[0:size, 128:256] = dv.astype(BF)
        for t in range(many):
            p = half_packs(2 * n + t)
            pT = pk_ref[p, :].T
            da, db = dkv_ref[PC * t:PC * t + ROWS, :], dkv_ref[PC * t + ROWS:PC * t + PC, :]
            g_ref[p, :] = (dot(da, u_ref[0, 0:256, :]) + dot(db, u_ref[1, 0:256, :])).astype(BF)
            wacc_ref[...] += dot(pT[0:E], da) + dot(pT[E:2 * E], db)

    @pl.loop(0, full)
    def _(n):
        pass_two(n, 2)

    @pl.when(odd == 1)
    def _():
        pass_two(full, 1)

    for q, hs in zip(lanes, subs):
        dqT_ref[hs, :] = (acc_ref[0:32, q] * SCALE).astype(BF)

    dq, at = dqT_ref[...].T, attT_ref[...].T
    dq_ref[...] = dq
    poT, goT = poT_ref[...], goT_ref[...]
    w_q = dot(poT[0:E], dq[0:PC]) + dot(poT[E:2 * E], dq[PC:NQ])
    w_o = dot(goT[0:E], at[0:PC]) + dot(goT[E:2 * E], at[PC:NQ])
    w_ref[...] = (
        dot(w_q.astype(BF), shifted((128, 384), 0, HALF))
        + dot(w_o.astype(BF), shifted((128, 384), HALF, HALF))
        + dot(wacc_ref[:, 0:128].astype(BF), shifted((128, 384), 2 * HALF, HALF))
        + dot(wacc_ref[:, 128:256].astype(BF), shifted((128, 384), 3 * HALF, HALF))
    ).astype(BF)


def reduce_kernel(g_ref, dq_ref, u_ref, w_ref, ret_ref, wf_ref,
                  tw, part, hp, hn, fp, fn, fin, rs, p2,
                  ts, tr, hs_, hr, fs, fr, ks, kr, as_, ar, bs, br, cs, cr):
    z, x, yl, yh, c = place()
    mine = x // 2 == c
    own = jnp.where(mine, 1, 0)
    zp, zo, zn = (z + 1) % 4, (z + 2) % 4, (z + 3) % 4
    up, down, twin = device(zp, x, yl, yh, c), device(zn, x, yl, yh, c), device(z, x, yl, yh, 1 - c)
    slot = (x % 2) * 2 + yl
    i16 = z * 4 + x
    i8 = (yh * 2 + yl) * 2 + c
    owner = i16 < SLABS
    owns = jnp.where(owner, 1, 0)

    barrier = pltpu.get_barrier_semaphore()

    def greet(to):
        pl.semaphore_signal(barrier, inc=1, device_id=to, device_id_type=MESH)

    for to in (twin, up, down):
        greet(to)
    for j in range(4):
        @pl.when(jnp.logical_not(jnp.logical_and(mine, slot == j)))
        def _():
            greet(device(z, 2 * c + j // 2, j % 2, yh, x // 2))

    zs_, xs_ = [z, zp, zo, zn], [x, (x + 1) % 4, (x + 2) % 4, (x + 3) % 4]
    around = [(zs_[n // 4], xs_[n % 4]) for n in range(16)]
    beside = [((yl + n // 2 % 2) % 2, (yh + n // 4) % 2, (c + n % 2) % 2) for n in range(8)]
    for n in range(1, 16):
        greet(device(*around[n], yl, yh, c))
    for n in range(1, 8):
        greet(device(z, x, *beside[n]))

    pl.semaphore_wait(barrier, 3 + 4 - own + 15 + 7)

    sent = []

    def go(copy):
        copy.start()
        sent.append(copy)

    def block(zz, cc):
        return pl.ds(pl.multiple_of((zz * 2 + cc) * PC, PC), PC)

    for n, zz in enumerate((zo, zp, zn, z)):
        go(rcopy(g_ref.at[block(zz, 1 - c), :], tw.at[n], ts.at[n], tr.at[n], twin))

    def slab(n):
        return pl.ds(pl.multiple_of(n * 16, 16), 16)

    def one(n):
        zz, xx = around[n]
        to = zz * 4 + xx
        ok = to < SLABS
        r = slab(jnp.minimum(to, SLABS - 1))
        return ok, rcopy(w_ref.at[r, :], rs.at[i16], as_.at[n], ar.at[i16], device(zz, xx, yl, yh, c))

    def two(n):
        return rcopy(p2.at[i8], p2.at[i8], bs.at[n], br.at[i8], device(z, x, *beside[n]))

    my_slab = slab(jnp.minimum(i16, SLABS - 1))

    def three(n):
        mine_ = wf_ref.at[:, my_slab, :]
        return rcopy(mine_, mine_, cs.at[n], cr.at[i16], device(*around[n], yl, yh, c))

    for n in range(1, 16):
        ok, copy = one(n)

        @pl.when(ok)
        def _():
            copy.start()

    def with_twin(n, zz):
        wait_for(tw.at[n], tr.at[n])
        return g_ref[block(zz, c), :].astype(F32) + tw[n].astype(F32)

    lo, hi = pl.ds(0, 192), pl.ds(192, 192)
    part[0] = with_twin(0, zo).astype(BF)
    go(rcopy(part.at[0, lo, :], hp, hs_.at[0], hr.at[0], up))
    go(rcopy(part.at[0, hi, :], hn, hs_.at[1], hr.at[1], down))
    part[1] = with_twin(1, zp).astype(BF)
    go(rcopy(part.at[1, hi, :], fp.at[hi, :], fs.at[0], fr.at[0], up))
    part[2] = with_twin(2, zn).astype(BF)
    go(rcopy(part.at[2, lo, :], fn.at[lo, :], fs.at[1], fr.at[1], down))

    @pl.when(owner)
    def _():
        rs[i16] = w_ref[slab(jnp.minimum(i16, SLABS - 1)), :]

        for n in range(1, 16):
            m = around[n][0] * 4 + around[n][1]
            wait_for(rs.at[m], ar.at[m])

        acc = rs[0].astype(F32)
        for n in range(1, 16):
            acc = acc + rs[n].astype(F32)
        p2[i8] = acc.astype(BF)

        for n in range(1, 8):
            two(n).start()

    wait_for(hp, hr.at[0])
    part[1, 0:192, :] = (part[1, 0:192, :].astype(F32) + hp[...].astype(F32)).astype(BF)
    go(rcopy(part.at[1, lo, :], fp.at[lo, :], fs.at[2], fr.at[2], up))
    wait_for(hn, hr.at[1])
    part[2, 192:384, :] = (part[2, 192:384, :].astype(F32) + hn[...].astype(F32)).astype(BF)
    go(rcopy(part.at[2, hi, :], fn.at[hi, :], fs.at[3], fr.at[3], down))

    @pl.when(owner)
    def _():
        for yl_, yh_, c_ in beside[1:]:
            m = (yh_ * 2 + yl_) * 2 + c_
            wait_for(p2.at[m], br.at[m])

        for half in range(2):
            n = 2 * half
            acc = p2[n].astype(F32) + p2[n + 1].astype(F32) + p2[n + 4].astype(F32) + p2[n + 5].astype(F32)
            wf_ref[half, slab(jnp.minimum(i16, SLABS - 1)), :] = acc.astype(BF)

        for n in range(1, 16):
            three(n).start()

    total = with_twin(3, z) + dot(dq_ref[0:PC, :], u_ref[0, 256:384, :]) + dot(dq_ref[PC:NQ, :], u_ref[1, 256:384, :])
    wait_for(fp.at[hi, :], fr.at[0])
    wait_for(fn.at[lo, :], fr.at[1])
    wait_for(fp.at[lo, :], fr.at[2])
    wait_for(fn.at[hi, :], fr.at[3])
    fin[...] = (total + fp[...].astype(F32) + fn[...].astype(F32)).astype(BF)

    def back(s):
        to = device(z, 2 * c + s // 2, s % 2, yh, x // 2)
        return rcopy(fin.at[pl.ds(s * HALF, HALF), :], ret_ref.at[slot], ks.at[s], kr.at[slot], to)

    for s in range(4):
        keep = jnp.logical_and(mine, slot == s)

        @pl.when(keep)
        def _():
            pltpu.make_async_copy(fin.at[pl.ds(s * HALF, HALF), :], ret_ref.at[slot], kr.at[slot]).start()

        @pl.when(jnp.logical_not(keep))
        def _():
            back(s).start()

    for n in range(4):
        wait_for(ret_ref.at[n], kr.at[n])

    for n in range(1, 16):
        m = around[n][0] * 4 + around[n][1]

        @pl.when(m < SLABS)
        def _():
            r = slab(jnp.minimum(m, SLABS - 1))
            wait_for(wf_ref.at[:, r, :], cr.at[m])

    for copy in sent:
        copy.wait_send()
    for s in range(4):
        @pl.when(jnp.logical_not(jnp.logical_and(mine, slot == s)))
        def _():
            back(s).wait_send()

    for n in range(1, 16):
        ok, copy = one(n)

        @pl.when(ok)
        def _():
            copy.wait_send()

    @pl.when(owner)
    def _():
        for n in range(1, 16):
            three(n).wait_send()
        for n in range(1, 8):
            two(n).wait_send()


def final_kernel(ret_ref, wf_ref, grad_ref, gc_ref, gwq_ref, gwk_ref, gwv_ref, gwo_ref):
    sort = by_feature()
    i, j = iotas((256, E))
    right = ones_where(i == j + 64)
    total = grad_ref[...].reshape(2 * ROWS, E).astype(F32)
    for half in range(2):
        parts = []
        for f in range(2):
            r = ret_ref[2 * f + half]
            parts += [r[:, 0:E], dot(r[:, 128:384], right).astype(BF)]
        total = total + t_dot(sort, jnp.concatenate(parts, 0))
    gc_ref[...] = total.astype(BF).reshape(ROWS, 2, E)

    i, j = iotas((384, E))

    def weight(first):
        low = ones_where((i == j + first) & (j < HALF))
        high = ones_where((i == j - HALF + first) & (j >= HALF))
        return dot(wf_ref[0], low) + dot(wf_ref[1], high)

    gwq_ref[...] = weight(0)
    gwo_ref[...] = weight(HALF).T
    gwk_ref[...] = weight(2 * HALF)
    gwv_ref[...] = weight(3 * HALF)


SLABS = 12
VM = pl.BlockSpec(memory_space=pltpu.VMEM)
DMA = pltpu.SemaphoreType.DMA


def sds(shape, dtype=BF):
    return jax.ShapeDtypeStruct(shape, dtype)


def share(*args):
    return pl.pallas_call(
        share_kernel,
        out_shape=[
            sds((NR // 2, 384)), sds((8, 128), F32), sds((2, 256, 256)), sds((2, 384, 384)), sds((128, NQ)), sds((128, NQ)),
            sds((384, PC)), sds((384, PC)),
        ],
        in_specs=[VM] * 2,
        out_specs=[VM] * 8,
        scratch_shapes=[
            pltpu.VMEM((PC, 384), BF), pltpu.VMEM((2, 2, 256, 128), BF),
            pltpu.VMEM((2, HALF, 384), BF), pltpu.VMEM((2, HALF, 384), BF),
            pltpu.VMEM((8, 128), F32), pltpu.VMEM((4, 8, 128), F32), pltpu.VMEM((2, 8, 128), F32), pltpu.VMEM((4, 8, 128), F32),
            DMA((4,)), DMA((4,)), DMA((4,)), DMA((4,)), DMA((8,)), DMA((8,)), DMA((4,)), DMA((4,)), DMA((16,)), DMA((16,)),
            DMA((4,)), DMA((4,)), DMA((4,)), DMA((4,)),
        ],
        compiler_params=pltpu.CompilerParams(collective_id=1, has_side_effects=True, vmem_limit_bytes=24 * 2**20),
        cost_estimate=pl.CostEstimate(flops=10**8, bytes_accessed=60 * 10**6, transcendentals=0),
        name="share",
    )(*args)


def attention(*args):
    return pl.pallas_call(
        attention_kernel,
        out_shape=[sds((NR // 2, 384)), sds((NQ, 128)), sds((E, 384))],
        in_specs=[VM] * 8,
        out_specs=[VM] * 3,
        scratch_shapes=[
            pltpu.VMEM((NR, 3 * NQ), BF), pltpu.VMEM((BLOCKS, 8, 3 * NQ), F32), pltpu.VMEM((NR, 256), BF),
            pltpu.VMEM((3 * NQ, 128), BF), pltpu.VMEM((3 * NQ, 128), BF),
            pltpu.VMEM((128, 3 * NQ), BF), pltpu.VMEM((128, 3 * NQ), BF),
            pltpu.VMEM((48, 3 * NQ), F32), pltpu.VMEM((8, 3 * NQ), F32),
            pltpu.VMEM((2, PC, NQ), F32), pltpu.VMEM((KC, 256), BF),
            pltpu.VMEM((128, NQ), BF), pltpu.VMEM((128, NQ), BF), pltpu.VMEM((E, 256), F32),
        ],
        compiler_params=pltpu.CompilerParams(vmem_limit_bytes=VLIM * 2**20),
        cost_estimate=pl.CostEstimate(flops=3 * 10**10, bytes_accessed=10**7, transcendentals=14 * 10**6),
        name="attention",
    )(*args)


VLIM = 45


def reduce(*args):
    return pl.pallas_call(
        reduce_kernel,
        out_shape=[sds((4, HALF, 384)), sds((2, E, 384))],
        in_specs=[VM] * 4,
        out_specs=[VM] * 2,
        scratch_shapes=[
            pltpu.VMEM((4, PC, 384), BF), pltpu.VMEM((3, PC, 384), BF),
            pltpu.VMEM((192, 384), BF), pltpu.VMEM((192, 384), BF),
            pltpu.VMEM((PC, 384), BF), pltpu.VMEM((PC, 384), BF), pltpu.VMEM((PC, 384), BF),
            pltpu.VMEM((16, 16, 384), BF), pltpu.VMEM((8, 16, 384), BF),
            DMA((4,)), DMA((4,)), DMA((2,)), DMA((2,)), DMA((4,)), DMA((4,)), DMA((4,)), DMA((4,)),
            DMA((16,)), DMA((16,)), DMA((8,)), DMA((8,)), DMA((16,)), DMA((16,)),
        ],
        compiler_params=pltpu.CompilerParams(collective_id=2, has_side_effects=True, vmem_limit_bytes=24 * 2**20),
        cost_estimate=pl.CostEstimate(flops=10**8, bytes_accessed=60 * 10**6, transcendentals=0),
        name="reduce",
    )(*args)


def final(*args):
    w = sds((E, E), F32)
    return pl.pallas_call(
        final_kernel,
        out_shape=[sds((ROWS, 2, E)), w, w, w, w],
        in_specs=[VM] * 3,
        out_specs=[VM] * 5,
        compiler_params=pltpu.CompilerParams(vmem_limit_bytes=24 * 2**20),
        name="final",
    )(*args)


def body(cells, w_query, w_key, w_value, w_out, train_flag, grad_out):
    flags = jnp.broadcast_to(train_flag.astype(BF), (1, 2, ROWS))
    parts = share(jnp.concatenate([cells, grad_out, flags], 0), jnp.concatenate([w_query, w_key, w_value, w_out], 0))
    g, dq, w = attention(*parts)
    ret, wf = reduce(g, dq, parts[3], w)
    return final(ret, wf, grad_out)


def solution(mesh):
    return jax.shard_map(
        body,
        mesh=mesh,
        in_specs=(P("row", "feat", None), P(), P(), P(), P(), P("row"), P("row", "feat", None)),
        out_specs=(P("row", "feat", None), P(), P(), P(), P()),
        check_vma=False,
    )
```
